32 devices in a mesh: dp: 2 (over x), space: 16 (over z, y, core).
Axes of the slice: x: 2, y: 2, z: 4, core: 2. Of those that a mesh axis runs over, the one named last changes fastest.
Arguments:
- images: bfloat16 [2, 16, 96, 64, 128], P('dp', 'space'), may hold values from -60 to 60
- first_weight: bfloat16 [3, 3, 128, 256], replicated, may hold values from -0.1875 to 0.1875
- norm_gain: float32 [256], replicated, may hold values from 0.5 to 2
- norm_bias: float32 [256], replicated, may hold values from -2 to 2
- second_weight: bfloat16 [3, 3, 256, 256], replicated, may hold values from -0.125 to 0.125
- upstream: bfloat16 [2, 16, 48, 32, 256], P('dp', 'space'), may hold values from -45 to 45
Outputs:
- input_grad: bfloat16 [2, 16, 96, 64, 128], P('dp', 'space')
- first_grad: float32 [3, 3, 128, 256], replicated
- second_grad: float32 [3, 3, 256, 256], replicated
- gain_grad: float32 [256], replicated
- bias_grad: float32 [256], replicated
The draws below stay inside these ranges and needn't reach their ends.
All inputs are finite; a program needn't handle non-finite values.
Results may differ from the reference program's by a relative error of at most 0.0049.
Values may be sent and summed in bfloat16 or wider, within the bound.
No kernel may reach another device: no remote copies, remote signals or barrier semaphores. Data moves between devices by JAX's collectives and lax.ppermute only.
A program may use at most 64 MiB of HBM per device.

```python
import math
import jax
import jax.numpy as jnp
from jax import lax

CIN = 128
CMID = 256
GROUPS = 32
TCOLS = 4
TH = 48
TW = 32
TILES = 16
TROWS = 4
BATCH = 2


def ramp_scales(key, tile_rows, strength):
    position = jnp.arange(TILES, dtype=jnp.float32) / (TILES - 1)
    ramp = jnp.exp(math.log(strength) * position)
    row_scale = jnp.exp(jax.random.uniform(key, (BATCH, TILES, tile_rows), jnp.float32, math.log(0.2), math.log(2.0)))
    return ramp[None, :, None] * row_scale


def draw_images(key, part):
    keys = jax.random.split(jax.random.fold_in(key, 11), 3)
    shape = (BATCH, TILES, 2 * TH, 2 * TW, CIN)
    base = jax.random.truncated_normal(keys[0], -4.0, 4.0, shape, jnp.float32)
    strength = 3.0
    offset = jax.random.uniform(keys[1], (BATCH, 1, 1, 1, CIN), jnp.float32, -0.8, 0.8)
    scales = ramp_scales(keys[2], 2 * TH, strength)[:, :, :, None, None]
    return (scales * (base + offset)).astype(jnp.bfloat16)


def draw_upstream(key, part):
    keys = jax.random.split(jax.random.fold_in(key, 23), 2)
    shape = (BATCH, TILES, TH, TW, CMID)
    base = jax.random.truncated_normal(keys[0], -4.0, 4.0, shape, jnp.float32)
    strength = 3.0
    scales = ramp_scales(keys[1], TH, strength)[:, :, :, None, None]
    return (scales * base).astype(jnp.bfloat16)


def normal_values(key, shape, deviation, reach, kind=jnp.bfloat16):
    entries = deviation * jax.random.normal(key, shape, jnp.float32)
    return jnp.clip(entries, min=-reach, max=reach).astype(kind)


def setup_inputs(seed: int = 0) -> dict:
    splits = jax.random.split(jax.random.key(seed), 7)
    images = draw_images(jax.random.fold_in(splits[6], 71), 0)
    first_weight = normal_values(splits[1], (3, 3, CIN, CMID), (9 * CIN) ** -0.5, 0.1875)
    norm_gain = jnp.clip(jnp.exp(jax.random.uniform(splits[2], (CMID,), jnp.float32, math.log(0.5), math.log(2.0))), 0.5, 2.0)
    norm_bias = normal_values(splits[3], (CMID,), 0.5, 2.0, jnp.float32)
    second_weight = normal_values(splits[4], (3, 3, CMID, CMID), (9 * CMID) ** -0.5, 0.125)
    upstream = draw_upstream(jax.random.fold_in(splits[6], 71), 0)
    return {"images": images, "first_weight": first_weight, "norm_gain": norm_gain, "norm_bias": norm_bias, "second_weight": second_weight, "upstream": upstream}


def to_image(tile_stack, tile_rows, tile_cols):
    depth = tile_stack.shape[-1]
    placed = jnp.roll(tile_stack, TCOLS + 2, axis=0)
    shaped = placed.reshape(TROWS, TCOLS, tile_rows, tile_cols, depth)
    return shaped.transpose(0, 2, 1, 3, 4).reshape(TROWS * tile_rows, TCOLS * tile_cols, depth)

def to_tiles(picture, tile_rows, tile_cols):
    depth = picture.shape[-1]
    shaped = picture.reshape(TROWS, tile_rows, TCOLS, tile_cols, depth)
    placed = shaped.transpose(0, 2, 1, 3, 4).reshape(TROWS * TCOLS, tile_rows, tile_cols, depth)
    return jnp.roll(placed, -(TCOLS + 2), axis=0)

def stride_conv(padded, weight, out_rows, out_cols):
    result = jnp.zeros((out_rows * out_cols, weight.shape[3]), jnp.float32)
    for tap_row in range(3):
        for tap_col in range(3):
            window = padded[tap_row:tap_row + 2 * out_rows:2, tap_col:tap_col + 2 * out_cols:2]
            result = result + jnp.dot(window.reshape(out_rows * out_cols, -1), weight[tap_row, tap_col], preferred_element_type=jnp.float32)
    return result

def stride_wgrad(padded, conv_grad, out_rows, out_cols):
    taps = []
    for tap_row in range(3):
        for tap_col in range(3):
            window = padded[tap_row:tap_row + 2 * out_rows:2, tap_col:tap_col + 2 * out_cols:2]
            taps.append(jnp.dot(window.reshape(out_rows * out_cols, -1).T, conv_grad, preferred_element_type=jnp.float32))
    stacked = jnp.stack(taps, 0)
    return stacked.reshape(3, 3, stacked.shape[1], stacked.shape[2])

def back_conv(grad_padded, weight, out_rows, out_cols):
    result = jnp.zeros((out_rows * out_cols, weight.shape[2]), jnp.float32)
    for tap_row in range(3):
        for tap_col in range(3):
            window = grad_padded[2 - tap_row:2 - tap_row + out_rows, 2 - tap_col:2 - tap_col + out_cols]
            result = result + jnp.dot(window.reshape(out_rows * out_cols, -1), weight[tap_row, tap_col].T, preferred_element_type=jnp.float32)
    return result

def conv_wgrad(activated, grad_padded, out_rows, out_cols):
    taps = []
    for tap_row in range(3):
        for tap_col in range(3):
            window = grad_padded[2 - tap_row:2 - tap_row + out_rows, 2 - tap_col:2 - tap_col + out_cols]
            taps.append(jnp.dot(activated.T, window.reshape(out_rows * out_cols, -1), preferred_element_type=jnp.float32))
    stacked = jnp.stack(taps, 0)
    return stacked.reshape(3, 3, stacked.shape[1], stacked.shape[2])

def tap_product(extended, weight, tap_row, tap_col, move_row, move_col, out_rows, out_cols):
    window = extended[move_row:move_row + out_rows, move_col:move_col + out_cols]
    return jnp.dot(window.reshape(out_rows * out_cols, -1), weight[tap_row, tap_col].T, preferred_element_type=jnp.float32)

def up_conv(extended, weight, out_rows, out_cols):
    even_even = tap_product(extended, weight, 1, 1, 0, 0, out_rows, out_cols)
    even_odd = tap_product(extended, weight, 1, 2, 0, 0, out_rows, out_cols) + tap_product(extended, weight, 1, 0, 0, 1, out_rows, out_cols)
    odd_even = tap_product(extended, weight, 2, 1, 0, 0, out_rows, out_cols) + tap_product(extended, weight, 0, 1, 1, 0, out_rows, out_cols)
    odd_odd = tap_product(extended, weight, 2, 2, 0, 0, out_rows, out_cols) + tap_product(extended, weight, 2, 0, 0, 1, out_rows, out_cols) + tap_product(extended, weight, 0, 2, 1, 0, out_rows, out_cols) + tap_product(extended, weight, 0, 0, 1, 1, out_rows, out_cols)
    depth = weight.shape[2]
    even_rows = jnp.stack([even_even.reshape(out_rows, out_cols, depth), even_odd.reshape(out_rows, out_cols, depth)], 2).reshape(out_rows, 2 * out_cols, depth)
    odd_rows = jnp.stack([odd_even.reshape(out_rows, out_cols, depth), odd_odd.reshape(out_rows, out_cols, depth)], 2).reshape(out_rows, 2 * out_cols, depth)
    return jnp.stack([even_rows, odd_rows], 1).reshape(2 * out_rows, 2 * out_cols, depth)

def reference(images, first_weight, norm_gain, norm_bias, second_weight, upstream):
    out_rows = TROWS * TH
    out_cols = TCOLS * TW
    group_size = CMID // GROUPS
    norm_count = out_rows * out_cols * group_size

    def per_sample(sample_pair):
        sample_tiles, grad_tiles = sample_pair
        picture = to_image(sample_tiles, 2 * TH, 2 * TW)
        grad_image = to_image(grad_tiles, TH, TW)
        padded = jnp.pad(picture, ((1, 0), (1, 0), (0, 0)))
        pre_norm = stride_conv(padded, first_weight, out_rows, out_cols)
        grouped = pre_norm.reshape(-1, GROUPS, group_size)
        group_mean = lax.optimization_barrier(jnp.sum(grouped, axis=(0, 2))) / norm_count
        centered = grouped - group_mean[None, :, None]
        group_var = lax.optimization_barrier(jnp.sum(centered * centered, axis=(0, 2))) / norm_count
        inv_std = 1.0 / jnp.sqrt(group_var + 1e-05)
        normed = (centered * inv_std[None, :, None]).reshape(-1, CMID)
        shifted = normed * norm_gain + norm_bias
        activated = jax.nn.silu(shifted).astype(jnp.bfloat16)
        grad_padded = jnp.pad(grad_image, ((1, 1), (1, 1), (0, 0)))
        act_grad = back_conv(grad_padded, second_weight, out_rows, out_cols)
        second_part = conv_wgrad(activated, grad_padded, out_rows, out_cols)
        sigmoid_h = jax.nn.sigmoid(shifted)
        pre_grad = act_grad * sigmoid_h * (1.0 + shifted * (1.0 - sigmoid_h))
        sum_one = lax.optimization_barrier(jnp.sum(pre_grad, axis=0))
        sum_two = lax.optimization_barrier(jnp.sum(pre_grad * normed, axis=0))
        mean_shift = lax.optimization_barrier(jnp.sum((norm_gain * sum_one).reshape(GROUPS, group_size), axis=1)) / norm_count
        mean_scale = lax.optimization_barrier(jnp.sum((norm_gain * sum_two).reshape(GROUPS, group_size), axis=1)) / norm_count
        inner = (norm_gain * pre_grad).reshape(-1, GROUPS, group_size) - mean_shift[None, :, None] - normed.reshape(-1, GROUPS, group_size) * mean_scale[None, :, None]
        conv_grad = (inner * inv_std[None, :, None]).reshape(-1, CMID).astype(jnp.bfloat16)
        first_part = stride_wgrad(padded, conv_grad, out_rows, out_cols)
        extended = jnp.pad(conv_grad.reshape(out_rows, out_cols, CMID), ((0, 1), (0, 1), (0, 0)))
        input_grad = up_conv(extended, first_weight, out_rows, out_cols).astype(jnp.bfloat16)
        return (to_tiles(input_grad, 2 * TH, 2 * TW), first_part, second_part, sum_one, sum_two)
    results = lax.map(per_sample, (images, upstream))
    return (results[0], lax.optimization_barrier(jnp.sum(results[1], axis=0)), lax.optimization_barrier(jnp.sum(results[2], axis=0)), lax.optimization_barrier(jnp.sum(results[4], axis=0)), lax.optimization_barrier(jnp.sum(results[3], axis=0)))
```

```python
import functools

import jax
import jax.numpy as jnp
from jax import lax
from jax.experimental import pallas as pl
from jax.experimental.pallas import tpu as pltpu
from jax.sharding import PartitionSpec as P

GROUPS = 32
TCOLS = 4
F32 = jnp.float32
BF16 = jnp.bfloat16
MIB = 1024 * 1024
CHUNK = 256


def call(kernel, outs, args, scratch=(), flops=0, aliases=None, limit=40, smem=0):
    specs = [pl.BlockSpec(memory_space=pltpu.SMEM)] * smem
    specs += [pl.BlockSpec(memory_space=pltpu.VMEM)] * (len(args) - smem)
    moved = sum(a.size * a.dtype.itemsize for a in list(args) + list(outs))
    return pl.pallas_call(
        kernel,
        out_shape=list(outs),
        in_specs=specs,
        out_specs=[pl.BlockSpec(memory_space=pltpu.VMEM)] * len(outs),
        scratch_shapes=list(scratch),
        input_output_aliases=aliases or {},
        compiler_params=pltpu.CompilerParams(vmem_limit_bytes=limit * MIB),
        cost_estimate=pl.CostEstimate(flops=flops, bytes_accessed=moved, transcendentals=0),
    )(*args)


def shape(dims, dtype):
    return jax.ShapeDtypeStruct(tuple(dims), dtype)


def dot(a, b):
    return lax.dot_general(a, b, (((1,), (0,)), ((), ())), preferred_element_type=F32)


def tree_sum(values):
    while len(values) > 1:
        values = [
            values[i] + values[i + 1] if i + 1 < len(values) else values[i]
            for i in range(0, len(values), 2)
        ]
    return values[0]


def planes_kernel(rows, cols, x_ref, w_ref, planes_ref, z_ref, wide):
    cin = x_ref.shape[2]
    planes_ref[0:cols, :] = jnp.zeros((cols, 6 * cin), BF16)
    step = CHUNK // cols
    wide[:, 0:8, :] = jnp.zeros((2 * step, 8, cin), F32)

    def deinterleave(i, carry):
        base = pl.multiple_of(i * 2 * step, 2 * step)
        wide[:, 8 : 8 + 2 * cols, :] = x_ref[pl.ds(base, 2 * step)].astype(F32)
        row = pl.multiple_of((i * step + 1) * cols, cols)
        for parity in range(2):
            for slot, first in enumerate((7, 8, 9)):
                part = wide[pl.ds(parity, step, stride=2), pl.ds(first, cols, stride=2), :]
                lane = (parity * 3 + slot) * cin
                planes_ref[pl.ds(row, CHUNK), lane : lane + cin] = part.reshape(CHUNK, cin).astype(BF16)
        return carry

    lax.fori_loop(0, rows // step, deinterleave, 0)

    def convolve(i, carry):
        row = pl.multiple_of(i * CHUNK, CHUNK)
        above = planes_ref[pl.ds(row, CHUNK), 3 * cin :]
        here = planes_ref[pl.ds(pl.multiple_of(row + cols, cols), CHUNK), :]
        z_ref[pl.ds(row, CHUNK), :] = dot(above, w_ref[0 : 3 * cin]) + dot(here, w_ref[3 * cin :])
        return carry

    lax.fori_loop(0, rows * cols // CHUNK, convolve, 0)


def edge_parts(cols, xcol_ref, xrow_ref, corner_ref, col_pad, row_pad):
    rows = xcol_ref.shape[0] // 2
    col_pad[0:8, :] = jnp.broadcast_to(corner_ref[0:1, :].astype(F32), (8, corner_ref.shape[1]))
    col_pad[8 : 8 + 2 * rows, :] = xcol_ref[...].astype(F32)
    row_pad[0:8, :] = jnp.zeros((8, xrow_ref.shape[1]), F32)
    row_pad[8 : 8 + 2 * cols, :] = xrow_ref[...].astype(F32)
    left = [col_pad[pl.ds(first, rows, stride=2), :] for first in (7, 8, 9)]
    over = [row_pad[pl.ds(first, cols, stride=2), :] for first in (7, 8, 9)]
    return left, over


def edges_kernel(rows, cols, z_in, xcol_ref, xrow_ref, corner_ref, w_ref, z_ref, stats_ref, col_pad, row_pad, rim):
    cin = xrow_ref.shape[1]
    left, over = edge_parts(cols, xcol_ref, xrow_ref, corner_ref, col_pad, row_pad)
    z_ref[...] = z_in[...]
    from_above = dot(jnp.concatenate(over, 1).astype(BF16), w_ref[0 : 3 * cin])
    from_left = (
        dot(left[0].astype(BF16), w_ref[0:cin])
        + dot(left[1].astype(BF16), w_ref[3 * cin : 4 * cin])
        + dot(left[2].astype(BF16), w_ref[6 * cin : 7 * cin])
    )
    z_ref[0:cols, :] = z_ref[0:cols, :] + from_above
    rim[...] = from_left
    for p in range(rows):
        z_ref[p * cols : p * cols + 1, :] = z_ref[p * cols : p * cols + 1, :] + rim[p : p + 1, :]
    z = z_ref[...]
    stats_ref[0:1, :] = jnp.sum(z, axis=0, keepdims=True)
    stats_ref[1:2, :] = jnp.sum(z * z, axis=0, keepdims=True)


def windows_kernel(rows, cols, planes_ref, xcol_ref, xrow_ref, corner_ref, t_ref, col_pad, row_pad, wide):
    cin = xrow_ref.shape[1]
    cells = rows * cols
    left, over = edge_parts(cols, xcol_ref, xrow_ref, corner_ref, col_pad, row_pad)
    for half, parts in ((0, left[1]), (3, left[2])):
        wide[...] = planes_ref[cols:, half * cin : (half + 1) * cin].astype(F32)
        wide[pl.ds(0, rows, stride=cols), :] = parts
        window = wide[...].astype(BF16)
        t_ref[(half + 3) * cin : (half + 4) * cin, :] = window.T
    wide[cols:, :] = planes_ref[cols:cells, 3 * cin : 4 * cin].astype(F32)
    wide[0:cols, :] = over[0]
    wide[pl.ds(0, rows, stride=cols), :] = left[0]
    t_ref[0:cin, :] = wide[...].astype(BF16).T
    for slot in (1, 2):
        lane = (3 + slot) * cin
        below = planes_ref[cols:cells, lane : lane + cin]
        window = jnp.concatenate([over[slot].astype(BF16), below], 0)
        t_ref[slot * cin : (slot + 1) * cin, :] = window.T
    for slot in (1, 2, 4, 5):
        lane = slot * cin
        t_ref[lane + 3 * cin : lane + 4 * cin, :] = planes_ref[cols:, lane : lane + cin].T


def upstream_kernel(rows, cols, g_ref, left_ref, right_ref, above_ref, below_ref, w_ref, taps_ref, act_grad_ref, wide, w_t, rims):
    pitch = cols + 16
    depth = g_ref.shape[1]
    for p in range(rows):
        wide[(p + 1) * pitch + 8 : (p + 1) * pitch + 8 + cols, :] = g_ref[p * cols : (p + 1) * cols, :].astype(F32)
    rims[0] = left_ref[...].astype(F32)
    rims[1] = right_ref[...].astype(F32)
    for p in range(rows):
        first = (p + 1) * pitch + 7
        wide[first : first + 1, :] = rims[0, p : p + 1, :]
        wide[first + 1 + cols : first + 2 + cols, :] = rims[1, p : p + 1, :]
    wide[7 : 9 + cols, :] = above_ref[...].astype(F32)
    last = (rows + 1) * pitch
    wide[last + 7 : last + 9 + cols, :] = below_ref[...].astype(F32)
    for r in range(rows + 2):
        for b in range(3):
            first = r * pitch + 9 - b
            taps_ref[b, r * cols : (r + 1) * cols, :] = wide[first : first + cols, :].astype(BF16)
    for tap in range(9):
        w_t[tap * depth : (tap + 1) * depth, :] = w_ref[tap * depth : (tap + 1) * depth, :].T

    def convolve(i, carry):
        row = pl.multiple_of(i * CHUNK, CHUNK)
        parts = []
        for a in range(3):
            for b in range(3):
                parts.append(taps_ref[b, pl.ds(pl.multiple_of(row + (2 - a) * cols, cols), CHUNK), :])
        act_grad_ref[pl.ds(row, CHUNK), :] = dot(jnp.concatenate(parts, 1), w_t[...])
        return carry

    lax.fori_loop(0, rows * cols // CHUNK, convolve, 0)


def group_sum(value, depth):
    size = depth // GROUPS
    one = lax.broadcasted_iota(jnp.int32, (depth, depth), 0) // size
    two = lax.broadcasted_iota(jnp.int32, (depth, depth), 1) // size
    same = jnp.where(one == two, 1.0, 0.0).astype(F32)
    return lax.dot_general(
        value, same, (((1,), (0,)), ((), ())), precision=lax.Precision.HIGHEST, preferred_element_type=F32
    )


def activate_kernel(count, norm_count, *refs):
    stats = refs[:count]
    z_ref, act_grad_ref, gain_ref, bias_ref, act_ref, pre_ref, sums_ref, moments_ref = refs[count:]
    cells, depth = z_ref.shape
    total = group_sum(tree_sum([s[...] for s in stats]), depth) / norm_count
    mean = total[0:1, :]
    inv_std = 1.0 / jnp.sqrt(total[1:2, :] - mean * mean + 1e-05)
    moments_ref[0:1, :] = mean
    moments_ref[1:2, :] = inv_std
    gain = gain_ref[...]
    bias = bias_ref[...]

    def chunk(i, carry):
        row = pl.multiple_of(i * 64, 64)
        normed = (z_ref[pl.ds(row, 64), :] - mean) * inv_std
        shifted = normed * gain + bias
        sig = 1.0 / (1.0 + jnp.exp(-shifted))
        act_ref[pl.ds(row, 64), :] = (shifted * sig).astype(BF16)
        pre = act_grad_ref[pl.ds(row, 64), :] * sig * (1.0 + shifted * (1.0 - sig))
        pre_ref[pl.ds(row, 64), :] = pre
        one = jnp.sum(pre.reshape(8, 8, depth), axis=0)
        two = jnp.sum((pre * normed).reshape(8, 8, depth), axis=0)
        return carry[0] + one, carry[1] + two

    zero = jnp.zeros((8, depth), F32)
    one, two = lax.fori_loop(0, cells // 64, chunk, (zero, zero))
    sums_ref[0:1, :] = jnp.sum(one, axis=0, keepdims=True)
    sums_ref[1:2, :] = jnp.sum(two, axis=0, keepdims=True)


def second_kernel(rows, cols, me_ref, act_ref, taps_ref, out_ref, whole):
    cells = rows * cols
    depth = act_ref.shape[1]
    act_t = act_ref[...].T
    for a in range(3):
        for b in range(3):
            first = (2 - a) * cols
            tap = a * 3 + b
            whole[tap * depth : (tap + 1) * depth, :] = dot(act_t, taps_ref[b, first : first + cells, :])
    spread(me_ref, whole, out_ref)


def spread(me_ref, whole, out_ref):
    size = out_ref.shape[1]
    for slot in range(8):
        first = pl.multiple_of((me_ref[0] ^ slot) * size, 16)
        out_ref[slot] = whole[pl.ds(first, size), :]


def conv_grad_kernel(count, norm_count, rows, cols, me_ref, *refs):
    sums = refs[:count]
    z_ref, pre_ref, moments_ref, gain_ref, t_ref, grad_ref, col_ref, total_ref, out_ref, whole, rims = refs[count:]
    cells, depth = z_ref.shape
    total = tree_sum([s[...] for s in sums])
    total_ref[...] = total
    gain = gain_ref[...]
    means = group_sum(total * gain, depth) / norm_count
    mean = moments_ref[0:1, :]
    inv_std = moments_ref[1:2, :]
    shift = means[0:1, :]
    scale = means[1:2, :]

    def value(z, pre):
        return ((gain * pre - shift - (z - mean) * inv_std * scale) * inv_std).astype(BF16)

    def chunk(i, carry):
        row = pl.multiple_of(i * 64, 64)
        grad_ref[pl.ds(row, 64), :] = value(z_ref[pl.ds(row, 64), :], pre_ref[pl.ds(row, 64), :])
        return carry

    lax.fori_loop(0, cells // 64, chunk, 0)
    for p in range(rows):
        rims[0, p : p + 1, :] = z_ref[p * cols : p * cols + 1, :]
        rims[1, p : p + 1, :] = pre_ref[p * cols : p * cols + 1, :]
    col_ref[...] = value(rims[0], rims[1])

    def product(i, carry):
        row = pl.multiple_of(i * 128, 128)
        whole[pl.ds(row, 128), :] = dot(t_ref[pl.ds(row, 128), :], grad_ref[...])
        return carry

    lax.fori_loop(0, t_ref.shape[0] // 128, product, 0)
    spread(me_ref, whole, out_ref)


def input_kernel(rows, cols, d_ref, right_ref, below_ref, corner_ref, w_ref, out_ref, moved, w_t, wide, mixed, rim):
    cells = rows * cols
    cin = out_ref.shape[2]
    depth = d_ref.shape[1]
    plain = moved.at[0]
    shifted = moved.at[1]
    plain[0:cells, :] = d_ref[...]
    plain[cells : cells + cols, :] = below_ref[...]
    wide[0:cells, :] = d_ref[...].astype(F32)
    wide[cells : cells + cols, :] = below_ref[...].astype(F32)
    wide[cells + cols :, :] = jnp.zeros((8, depth), F32)
    right = right_ref[...].astype(F32)
    corner = corner_ref[...].astype(F32)
    shifted[...] = wide[1 : 1 + cells + cols, :].astype(BF16)
    for tap in range(9):
        w_t[tap] = w_ref[tap * cin : (tap + 1) * cin, :].T
    wide[0 : cells + cols, :] = shifted[...].astype(F32)
    rim[...] = right
    for p in range(rows):
        last = (p + 1) * cols - 1
        wide[last : last + 1, :] = rim[p : p + 1, :]
    wide[cells + cols - 1 : cells + cols, :] = corner
    shifted[...] = wide[0 : cells + cols, :].astype(BF16)
    step = CHUNK // cols

    def chunk(i, carry):
        row = pl.multiple_of(i * CHUNK, CHUNK)
        under = pl.multiple_of(row + cols, cols)
        d = plain[pl.ds(row, CHUNK), :]
        dc = shifted[pl.ds(row, CHUNK), :]
        dr = plain[pl.ds(under, CHUNK), :]
        drc = shifted[pl.ds(under, CHUNK), :]
        even_even = dot(d, w_t[4])
        even_odd = dot(d, w_t[5]) + dot(dc, w_t[3])
        odd_even = dot(d, w_t[7]) + dot(dr, w_t[1])
        odd_odd = dot(d, w_t[8]) + dot(dc, w_t[6]) + dot(dr, w_t[2]) + dot(drc, w_t[0])
        for parity, pair in enumerate(((even_even, even_odd), (odd_even, odd_odd))):
            for side in range(2):
                mixed[pl.ds(parity, step, stride=2), pl.ds(side, cols, stride=2), :] = pair[side].reshape(
                    step, cols, cin
                )
        out_ref[pl.ds(pl.multiple_of(i * 2 * step, 2 * step), 2 * step)] = mixed[...].astype(BF16)
        return carry

    lax.fori_loop(0, rows // step, chunk, 0)


def gather_kernel(me_ref, *refs):
    me = me_ref[0]
    count = len(refs) // 6
    for g in range(count):
        own = refs[g * 5 : g * 5 + 4]
        other = refs[g * 5 + 4]
        out_ref = refs[count * 5 + g]
        for slot in range(4):
            out_ref[me ^ slot] = own[slot][...].astype(F32)
            out_ref[me ^ slot ^ 4] = other[slot].astype(F32)


def on_device(dp_size, tiles, images, first_weight, norm_gain, norm_bias, second_weight, upstream):
    rows, cols, depth = upstream.shape[2:]
    cin = images.shape[4]
    cells = rows * cols
    group_size = depth // GROUPS
    norm_count = float(cells * tiles * group_size)
    tile_rows = tiles // TCOLS
    axes = ("dp", "space")
    devices = dp_size * tiles

    def flip(value, mask):
        return lax.ppermute(value, axes, [(i, i ^ mask) for i in range(devices)])

    def moved(value, down, right):
        pairs = []
        for t in range(tiles):
            place = (t + TCOLS + 2) % tiles
            r, c = place // TCOLS + down, place % TCOLS + right
            if 0 <= r < tile_rows and 0 <= c < TCOLS:
                pairs.append((t, (r * TCOLS + c - TCOLS - 2) % tiles))
        return lax.ppermute(value, "space", pairs)

    def all_sums(value):
        value = value + flip(value, 1)
        value = value + flip(value, 2)
        return [value] + [flip(value, 4 * k) for k in range(1, tiles // 4)]

    def summed(parts):
        return tree_sum([p.astype(F32) for p in parts])

    masks = [0, 2, tiles, tiles + 2]

    def scattered(slots):
        half = slots[0:4] + flip(slots[4:8], 1)
        sent = half[1:4].astype(BF16)
        shard = summed([half[0]] + [flip(sent[k - 1], masks[k]) for k in (1, 2, 3)]).astype(BF16)
        if dp_size > 2:
            shard = summed([shard] + [flip(shard, 2 * tiles * k) for k in range(1, dp_size // 2)]).astype(BF16)
        return summed([shard] + [flip(shard, 4 * k) for k in range(1, tiles // 4)]).astype(BF16)

    def gathered(shard):
        own = [shard] + [flip(shard, masks[k]) for k in (1, 2, 3)]
        return own + [flip(jnp.stack(own), 1)]

    space = lax.axis_index("space")
    me = (space % 2) * 4 + (lax.axis_index("dp") % 2) * 2 + (space // 2) % 2
    me = me.astype(jnp.int32).reshape(1)
    x = images[0, 0]
    w1 = first_weight.reshape(9 * cin, depth)
    w2 = second_weight.reshape(9 * depth, depth)
    gain = norm_gain.reshape(1, depth)
    bias = norm_bias.reshape(1, depth)
    xcol = moved(x[:, -1, :], 0, 1)
    xrow = moved(x[-1], 1, 0)
    corner = moved(x[-1, -1:], 1, 1)

    g3 = upstream[0, 0]
    gleft = moved(g3[:, -1, :], 0, 1)
    gright = moved(g3[:, 0, :], 0, -1)
    gabove = moved(jnp.concatenate([gleft[-1:], g3[-1], gright[-1:]], 0), 1, 0)
    gbelow = moved(jnp.concatenate([gleft[:1], g3[0], gright[:1]], 0), -1, 0)

    planes, z = call(
        functools.partial(planes_kernel, rows, cols),
        [shape((cells + cols, 6 * cin), BF16), shape((cells, depth), F32)],
        [x, w1],
        [pltpu.VMEM((2 * CHUNK // cols, 2 * cols + 8, cin), F32)],
        flops=2 * cells * 9 * cin * depth,
    )
    pads = [pltpu.VMEM((2 * rows + 8, cin), F32), pltpu.VMEM((2 * cols + 8, cin), F32)]
    z, stats = call(
        functools.partial(edges_kernel, rows, cols),
        [shape((cells, depth), F32), shape((2, depth), F32)],
        [z, xcol, xrow, corner, w1],
        pads + [pltpu.VMEM((rows, depth), F32)],
        flops=2 * 80 * 3 * cin * depth,
    )
    stats = all_sums(stats)
    taps, act_grad = call(
        functools.partial(upstream_kernel, rows, cols),
        [shape((3, cells + 2 * cols, depth), BF16), shape((cells, depth), F32)],
        [g3.reshape(cells, depth), gleft, gright, gabove, gbelow, w2],
        [pltpu.VMEM(((rows + 2) * (cols + 16), depth), F32), pltpu.VMEM((9 * depth, depth), BF16), pltpu.VMEM((2, rows, depth), F32)],
        flops=2 * cells * 9 * depth * depth,
    )
    (windows,) = call(
        functools.partial(windows_kernel, rows, cols),
        [shape((9 * cin, cells), BF16)],
        [planes, xcol, xrow, corner],
        pads + [pltpu.VMEM((cells, cin), F32)],
        flops=2 * cells * 9 * cin * depth,
    )
    activated, pre_grad, sums, moments = call(
        functools.partial(activate_kernel, len(stats), norm_count),
        [shape((cells, depth), BF16), shape((cells, depth), F32), shape((2, depth), F32), shape((2, depth), F32)],
        stats + [z, act_grad, gain, bias],
        flops=cells * depth * 30,
    )
    sums = all_sums(sums)
    (second_slots,) = call(
        functools.partial(second_kernel, rows, cols),
        [shape((8, 9 * depth // 8, depth), F32)],
        [me, activated, taps],
        [pltpu.VMEM((9 * depth, depth), F32)],
        flops=2 * cells * 9 * depth * depth,
        smem=1,
    )
    second_shard = scattered(second_slots)
    conv_grad, dcol, total, first_slots = call(
        functools.partial(conv_grad_kernel, len(sums), norm_count, rows, cols),
        [
            shape((cells, depth), BF16),
            shape((rows, depth), BF16),
            shape((2, depth), F32),
            shape((8, 9 * cin // 8, depth), F32),
        ],
        [me] + sums + [z, pre_grad, moments, gain, windows],
        [pltpu.VMEM((9 * cin, depth), F32), pltpu.VMEM((2, rows, depth), F32)],
        flops=2 * cells * 9 * cin * depth,
        smem=1,
    )
    first_shard = scattered(first_slots)
    dright = moved(dcol, 0, -1)
    dbelow = moved(conv_grad[:cols], -1, 0)
    dcorner = moved(conv_grad[:1], -1, -1)
    (input_grad,) = call(
        functools.partial(input_kernel, rows, cols),
        [shape((2 * rows, 2 * cols, cin), BF16)],
        [conv_grad, dright, dbelow, dcorner, w1],
        [
            pltpu.VMEM((2, cells + cols, depth), BF16),
            pltpu.VMEM((9, depth, cin), BF16),
            pltpu.VMEM((cells + cols + 8, depth), F32),
            pltpu.VMEM((2 * CHUNK // cols, 2 * cols, cin), F32),
            pltpu.VMEM((rows, depth), F32),
        ],
        flops=2 * cells * 9 * cin * depth,
    )
    for k in range(dp_size.bit_length() - 1):
        total = total + flip(total, tiles << k)
    second_grad, first_grad = call(
        gather_kernel,
        [shape((8, 9 * depth // 8, depth), F32), shape((8, 9 * cin // 8, depth), F32)],
        [me] + gathered(second_shard) + gathered(first_shard),
        smem=1,
    )
    return (
        input_grad[None, None],
        first_grad.reshape(first_weight.shape),
        second_grad.reshape(second_weight.shape),
        total[1],
        total[0],
    )


def solution(mesh):
    placed = (
        P("dp", "space", None, None, None),
        P(),
        P(),
        P(),
        P(),
        P("dp", "space", None, None, None),
    )
    return jax.shard_map(
        functools.partial(on_device, mesh.shape["dp"], mesh.shape["space"]),
        mesh=mesh,
        in_specs=placed,
        out_specs=(P("dp", "space", None, None, None), P(), P(), P(), P()),
        check_vma=False,
    )
```

```python
import functools

import jax
import jax.numpy as jnp
from jax import lax
from jax.experimental import pallas as pl
from jax.experimental.pallas import tpu as pltpu
from jax.sharding import PartitionSpec as P

GROUPS = 32
TCOLS = 4
F32 = jnp.float32
BF16 = jnp.bfloat16
MIB = 1024 * 1024
CHUNK = 256
LONG = 512


def call(kernel, outs, args, scratch=(), flops=0, limit=20, smem=0, after=(), specs=None, grid=()):
    if specs is None:
        specs = [pl.BlockSpec(memory_space=pltpu.SMEM)] * smem
        specs += [pl.BlockSpec(memory_space=pltpu.VMEM)] * (len(args) - smem)
    moved = sum(a.size * a.dtype.itemsize for a in list(args) + list(outs))
    count = len(args)

    def body(*refs):
        kernel(*refs[:count], *refs[count + len(after) :])

    return pl.pallas_call(
        body,
        out_shape=list(outs),
        grid=grid,
        in_specs=list(specs) + [pl.BlockSpec(memory_space=pl.ANY)] * len(after),
        out_specs=[pl.BlockSpec(memory_space=pltpu.VMEM)] * len(outs),
        scratch_shapes=list(scratch),
        compiler_params=pltpu.CompilerParams(vmem_limit_bytes=limit * MIB),
        cost_estimate=pl.CostEstimate(flops=flops, bytes_accessed=moved, transcendentals=0),
    )(*args, *after)


def shape(dims, dtype):
    return jax.ShapeDtypeStruct(tuple(dims), dtype)


def dot(a, b):
    return lax.dot_general(a, b, (((1,), (0,)), ((), ())), preferred_element_type=F32)


def tree_sum(values):
    while len(values) > 1:
        values = [
            values[i] + values[i + 1] if i + 1 < len(values) else values[i]
            for i in range(0, len(values), 2)
        ]
    return values[0]


def pack_kernel(rows, cols, place_ref, x_first, x_last, g_first, g_last, one_ref, two_ref, own_ref, wide, flat):
    cin = x_first.shape[2]
    even = place_ref[0] == 0

    def x_column(ref, index):
        wide[...] = ref[...].astype(F32).reshape(2 * rows * 16, cin)
        return wide[pl.ds(index, 2 * rows, stride=16), :]

    def g_column(ref, index):
        halves = []
        for half in range(ref.shape[2] // 128):
            flat[...] = ref[:, :, half * 128 : (half + 1) * 128].astype(F32).reshape(rows * 16, 128)
            halves.append(flat[pl.ds(index, rows, stride=16), :])
        return jnp.concatenate(halves, 0)

    size = 2 * rows
    rightwards = (x_column(x_last, 15), g_column(g_last, 15))
    leftwards = (x_column(x_first, 0), x_column(x_first, 1))
    for k in range(2):
        part = slice(k * size, (k + 1) * size)
        own_ref[part, :] = rightwards[k].astype(BF16)
        one_ref[part, :] = jnp.where(even, rightwards[k], leftwards[k]).astype(BF16)
        two_ref[part, :] = jnp.where(even, leftwards[k], rightwards[k]).astype(BF16)
        both = g_column(g_first, k).astype(BF16)
        one_ref[(k + 2) * size : (k + 3) * size, :] = both
        two_ref[(k + 2) * size : (k + 3) * size, :] = both


def choose(even, one, two):
    return jnp.where(even, one.astype(F32), two.astype(F32)).astype(BF16)


def rows_kernel(
    rows, cols, place_ref, x_last, x_first, g_last, g_first, got_one, got_two,
    left_ref, right_ref, one_ref, two_ref, own_ref, x_wide, g_wide,
):
    cin = x_last.shape[2]
    depth = g_last.shape[2]
    even_col = place_ref[0] == 0
    even_row = place_ref[1] == 0
    size = 2 * rows
    left_ref[...] = choose(even_col, got_two[0 : 2 * size, :], got_one[0 : 2 * size, :])
    right_ref[...] = choose(even_col, got_one[...], got_two[...])

    def cell(ref, index):
        first = index // 16 * 16
        return ref[first : first + 16, :].astype(F32)[index - first : index - first + 1, :]

    def x_line(cells, r):
        x_wide[...] = jnp.zeros((2 * cols + 32, cin), F32)
        x_wide[16 : 16 + 2 * cols, :] = cells.astype(F32)
        x_wide[15:16, :] = cell(left_ref, r)
        x_wide[16 + 2 * cols : 17 + 2 * cols, :] = cell(right_ref, r)
        x_wide[17 + 2 * cols : 18 + 2 * cols, :] = cell(right_ref, size + r)
        return x_wide[...]

    def g_line(cells, p):
        halves = []
        for half in range(depth // 128):
            g_wide[...] = jnp.zeros((cols + 16, 128), F32)
            g_wide[8 : 8 + cols, :] = cells[:, half * 128 : (half + 1) * 128].astype(F32)
            g_wide[7:8, :] = cell(left_ref, size + half * rows + p)
            g_wide[8 + cols : 9 + cols, :] = cell(right_ref, 2 * size + half * rows + p)
            g_wide[9 + cols : 10 + cols, :] = cell(right_ref, 3 * size + half * rows + p)
            halves.append(g_wide[...])
        return jnp.concatenate(halves, 0)

    line = 2 * cols + 32
    down = (x_line(x_last[0], 2 * rows - 1), g_line(g_last[0], rows - 1))
    up = (x_line(x_first[0], 0), x_line(x_first[1], 1))
    for k in range(2):
        part = slice(k * line, (k + 1) * line)
        own_ref[part, :] = down[k].astype(BF16)
        one_ref[part, :] = jnp.where(even_row, down[k], up[k]).astype(BF16)
        two_ref[part, :] = jnp.where(even_row, up[k], down[k]).astype(BF16)
        both = g_line(g_first[k], k).astype(BF16)
        one_ref[(k + 2) * line : (k + 3) * line, :] = both
        two_ref[(k + 2) * line : (k + 3) * line, :] = both


def planes_kernel(rows, cols, x_ref, planes_ref, wide):
    cin = x_ref.shape[2]
    planes_ref[0:cols, :] = jnp.zeros((cols, 6 * cin), BF16)
    step = CHUNK // cols
    wide[:, 0:8, :] = jnp.zeros((2 * step, 8, cin), F32)

    def deinterleave(i, carry):
        base = pl.multiple_of(i * 2 * step, 2 * step)
        wide[:, 8 : 8 + 2 * cols, :] = x_ref[pl.ds(base, 2 * step)].astype(F32)
        row = pl.multiple_of((i * step + 1) * cols, cols)
        for parity in range(2):
            for slot, first in enumerate((7, 8, 9)):
                part = wide[pl.ds(parity, step, stride=2), pl.ds(first, cols, stride=2), :]
                lane = (parity * 3 + slot) * cin
                planes_ref[pl.ds(row, CHUNK), lane : lane + cin] = part.reshape(CHUNK, cin).astype(BF16)
        return carry

    lax.fori_loop(0, rows // step, deinterleave, 0)


def stride_kernel(rows, cols, planes_ref, w_ref, z_ref):
    cin = planes_ref.shape[1] // 6

    def convolve(i, carry):
        row = pl.multiple_of(i * LONG, LONG)
        above = planes_ref[pl.ds(row, LONG), 3 * cin :]
        here = planes_ref[pl.ds(pl.multiple_of(row + cols, cols), LONG), :]
        z_ref[pl.ds(row, LONG), :] = dot(jnp.concatenate([above, here], 1), w_ref[...])
        return carry

    lax.fori_loop(0, rows * cols // LONG, convolve, 0)


def edge_parts(rows, cols, xcol_ref, xrow_ref, col_pad, row_pad):
    col_pad[0:8, :] = xrow_ref[0:16, :].astype(F32)[8:16, :]
    col_pad[8 : 8 + 2 * rows, :] = xcol_ref[0 : 2 * rows, :].astype(F32)
    row_pad[0:8, :] = jnp.zeros((8, xrow_ref.shape[1]), F32)
    row_pad[8 : 8 + 2 * cols, :] = xrow_ref[16 : 16 + 2 * cols, :].astype(F32)
    left = [col_pad[pl.ds(first, rows, stride=2), :] for first in (7, 8, 9)]
    over = [row_pad[pl.ds(first, cols, stride=2), :] for first in (7, 8, 9)]
    return left, over


def edges_kernel(
    rows, cols, place_ref, z_in, xcol_ref, right_ref, own_col_ref, own_row_ref, got_one, got_two, w_ref,
    z_ref, stats_ref, xrow_ref, below_ref, z_rim_ref, col_pad, row_pad, rim, bottom, side,
):
    cin = xcol_ref.shape[1]
    even_row = place_ref[1] == 0
    line = 2 * cols + 32
    xrow_ref[...] = choose(even_row, got_two[0 : 2 * line, :], got_one[0 : 2 * line, :])
    below_ref[...] = choose(even_row, got_one[...], got_two[...])
    left, over = edge_parts(rows, cols, xcol_ref, xrow_ref, col_pad, row_pad)
    z_ref[...] = z_in[...]
    from_above = dot(jnp.concatenate(over, 1).astype(BF16), w_ref[0 : 3 * cin])
    from_left = (
        dot(left[0].astype(BF16), w_ref[0:cin])
        + dot(left[1].astype(BF16), w_ref[3 * cin : 4 * cin])
        + dot(left[2].astype(BF16), w_ref[6 * cin : 7 * cin])
    )
    z_ref[0:cols, :] = z_ref[0:cols, :] + from_above
    rim[...] = from_left
    for p in range(rows):
        z_ref[p * cols : p * cols + 1, :] = z_ref[p * cols : p * cols + 1, :] + rim[p : p + 1, :]
    z = z_ref[...]
    stats_ref[0:1, :] = jnp.sum(z, axis=0, keepdims=True)
    stats_ref[1:2, :] = jnp.sum(z * z, axis=0, keepdims=True)
    bottom[0] = own_row_ref[0:line, :].astype(F32)
    bottom[1] = below_ref[0:line, :].astype(F32)
    bottom[2] = below_ref[line : 2 * line, :].astype(F32)
    over_end = xrow_ref[2 * cols : 2 * cols + 32, :].astype(F32)
    for b, ref in enumerate((own_col_ref, right_ref, right_ref)):
        first = 2 * rows if b == 2 else 0
        side[b, 8:, :] = ref[first : first + 2 * rows, :].astype(F32)
        side[b, 7:8, :] = over_end[15 + b : 16 + b, :]
    parts = []
    for a in range(3):
        for b in range(3):
            low = bottom[a, pl.ds(15 + b, cols + 8, stride=2), :]
            beside = side[b, pl.ds(7 + a, rows, stride=2), :]
            parts.append(jnp.concatenate([low, beside], 0).astype(BF16))
    z_rim_ref[...] = dot(jnp.concatenate(parts, 1), w_ref[...])


def windows_kernel(rows, cols, planes_ref, xcol_ref, xrow_ref, t_ref, col_pad, row_pad, wide):
    cin = xrow_ref.shape[1]
    cells = rows * cols
    left, over = edge_parts(rows, cols, xcol_ref, xrow_ref, col_pad, row_pad)
    for half, parts in ((0, left[1]), (3, left[2])):
        wide[...] = planes_ref[cols:, half * cin : (half + 1) * cin].astype(F32)
        wide[pl.ds(0, rows, stride=cols), :] = parts
        window = wide[...].astype(BF16)
        t_ref[(half + 3) * cin : (half + 4) * cin, :] = window.T
    wide[cols:, :] = planes_ref[cols:cells, 3 * cin : 4 * cin].astype(F32)
    wide[0:cols, :] = over[0]
    wide[pl.ds(0, rows, stride=cols), :] = left[0]
    t_ref[0:cin, :] = wide[...].astype(BF16).T
    for slot in (1, 2):
        lane = (3 + slot) * cin
        below = planes_ref[cols:cells, lane : lane + cin]
        window = jnp.concatenate([over[slot].astype(BF16), below], 0)
        t_ref[slot * cin : (slot + 1) * cin, :] = window.T
    for slot in (1, 2, 4, 5):
        lane = slot * cin
        t_ref[lane + 3 * cin : lane + 4 * cin, :] = planes_ref[cols:, lane : lane + cin].T


def upstream_kernel(
    rows, cols, g_ref, left_ref, right_ref, own_col_ref, own_row_ref, above_ref, below_ref, w_ref,
    taps_ref, act_grad_ref, rim_ref, wide, w_t, rims, bottom, side,
):
    pitch = cols + 16
    depth = g_ref.shape[1]
    last = (rows + 1) * pitch
    size = 2 * rows
    line = 2 * cols + 32
    for p in range(rows):
        wide[(p + 1) * pitch + 8 : (p + 1) * pitch + 8 + cols, :] = g_ref[p * cols : (p + 1) * cols, :].astype(F32)
    for half in range(depth // 128):
        lanes = slice(half * 128, (half + 1) * 128)
        own = own_col_ref[size + half * rows : size + (half + 1) * rows, :].astype(F32)
        rims[0, :, lanes] = left_ref[size + half * rows : size + (half + 1) * rows, :].astype(F32)
        rims[1, :, lanes] = right_ref[2 * size + half * rows : 2 * size + (half + 1) * rows, :].astype(F32)
        side[0, 8 : 8 + rows, lanes] = right_ref[3 * size + half * rows : 3 * size + (half + 1) * rows, :].astype(F32)
        side[1, 8 : 8 + rows, lanes] = rims[1, :, lanes]
        side[2, 8 : 8 + rows, lanes] = own
        over = above_ref[line + half * pitch : line + (half + 1) * pitch, :].astype(F32)
        under = below_ref[2 * line + half * pitch : 2 * line + (half + 1) * pitch, :].astype(F32)
        wide[0:pitch, lanes] = over
        wide[last : last + pitch, lanes] = under
        for b in range(3):
            side[b, 7:8, lanes] = over[9 + cols - b : 10 + cols - b, :]
            side[b, 8 + rows : 9 + rows, lanes] = under[9 + cols - b : 10 + cols - b, :]
        bottom[0, 0:pitch, lanes] = below_ref[3 * line + half * pitch : 3 * line + (half + 1) * pitch, :].astype(F32)
        bottom[1, 0:pitch, lanes] = under
        bottom[2, 0:pitch, lanes] = own_row_ref[line + half * pitch : line + (half + 1) * pitch, :].astype(F32)
    bottom[:, pitch:, :] = jnp.zeros((3, 8, depth), F32)
    for p in range(rows):
        first = (p + 1) * pitch + 7
        wide[first : first + 1, :] = rims[0, p : p + 1, :]
        wide[first + 1 + cols : first + 2 + cols, :] = rims[1, p : p + 1, :]
    for r in range(rows + 2):
        for b in (0, 2):
            first = r * pitch + 9 - b
            taps_ref[b, r * cols : (r + 1) * cols, :] = wide[first : first + cols, :].astype(BF16)
    taps_ref[1, cols : (rows + 1) * cols, :] = g_ref[...]
    taps_ref[1, 0:cols, :] = wide[8 : 8 + cols, :].astype(BF16)
    taps_ref[1, (rows + 1) * cols :, :] = wide[last + 8 : last + 8 + cols, :].astype(BF16)
    for tap in range(9):
        w_t[tap * depth : (tap + 1) * depth, :] = w_ref[tap * depth : (tap + 1) * depth, :].T

    def convolve(i, carry):
        row = pl.multiple_of(i * LONG, LONG)
        parts = []
        for a in range(3):
            for b in range(3):
                parts.append(taps_ref[b, pl.ds(pl.multiple_of(row + (2 - a) * cols, cols), LONG), :])
        act_grad_ref[pl.ds(row, LONG), :] = dot(jnp.concatenate(parts, 1), w_t[...])
        return carry

    lax.fori_loop(0, rows * cols // LONG, convolve, 0)
    parts = []
    for a in range(3):
        for b in range(3):
            low = bottom[a, 9 - b : 17 - b + cols, :]
            beside = side[b, 9 - a : 9 - a + rows, :]
            parts.append(jnp.concatenate([low, beside], 0).astype(BF16))
    rim_ref[...] = dot(jnp.concatenate(parts, 1), w_t[...])


def group_sum(value, depth):
    size = depth // GROUPS
    one = lax.broadcasted_iota(jnp.int32, (depth, depth), 0) // size
    two = lax.broadcasted_iota(jnp.int32, (depth, depth), 1) // size
    same = jnp.where(one == two, 1.0, 0.0).astype(F32)
    return lax.dot_general(
        value, same, (((1,), (0,)), ((), ())), precision=lax.Precision.HIGHEST, preferred_element_type=F32
    )


def space_sum(core_ref, own_ref, pair_ref):
    even = core_ref[0] == 0
    values = [own_ref[0]]
    for k in range(1, own_ref.shape[0]):
        values.append(jnp.where(even, own_ref[k], pair_ref[k]))
        values.append(jnp.where(even, pair_ref[k], own_ref[k]))
    return tree_sum(values[:-1])


def add_kernel(one_ref, two_ref, out_ref):
    out_ref[...] = one_ref[...] + two_ref[...]


def stack_kernel(*refs):
    for k, ref in enumerate(refs[:-1]):
        refs[-1][k] = ref[...]


def normalize(norm_count, core_ref, own_ref, pair_ref, z_ref, act_grad_ref, gain_ref, bias_ref, act_ref, pre_ref, sums_ref, moments_ref):
    cells, depth = z_ref.shape
    total = group_sum(space_sum(core_ref, own_ref, pair_ref), depth) / norm_count
    mean = total[0:1, :]
    inv_std = 1.0 / jnp.sqrt(total[1:2, :] - mean * mean + 1e-05)
    moments_ref[0:1, :] = mean
    moments_ref[1:2, :] = inv_std
    gain = gain_ref[...]
    bias = bias_ref[...]

    def chunk(i, carry):
        row = pl.multiple_of(i * 64, 64)
        normed = (z_ref[pl.ds(row, 64), :] - mean) * inv_std
        shifted = normed * gain + bias
        sig = 1.0 / (1.0 + jnp.exp(-shifted))
        act_ref[pl.ds(row, 64), :] = (shifted * sig).astype(BF16)
        pre = act_grad_ref[pl.ds(row, 64), :] * sig * (1.0 + shifted * (1.0 - sig))
        pre_ref[pl.ds(row, 64), :] = pre
        one = jnp.sum(pre.reshape(8, 8, depth), axis=0)
        two = jnp.sum((pre * normed).reshape(8, 8, depth), axis=0)
        return carry[0] + one, carry[1] + two

    zero = jnp.zeros((8, depth), F32)
    one, two = lax.fori_loop(0, cells // 64, chunk, (zero, zero))
    sums_ref[0:1, :] = jnp.sum(one, axis=0, keepdims=True)
    sums_ref[1:2, :] = jnp.sum(two, axis=0, keepdims=True)


def activate_kernel(norm_count, rows, cols, me_ref, *refs):
    *plain, taps_ref, pre_ref, sums_ref, moments_ref, out_ref, act_ref, whole = refs
    normalize(norm_count, *plain, act_ref, pre_ref, sums_ref, moments_ref)
    cells = rows * cols
    depth = act_ref.shape[1]
    act_t = act_ref[...].T
    for a in range(3):
        for b in range(3):
            first = (2 - a) * cols
            tap = a * 3 + b
            whole[tap * depth : (tap + 1) * depth, :] = dot(act_t, taps_ref[b, first : first + cells, :])
    spread(me_ref, whole, out_ref)


def spread(me_ref, whole, out_ref):
    size = out_ref.shape[1]
    for slot in range(8):
        first = pl.multiple_of((me_ref[0] ^ slot) * size, 16)
        out_ref[slot] = whole[pl.ds(first, size), :]


def conv_grad_kernel(norm_count, rows, cols, me_ref, *refs):
    count = 3
    sums = refs[:count]
    place_ref, z_ref, pre_ref, moments_ref, gain_ref, bias_ref, z_rim_ref, act_rim_ref, t_ref, grad_ref, rim_ref, total_ref, out_ref, whole = refs[count:]
    cells, depth = z_ref.shape
    total = space_sum(*sums)
    total_ref[...] = total
    gain = gain_ref[...]
    means = group_sum(total * gain, depth) / norm_count
    mean = moments_ref[0:1, :]
    inv_std = moments_ref[1:2, :]
    shift = means[0:1, :]
    scale = means[1:2, :]

    def value(z, pre):
        return ((gain * pre - shift - (z - mean) * inv_std * scale) * inv_std).astype(BF16)

    def chunk(i, carry):
        row = pl.multiple_of(i * 64, 64)
        grad_ref[pl.ds(row, 64), :] = value(z_ref[pl.ds(row, 64), :], pre_ref[pl.ds(row, 64), :])
        return carry

    lax.fori_loop(0, cells // 64, chunk, 0)
    z = z_rim_ref[...]
    shifted = (z - mean) * inv_std * gain + bias_ref[...]
    sig = 1.0 / (1.0 + jnp.exp(-shifted))
    pre = act_rim_ref[...] * sig * (1.0 + shifted * (1.0 - sig))
    cell = lax.broadcasted_iota(jnp.int32, z.shape, 0)
    to_right = jnp.where(cell >= cols, place_ref[2], 1)
    to_below = jnp.where(cell < cols + 8, place_ref[3], 1)
    rim_ref[...] = jnp.where(to_right * to_below == 1, value(z, pre).astype(F32), 0.0)

    def product(i, carry):
        row = pl.multiple_of(i * size, 128)
        whole[pl.ds(row, size), :] = dot(t_ref[pl.ds(row, size), :], grad_ref[...])
        return carry

    size = t_ref.shape[0] // 3
    lax.fori_loop(0, 3, product, 0)
    spread(me_ref, whole, out_ref)


def input_kernel(rows, cols, d_ref, rim_ref, w_ref, out_ref, plain, shifted, w_t, wide, mixed):
    cells = rows * cols
    cin = out_ref.shape[2]
    depth = d_ref.shape[1]
    pitch = cols + 8
    plain[0:cells, :] = d_ref[...]
    plain[cells:, :] = rim_ref[0:cols, :].astype(BF16)
    for p in range(rows + 1):
        first = p * pitch
        wide[first : first + cols, :] = plain[p * cols : (p + 1) * cols, :].astype(F32)
        next_cell = cols + 8 + p if p < rows else cols
        wide[first + cols : first + cols + 1, :] = rim_ref[next_cell : next_cell + 1, :]
        shifted[p * cols : (p + 1) * cols, :] = wide[first + 1 : first + 1 + cols, :].astype(BF16)
    for place, tap in enumerate((4, 5, 7, 8, 3, 6, 1, 2, 0)):
        w_t[:, place * cin : (place + 1) * cin] = w_ref[tap * cin : (tap + 1) * cin, :].T
    step = CHUNK // cols

    def chunk(i, carry):
        row = pl.multiple_of(i * CHUNK, CHUNK)
        under = pl.multiple_of(row + cols, cols)
        own = dot(plain[pl.ds(row, CHUNK), :], w_t[:, 0 : 4 * cin])
        right = dot(shifted[pl.ds(row, CHUNK), :], w_t[:, 4 * cin : 6 * cin])
        below = dot(plain[pl.ds(under, CHUNK), :], w_t[:, 6 * cin : 8 * cin])
        corner = dot(shifted[pl.ds(under, CHUNK), :], w_t[:, 8 * cin :])
        even_even = own[:, 0:cin]
        even_odd = own[:, cin : 2 * cin] + right[:, 0:cin]
        odd_even = own[:, 2 * cin : 3 * cin] + below[:, 0:cin]
        odd_odd = own[:, 3 * cin :] + right[:, cin:] + below[:, cin:] + corner
        for parity, pair in enumerate(((even_even, even_odd), (odd_even, odd_odd))):
            for side in range(2):
                mixed[pl.ds(parity, step, stride=2), pl.ds(side, cols, stride=2), :] = pair[side].reshape(
                    step, cols, cin
                )
        out_ref[pl.ds(pl.multiple_of(i * 2 * step, 2 * step), 2 * step)] = mixed[...].astype(BF16)
        return carry

    lax.fori_loop(0, rows // step, chunk, 0)


def half_kernel(slots_ref, other_ref, *refs):
    own_ref, one_ref, two_ref, three_ref = refs[-4:]
    rows = slots_ref.shape[1]
    own_ref[...] = slots_ref[0] + other_ref[0]
    for k, ref in enumerate((one_ref, two_ref, three_ref)):
        ref[0:rows, :] = (slots_ref[k + 1] + other_ref[k + 1]).astype(BF16)
    if len(refs) > 4:
        two_ref[rows:, :] = three_parts(refs[0][...])


def three_parts(pair):
    high = pair.astype(BF16).astype(F32)
    rest = pair - high
    middle = rest.astype(BF16).astype(F32)
    low = rest - middle
    zeros = jnp.zeros((10, pair.shape[1]), F32)
    return jnp.concatenate([high, middle, low, zeros], 0).astype(BF16)


def from_parts(parts):
    parts = parts.astype(F32)
    return parts[0:2, :] + parts[2:4, :] + parts[4:6, :]


def total_kernel(*refs):
    rows = refs[-1].shape[0]
    refs[-1][...] = tree_sum([r[0:rows, :].astype(F32) for r in refs[:-1]]).astype(BF16)


def both_kernel(count, *refs):
    second, first, out_ref = refs[:count], refs[count:-1], refs[-1]
    rows = second[0].shape[0]
    out_ref[0:rows, :] = tree_sum([r[...].astype(F32) for r in second]).astype(BF16)
    out_ref[rows:, :] = tree_sum([r[...].astype(F32) for r in first]).astype(BF16)


def first_total_kernel(own_ref, one_ref, two_ref, three_ref, pair_ref, out_ref, both_ref):
    total_kernel(own_ref, one_ref, two_ref, three_ref, out_ref)
    rows = out_ref.shape[0]
    both_ref[...] = from_parts(three_parts(pair_ref[...])) + from_parts(two_ref[rows:, :])


def gather_kernel(me_ref, *refs):
    me = me_ref[0]
    *own, other_ref, second_ref, first_ref = refs
    rows = second_ref.shape[1]
    for slot in range(4):
        second_ref[me ^ slot] = own[slot][0:rows, :].astype(F32)
        first_ref[me ^ slot] = own[slot][rows:, :].astype(F32)
        second_ref[me ^ slot ^ 4] = other_ref[slot, 0:rows, :].astype(F32)
        first_ref[me ^ slot ^ 4] = other_ref[slot, rows:, :].astype(F32)


def on_device(dp_size, tiles, images, first_weight, norm_gain, norm_bias, second_weight, upstream):
    rows, cols, depth = upstream.shape[2:]
    cin = images.shape[4]
    cells = rows * cols
    group_size = depth // GROUPS
    norm_count = float(cells * tiles * group_size)
    tile_rows = tiles // TCOLS
    axes = ("dp", "space")
    devices = dp_size * tiles

    def flip(value, mask):
        return lax.ppermute(value, axes, [(i, i ^ mask) for i in range(devices)])

    def swapped(value, down, right):
        pairs = []
        for t in range(tiles):
            spot = (t + TCOLS + 2) % tiles
            r, c = spot // TCOLS, spot % TCOLS
            r = r if not down else ((r + down - 1) ^ 1) - down + 1
            c = c if not right else ((c + right - 1) ^ 1) - right + 1
            if 0 <= r < tile_rows and 0 <= c < TCOLS:
                pairs.append((t, (r * TCOLS + c - TCOLS - 2) % tiles))
        return lax.ppermute(value, "space", pairs)

    def space_sums(value, after=()):
        (near,) = call(add_kernel, [shape(value.shape, F32)], [value, flip(value, 1)], after=after)
        parts = [near]
        chips = tiles // 2
        for k in range(1, chips, 2):
            pairs = [(i, i ^ (2 * (k + i % 2))) for i in range(devices) if k + i % 2 < chips]
            parts.append(lax.ppermute(near, axes, pairs))
        (own,) = call(stack_kernel, [shape((len(parts),) + near.shape, F32)], parts)
        return near, parts, [core, own, flip(own, 1)]

    def along(value, size, step):
        return [value] + [flip(value, step * k) for k in range(1, size)]

    def total(parts, after=()):
        if len(parts) == 1:
            return parts[0]
        return call(total_kernel, [shape(parts[0].shape, BF16)], parts, after=after)[0]

    def halved(slots, more=()):
        part = slots.shape[1:]
        longer = (part[0] + 16 * len(more), part[1])
        outs = [shape(part, F32), shape(part, BF16), shape(longer, BF16), shape(part, BF16)]
        return call(half_kernel, outs, [slots, flip(slots[4:8], 1), *more])

    masks = [0, 2, tiles, tiles + 2]

    def quartered(parts):
        return [parts[0]] + [flip(parts[k], masks[k]) for k in (1, 2, 3)]

    def quarters(shard):
        return [shard] + [flip(shard, masks[k]) for k in (1, 2, 3)]

    def gathered(own, after=()):
        (stacked,) = call(stack_kernel, [shape((4,) + own[0].shape, BF16)], own, after=after)
        return own + [flip(stacked, 1)]

    space = lax.axis_index("space")
    me = (space % 2) * 4 + (lax.axis_index("dp") % 2) * 2 + (space // 2) % 2
    me = me.astype(jnp.int32).reshape(1)
    core = (space % 2).astype(jnp.int32).reshape(1)
    spot = (space + TCOLS + 2) % tiles
    column, row = spot % TCOLS, spot // TCOLS
    place = jnp.stack([column % 2, row % 2, column < TCOLS - 1, row < tile_rows - 1]).astype(jnp.int32)
    x = images[0, 0]
    g3 = upstream[0, 0]
    w1 = first_weight.reshape(9 * cin, depth)
    w2 = second_weight.reshape(9 * depth, depth)
    gain = norm_gain.reshape(1, depth)
    bias = norm_bias.reshape(1, depth)

    g_block = (rows, 16, depth)
    smem = pl.BlockSpec(memory_space=pltpu.SMEM)
    vmem = pl.BlockSpec(memory_space=pltpu.VMEM)
    ends = shape((4 * 2 * rows, cin), BF16)
    half_ends = shape((2 * 2 * rows, cin), BF16)
    one, two, own_column = call(
        functools.partial(pack_kernel, rows, cols),
        [ends, ends, half_ends],
        [place, x, x, g3, g3],
        [pltpu.VMEM((2 * rows * 16, cin), F32), pltpu.VMEM((rows * 16, 128), F32)],
        specs=[
            smem,
            pl.BlockSpec((2 * rows, 16, cin), lambda i: (0, 0, 0)),
            pl.BlockSpec((2 * rows, 16, cin), lambda i: (0, 2 * cols // 16 - 1, 0)),
            pl.BlockSpec(g_block, lambda i: (0, 0, 0)),
            pl.BlockSpec(g_block, lambda i: (0, cols // 16 - 1, 0)),
        ],
        grid=(1,),
    )
    one = swapped(one, 0, 1)
    two = swapped(two, 0, 2)
    (planes,) = call(
        functools.partial(planes_kernel, rows, cols),
        [shape((cells + cols, 6 * cin), BF16)],
        [x],
        [pltpu.VMEM((2 * CHUNK // cols, 2 * cols + 8, cin), F32)],
        flops=cells * 9 * cin * depth,
    )
    lines = shape((4 * (2 * cols + 32), cin), BF16)
    half_lines = shape((2 * (2 * cols + 32), cin), BF16)
    from_left, from_right, one, two, own_row = call(
        functools.partial(rows_kernel, rows, cols),
        [half_ends, ends, lines, lines, half_lines],
        [place, x, x, g3, g3, one, two],
        [pltpu.VMEM((2 * cols + 32, cin), F32), pltpu.VMEM((cols + 16, 128), F32)],
        specs=[
            smem,
            pl.BlockSpec((1, 2 * cols, cin), lambda i: (2 * rows - 1, 0, 0)),
            pl.BlockSpec((2, 2 * cols, cin), lambda i: (0, 0, 0)),
            pl.BlockSpec((1, cols, depth), lambda i: (rows - 1, 0, 0)),
            pl.BlockSpec((2, cols, depth), lambda i: (0, 0, 0)),
            vmem,
            vmem,
        ],
        grid=(1,),
        after=[planes],
    )
    got_one = swapped(one, 1, 0)
    got_two = swapped(two, 2, 0)
    (z,) = call(
        functools.partial(stride_kernel, rows, cols),
        [shape((cells, depth), F32)],
        [planes, w1],
        flops=2 * cells * 9 * cin * depth,
        after=[one],
    )
    pads = [pltpu.VMEM((2 * rows + 8, cin), F32), pltpu.VMEM((2 * cols + 8, cin), F32)]
    rim = rows + cols + 8
    z, stats, from_above, from_below, z_rim = call(
        functools.partial(edges_kernel, rows, cols),
        [shape((cells, depth), F32), shape((2, depth), F32), half_lines, lines, shape((rim, depth), F32)],
        [place, z, from_left, from_right, own_column, own_row, got_one, got_two, w1],
        pads
        + [
            pltpu.VMEM((rows, depth), F32),
            pltpu.VMEM((3, 2 * cols + 32, cin), F32),
            pltpu.VMEM((3, 2 * rows + 8, cin), F32),
        ],
        smem=1,
        flops=2 * 80 * 3 * cin * depth,
    )
    _, _, stats = space_sums(stats)
    taps, act_grad, act_rim = call(
        functools.partial(upstream_kernel, rows, cols),
        [shape((3, cells + 2 * cols, depth), BF16), shape((cells, depth), F32), shape((rim, depth), F32)],
        [g3.reshape(cells, depth), from_left, from_right, own_column, own_row, from_above, from_below, w2],
        [
            pltpu.VMEM(((rows + 2) * (cols + 16), depth), F32),
            pltpu.VMEM((9 * depth, depth), BF16),
            pltpu.VMEM((2, rows, depth), F32),
            pltpu.VMEM((3, cols + 24, depth), F32),
            pltpu.VMEM((3, rows + 16, depth), F32),
        ],
        flops=2 * cells * 9 * depth * depth,
    )
    pre_grad, sums, moments, second_slots = call(
        functools.partial(activate_kernel, norm_count, rows, cols),
        [
            shape((cells, depth), F32),
            shape((2, depth), F32),
            shape((2, depth), F32),
            shape((8, 9 * depth // 8, depth), F32),
        ],
        [me] + stats + [z, act_grad, gain, bias, taps],
        [pltpu.VMEM((cells, depth), BF16), pltpu.VMEM((9 * depth, depth), F32)],
        flops=2 * cells * 9 * depth * depth,
        smem=2,
    )
    second_parts = quartered(halved(second_slots))
    near, parts, sums = space_sums(sums, second_parts[:1])
    (windows,) = call(
        functools.partial(windows_kernel, rows, cols),
        [shape((9 * cin, cells), BF16)],
        [planes, from_left, from_above],
        pads + [pltpu.VMEM((cells, cin), F32)],
        flops=2 * cells * 9 * cin * depth,
        after=[parts[0]],
    )
    second_shard = along(total(along(total(second_parts), dp_size // 2, 2 * tiles)), tiles // 4, 4)
    conv_grad, grad_rim, sum_pair, first_slots = call(
        functools.partial(conv_grad_kernel, norm_count, rows, cols),
        [
            shape((cells, depth), BF16),
            shape((rim, depth), F32),
            shape((2, depth), F32),
            shape((8, 9 * cin // 8, depth), F32),
        ],
        [me] + sums + [place, z, pre_grad, moments, gain, bias, z_rim, act_rim, windows],
        [pltpu.VMEM((9 * cin, depth), F32)],
        flops=2 * cells * 9 * cin * depth,
        specs=[smem, smem, vmem, vmem, smem] + [vmem] * 8,
        after=second_shard[:1],
    )
    first_parts = quartered(halved(first_slots, [sum_pair]))
    first_shard, sum_pair = call(
        first_total_kernel,
        [shape(first_slots.shape[1:], BF16), shape((2, depth), F32)],
        first_parts + [sum_pair],
        after=second_shard[1:],
    )
    first_shard = along(total(along(first_shard, dp_size // 2, 2 * tiles)), tiles // 4, 4)
    (input_grad,) = call(
        functools.partial(input_kernel, rows, cols),
        [shape((2 * rows, 2 * cols, cin), BF16)],
        [conv_grad, grad_rim, w1],
        [
            pltpu.VMEM((cells + cols, depth), BF16),
            pltpu.VMEM((cells + cols, depth), BF16),
            pltpu.VMEM((depth, 9 * cin), BF16),
            pltpu.VMEM(((rows + 1) * (cols + 8), depth), F32),
            pltpu.VMEM((2 * CHUNK // cols, 2 * cols, cin), F32),
        ],
        flops=2 * cells * 9 * cin * depth,
    )
    sizes = second_slots.shape[1], first_slots.shape[1]
    (shard,) = call(
        functools.partial(both_kernel, len(second_shard)),
        [shape((sum(sizes), depth), BF16)],
        second_shard + first_shard,
        after=[input_grad],
    )
    for k in range(1, dp_size.bit_length() - 1):
        sum_pair = sum_pair + flip(sum_pair, tiles << k)
    second_grad, first_grad = call(
        gather_kernel,
        [shape((8, sizes[0], depth), F32), shape((8, sizes[1], depth), F32)],
        [me] + gathered(quarters(shard)),
        smem=1,
    )
    return (
        input_grad[None, None],
        first_grad.reshape(first_weight.shape),
        second_grad.reshape(second_weight.shape),
        sum_pair[1],
        sum_pair[0],
    )


def solution(mesh):
    placed = (
        P("dp", "space", None, None, None),
        P(),
        P(),
        P(),
        P(),
        P("dp", "space", None, None, None),
    )
    return jax.shard_map(
        functools.partial(on_device, mesh.shape["dp"], mesh.shape["space"]),
        mesh=mesh,
        in_specs=placed,
        out_specs=(P("dp", "space", None, None, None), P(), P(), P(), P()),
        check_vma=False,
    )
```

```python
import functools

import jax
import jax.numpy as jnp
from jax import lax
from jax.experimental import pallas as pl
from jax.experimental.pallas import tpu as pltpu
from jax.sharding import PartitionSpec as P

GROUPS = 32
TCOLS = 4
F32 = jnp.float32
BF16 = jnp.bfloat16
MIB = 1024 * 1024
CHUNK = 256
LONG = 512


def call(kernel, outs, args, scratch=(), flops=0, limit=20, smem=0, after=(), specs=None, grid=()):
    if specs is None:
        specs = [pl.BlockSpec(memory_space=pltpu.SMEM)] * smem
        specs += [pl.BlockSpec(memory_space=pltpu.VMEM)] * (len(args) - smem)
    moved = sum(a.size * a.dtype.itemsize for a in list(args) + list(outs))
    count = len(args)

    def body(*refs):
        kernel(*refs[:count], *refs[count + len(after) :])

    return pl.pallas_call(
        body,
        out_shape=list(outs),
        grid=grid,
        in_specs=list(specs) + [pl.BlockSpec(memory_space=pl.ANY)] * len(after),
        out_specs=[pl.BlockSpec(memory_space=pltpu.VMEM)] * len(outs),
        scratch_shapes=list(scratch),
        compiler_params=pltpu.CompilerParams(vmem_limit_bytes=limit * MIB),
        cost_estimate=pl.CostEstimate(flops=flops, bytes_accessed=moved, transcendentals=0),
    )(*args, *after)


def shape(dims, dtype):
    return jax.ShapeDtypeStruct(tuple(dims), dtype)


def dot(a, b):
    return lax.dot_general(a, b, (((1,), (0,)), ((), ())), preferred_element_type=F32)


def tree_sum(values):
    while len(values) > 1:
        values = [
            values[i] + values[i + 1] if i + 1 < len(values) else values[i]
            for i in range(0, len(values), 2)
        ]
    return values[0]


def pack_kernel(rows, cols, place_ref, x_first, x_last, g_first, g_last, one_ref, two_ref, own_ref, wide, flat):
    cin = x_first.shape[2]
    even = place_ref[0] == 0

    def x_column(ref, index):
        wide[...] = ref[...].astype(F32).reshape(2 * rows * 16, cin)
        return wide[pl.ds(index, 2 * rows, stride=16), :]

    def g_column(ref, index):
        halves = []
        for half in range(ref.shape[2] // 128):
            flat[...] = ref[:, :, half * 128 : (half + 1) * 128].astype(F32).reshape(rows * 16, 128)
            halves.append(flat[pl.ds(index, rows, stride=16), :])
        return jnp.concatenate(halves, 0)

    size = 2 * rows
    rightwards = (x_column(x_last, 15), g_column(g_last, 15))
    leftwards = (x_column(x_first, 0), x_column(x_first, 1))
    for k in range(2):
        part = slice(k * size, (k + 1) * size)
        own_ref[part, :] = rightwards[k].astype(BF16)
        one_ref[part, :] = jnp.where(even, rightwards[k], leftwards[k]).astype(BF16)
        two_ref[part, :] = jnp.where(even, leftwards[k], rightwards[k]).astype(BF16)
        both = g_column(g_first, k).astype(BF16)
        one_ref[(k + 2) * size : (k + 3) * size, :] = both
        two_ref[(k + 2) * size : (k + 3) * size, :] = both


def choose(even, one, two):
    return jnp.where(even, one.astype(F32), two.astype(F32)).astype(BF16)


def rows_kernel(
    rows, cols, place_ref, x_last, x_first, g_last, g_first, got_one, got_two,
    left_ref, right_ref, one_ref, two_ref, own_ref, x_wide, g_wide,
):
    cin = x_last.shape[2]
    depth = g_last.shape[2]
    even_col = place_ref[0] == 0
    even_row = place_ref[1] == 0
    size = 2 * rows
    left_ref[...] = choose(even_col, got_two[0 : 2 * size, :], got_one[0 : 2 * size, :])
    right_ref[...] = choose(even_col, got_one[...], got_two[...])

    def cell(ref, index):
        first = index // 16 * 16
        return ref[first : first + 16, :].astype(F32)[index - first : index - first + 1, :]

    def x_line(cells, r):
        x_wide[...] = jnp.zeros((2 * cols + 32, cin), F32)
        x_wide[16 : 16 + 2 * cols, :] = cells.astype(F32)
        x_wide[15:16, :] = cell(left_ref, r)
        x_wide[16 + 2 * cols : 17 + 2 * cols, :] = cell(right_ref, r)
        x_wide[17 + 2 * cols : 18 + 2 * cols, :] = cell(right_ref, size + r)
        return x_wide[...]

    def g_line(cells, p):
        halves = []
        for half in range(depth // 128):
            g_wide[...] = jnp.zeros((cols + 16, 128), F32)
            g_wide[8 : 8 + cols, :] = cells[:, half * 128 : (half + 1) * 128].astype(F32)
            g_wide[7:8, :] = cell(left_ref, size + half * rows + p)
            g_wide[8 + cols : 9 + cols, :] = cell(right_ref, 2 * size + half * rows + p)
            g_wide[9 + cols : 10 + cols, :] = cell(right_ref, 3 * size + half * rows + p)
            halves.append(g_wide[...])
        return jnp.concatenate(halves, 0)

    line = 2 * cols + 32
    down = (x_line(x_last[0], 2 * rows - 1), g_line(g_last[0], rows - 1))
    up = (x_line(x_first[0], 0), x_line(x_first[1], 1))
    for k in range(2):
        part = slice(k * line, (k + 1) * line)
        own_ref[part, :] = down[k].astype(BF16)
        one_ref[part, :] = jnp.where(even_row, down[k], up[k]).astype(BF16)
        two_ref[part, :] = jnp.where(even_row, up[k], down[k]).astype(BF16)
        both = g_line(g_first[k], k).astype(BF16)
        one_ref[(k + 2) * line : (k + 3) * line, :] = both
        two_ref[(k + 2) * line : (k + 3) * line, :] = both


def planes_kernel(rows, cols, x_ref, planes_ref, wide):
    cin = x_ref.shape[2]
    planes_ref[0:cols, :] = jnp.zeros((cols, 6 * cin), BF16)
    step = CHUNK // cols
    wide[:, 0:8, :] = jnp.zeros((2 * step, 8, cin), F32)

    def deinterleave(i, carry):
        base = pl.multiple_of(i * 2 * step, 2 * step)
        wide[:, 8 : 8 + 2 * cols, :] = x_ref[pl.ds(base, 2 * step)].astype(F32)
        row = pl.multiple_of((i * step + 1) * cols, cols)
        for parity in range(2):
            for slot, first in enumerate((7, 8, 9)):
                part = wide[pl.ds(parity, step, stride=2), pl.ds(first, cols, stride=2), :]
                lane = (parity * 3 + slot) * cin
                planes_ref[pl.ds(row, CHUNK), lane : lane + cin] = part.reshape(CHUNK, cin).astype(BF16)
        return carry

    lax.fori_loop(0, rows // step, deinterleave, 0)


def stride_kernel(rows, cols, planes_ref, w_ref, z_ref):
    cin = planes_ref.shape[1] // 6

    def convolve(i, carry):
        row = pl.multiple_of(i * LONG, LONG)
        above = planes_ref[pl.ds(row, LONG), 3 * cin :]
        here = planes_ref[pl.ds(pl.multiple_of(row + cols, cols), LONG), :]
        z_ref[pl.ds(row, LONG), :] = dot(jnp.concatenate([above, here], 1), w_ref[...])
        return carry

    lax.fori_loop(0, rows * cols // LONG, convolve, 0)


def edge_parts(rows, cols, xcol_ref, xrow_ref, col_pad, row_pad):
    col_pad[0:8, :] = xrow_ref[0:16, :].astype(F32)[8:16, :]
    col_pad[8 : 8 + 2 * rows, :] = xcol_ref[0 : 2 * rows, :].astype(F32)
    row_pad[0:8, :] = jnp.zeros((8, xrow_ref.shape[1]), F32)
    row_pad[8 : 8 + 2 * cols, :] = xrow_ref[16 : 16 + 2 * cols, :].astype(F32)
    left = [col_pad[pl.ds(first, rows, stride=2), :] for first in (7, 8, 9)]
    over = [row_pad[pl.ds(first, cols, stride=2), :] for first in (7, 8, 9)]
    return left, over


def edges_kernel(
    rows, cols, place_ref, z_in, xcol_ref, right_ref, own_col_ref, own_row_ref, got_one, got_two, w_ref,
    z_ref, stats_ref, xrow_ref, below_ref, z_rim_ref, col_pad, row_pad, rim, bottom, side,
):
    cin = xcol_ref.shape[1]
    even_row = place_ref[1] == 0
    line = 2 * cols + 32
    xrow_ref[...] = choose(even_row, got_two[0 : 2 * line, :], got_one[0 : 2 * line, :])
    below_ref[...] = choose(even_row, got_one[...], got_two[...])
    left, over = edge_parts(rows, cols, xcol_ref, xrow_ref, col_pad, row_pad)
    z_ref[...] = z_in[...]
    from_above = dot(jnp.concatenate(over, 1).astype(BF16), w_ref[0 : 3 * cin])
    from_left = (
        dot(left[0].astype(BF16), w_ref[0:cin])
        + dot(left[1].astype(BF16), w_ref[3 * cin : 4 * cin])
        + dot(left[2].astype(BF16), w_ref[6 * cin : 7 * cin])
    )
    z_ref[0:cols, :] = z_ref[0:cols, :] + from_above
    rim[...] = from_left
    for p in range(rows):
        z_ref[p * cols : p * cols + 1, :] = z_ref[p * cols : p * cols + 1, :] + rim[p : p + 1, :]
    z = z_ref[...]
    stats_ref[0:1, :] = jnp.sum(z, axis=0, keepdims=True)
    stats_ref[1:2, :] = jnp.sum(z * z, axis=0, keepdims=True)
    bottom[0] = own_row_ref[0:line, :].astype(F32)
    bottom[1] = below_ref[0:line, :].astype(F32)
    bottom[2] = below_ref[line : 2 * line, :].astype(F32)
    over_end = xrow_ref[2 * cols : 2 * cols + 32, :].astype(F32)
    for b, ref in enumerate((own_col_ref, right_ref, right_ref)):
        first = 2 * rows if b == 2 else 0
        side[b, 8:, :] = ref[first : first + 2 * rows, :].astype(F32)
        side[b, 7:8, :] = over_end[15 + b : 16 + b, :]
    parts = []
    for a in range(3):
        for b in range(3):
            low = bottom[a, pl.ds(15 + b, cols + 8, stride=2), :]
            beside = side[b, pl.ds(7 + a, rows, stride=2), :]
            parts.append(jnp.concatenate([low, beside], 0).astype(BF16))
    z_rim_ref[...] = dot(jnp.concatenate(parts, 1), w_ref[...])


def windows_kernel(rows, cols, planes_ref, xcol_ref, xrow_ref, t_ref, col_pad, row_pad, wide):
    cin = xrow_ref.shape[1]
    cells = rows * cols
    left, over = edge_parts(rows, cols, xcol_ref, xrow_ref, col_pad, row_pad)
    for half, parts in ((0, left[1]), (3, left[2])):
        wide[...] = planes_ref[cols:, half * cin : (half + 1) * cin].astype(F32)
        wide[pl.ds(0, rows, stride=cols), :] = parts
        window = wide[...].astype(BF16)
        t_ref[(half + 3) * cin : (half + 4) * cin, :] = window.T
    wide[cols:, :] = planes_ref[cols:cells, 3 * cin : 4 * cin].astype(F32)
    wide[0:cols, :] = over[0]
    wide[pl.ds(0, rows, stride=cols), :] = left[0]
    t_ref[0:cin, :] = wide[...].astype(BF16).T
    for slot in (1, 2):
        lane = (3 + slot) * cin
        below = planes_ref[cols:cells, lane : lane + cin]
        window = jnp.concatenate([over[slot].astype(BF16), below], 0)
        t_ref[slot * cin : (slot + 1) * cin, :] = window.T
    for slot in (1, 2, 4, 5):
        lane = slot * cin
        t_ref[lane + 3 * cin : lane + 4 * cin, :] = planes_ref[cols:, lane : lane + cin].T


def upstream_kernel(
    rows, cols, g_ref, left_ref, right_ref, own_col_ref, own_row_ref, above_ref, below_ref, w_ref,
    taps_ref, act_grad_ref, rim_ref, wide, w_t, rims, bottom, side,
):
    pitch = cols + 16
    depth = g_ref.shape[1]
    last = (rows + 1) * pitch
    size = 2 * rows
    line = 2 * cols + 32
    for p in range(rows):
        wide[(p + 1) * pitch + 8 : (p + 1) * pitch + 8 + cols, :] = g_ref[p * cols : (p + 1) * cols, :].astype(F32)
    for half in range(depth // 128):
        lanes = slice(half * 128, (half + 1) * 128)
        own = own_col_ref[size + half * rows : size + (half + 1) * rows, :].astype(F32)
        rims[0, :, lanes] = left_ref[size + half * rows : size + (half + 1) * rows, :].astype(F32)
        rims[1, :, lanes] = right_ref[2 * size + half * rows : 2 * size + (half + 1) * rows, :].astype(F32)
        side[0, 8 : 8 + rows, lanes] = right_ref[3 * size + half * rows : 3 * size + (half + 1) * rows, :].astype(F32)
        side[1, 8 : 8 + rows, lanes] = rims[1, :, lanes]
        side[2, 8 : 8 + rows, lanes] = own
        over = above_ref[line + half * pitch : line + (half + 1) * pitch, :].astype(F32)
        under = below_ref[2 * line + half * pitch : 2 * line + (half + 1) * pitch, :].astype(F32)
        wide[0:pitch, lanes] = over
        wide[last : last + pitch, lanes] = under
        for b in range(3):
            side[b, 7:8, lanes] = over[9 + cols - b : 10 + cols - b, :]
            side[b, 8 + rows : 9 + rows, lanes] = under[9 + cols - b : 10 + cols - b, :]
        bottom[0, 0:pitch, lanes] = below_ref[3 * line + half * pitch : 3 * line + (half + 1) * pitch, :].astype(F32)
        bottom[1, 0:pitch, lanes] = under
        bottom[2, 0:pitch, lanes] = own_row_ref[line + half * pitch : line + (half + 1) * pitch, :].astype(F32)
    bottom[:, pitch:, :] = jnp.zeros((3, 8, depth), F32)
    for p in range(rows):
        first = (p + 1) * pitch + 7
        wide[first : first + 1, :] = rims[0, p : p + 1, :]
        wide[first + 1 + cols : first + 2 + cols, :] = rims[1, p : p + 1, :]
    for r in range(rows + 2):
        for b in (0, 2):
            first = r * pitch + 9 - b
            taps_ref[b, r * cols : (r + 1) * cols, :] = wide[first : first + cols, :].astype(BF16)
    taps_ref[1, cols : (rows + 1) * cols, :] = g_ref[...]
    taps_ref[1, 0:cols, :] = wide[8 : 8 + cols, :].astype(BF16)
    taps_ref[1, (rows + 1) * cols :, :] = wide[last + 8 : last + 8 + cols, :].astype(BF16)
    for tap in range(9):
        w_t[tap * depth : (tap + 1) * depth, :] = w_ref[tap * depth : (tap + 1) * depth, :].T

    def convolve(i, carry):
        row = pl.multiple_of(i * LONG, LONG)
        parts = []
        for a in range(3):
            for b in range(3):
                parts.append(taps_ref[b, pl.ds(pl.multiple_of(row + (2 - a) * cols, cols), LONG), :])
        act_grad_ref[pl.ds(row, LONG), :] = dot(jnp.concatenate(parts, 1), w_t[...])
        return carry

    lax.fori_loop(0, rows * cols // LONG, convolve, 0)
    parts = []
    for a in range(3):
        for b in range(3):
            low = bottom[a, 9 - b : 17 - b + cols, :]
            beside = side[b, 9 - a : 9 - a + rows, :]
            parts.append(jnp.concatenate([low, beside], 0).astype(BF16))
    rim_ref[...] = dot(jnp.concatenate(parts, 1), w_t[...])


def group_sum(value, depth):
    size = depth // GROUPS
    one = lax.broadcasted_iota(jnp.int32, (depth, depth), 0) // size
    two = lax.broadcasted_iota(jnp.int32, (depth, depth), 1) // size
    same = jnp.where(one == two, 1.0, 0.0).astype(F32)
    return lax.dot_general(
        value, same, (((1,), (0,)), ((), ())), precision=lax.Precision.HIGHEST, preferred_element_type=F32
    )


def add_kernel(*refs):
    refs[-1][...] = tree_sum([r[...] for r in refs[:-1]])


def stack_kernel(*refs):
    for k, ref in enumerate(refs[:-1]):
        refs[-1][k] = ref[...]


def activate_kernel(norm_count, own_ref, pair_ref, z_ref, act_grad_ref, gain_ref, bias_ref, act_ref, pre_ref, sums_ref, moments_ref):
    cells, depth = z_ref.shape
    total = group_sum(own_ref[...] + pair_ref[...], depth) / norm_count
    mean = total[0:1, :]
    inv_std = 1.0 / jnp.sqrt(total[1:2, :] - mean * mean + 1e-05)
    moments_ref[0:1, :] = mean
    moments_ref[1:2, :] = inv_std
    gain = gain_ref[...]
    bias = bias_ref[...]

    def chunk(i, carry):
        row = pl.multiple_of(i * 64, 64)
        normed = (z_ref[pl.ds(row, 64), :] - mean) * inv_std
        shifted = normed * gain + bias
        sig = 1.0 / (1.0 + jnp.exp(-shifted))
        act_ref[pl.ds(row, 64), :] = (shifted * sig).astype(BF16)
        pre = act_grad_ref[pl.ds(row, 64), :] * sig * (1.0 + shifted * (1.0 - sig))
        pre_ref[pl.ds(row, 64), :] = pre
        one = jnp.sum(pre.reshape(8, 8, depth), axis=0)
        two = jnp.sum((pre * normed).reshape(8, 8, depth), axis=0)
        return carry[0] + one, carry[1] + two

    zero = jnp.zeros((8, depth), F32)
    one, two = lax.fori_loop(0, cells // 64, chunk, (zero, zero))
    sums_ref[0:1, :] = jnp.sum(one, axis=0, keepdims=True)
    sums_ref[1:2, :] = jnp.sum(two, axis=0, keepdims=True)


def second_kernel(rows, cols, place_ref, act_ref, taps_ref, keep_ref, send_ref, whole):
    cells = rows * cols
    depth = act_ref.shape[1]
    act_t = act_ref[...].T
    for a in range(3):
        for b in range(3):
            first = (2 - a) * cols
            tap = a * 3 + b
            whole[tap * depth : (tap + 1) * depth, :] = dot(act_t, taps_ref[b, first : first + cells, :])
    spread(place_ref, whole, keep_ref, send_ref)


def spread(place_ref, whole, keep_ref, send_ref):
    size = keep_ref.shape[1]
    for slot in range(4):
        first = pl.multiple_of((place_ref[5] ^ slot) * size, 16)
        keep_ref[slot] = whole[pl.ds(first, size), :]
        first = pl.multiple_of((place_ref[5] ^ slot ^ 4) * size, 16)
        send_ref[slot] = whole[pl.ds(first, size), :].astype(BF16)


def conv_grad_kernel(norm_count, rows, cols, place_ref, own_ref, pair_ref, *refs):
    z_ref, pre_ref, moments_ref, gain_ref, bias_ref, z_rim_ref, act_rim_ref, t_ref = refs[:8]
    grad_ref, rim_ref, total_ref, keep_ref, send_ref, whole = refs[8:]
    cells, depth = z_ref.shape
    total = own_ref[...] + pair_ref[...]
    total_ref[...] = total
    gain = gain_ref[...]
    means = group_sum(total * gain, depth) / norm_count
    mean = moments_ref[0:1, :]
    inv_std = moments_ref[1:2, :]
    shift = means[0:1, :]
    scale = means[1:2, :]

    def value(z, pre):
        return ((gain * pre - shift - (z - mean) * inv_std * scale) * inv_std).astype(BF16)

    def chunk(i, carry):
        row = pl.multiple_of(i * 64, 64)
        grad_ref[pl.ds(row, 64), :] = value(z_ref[pl.ds(row, 64), :], pre_ref[pl.ds(row, 64), :])
        return carry

    lax.fori_loop(0, cells // 64, chunk, 0)
    z = z_rim_ref[...]
    shifted = (z - mean) * inv_std * gain + bias_ref[...]
    sig = 1.0 / (1.0 + jnp.exp(-shifted))
    pre = act_rim_ref[...] * sig * (1.0 + shifted * (1.0 - sig))
    cell = lax.broadcasted_iota(jnp.int32, z.shape, 0)
    to_right = jnp.where(cell >= cols, place_ref[2], 1)
    to_below = jnp.where(cell < cols + 8, place_ref[3], 1)
    rim_ref[...] = jnp.where(to_right * to_below == 1, value(z, pre).astype(F32), 0.0)

    def product(i, carry):
        row = pl.multiple_of(i * size, 128)
        whole[pl.ds(row, size), :] = dot(t_ref[pl.ds(row, size), :], grad_ref[...])
        return carry

    size = t_ref.shape[0] // 3
    lax.fori_loop(0, 3, product, 0)
    spread(place_ref, whole, keep_ref, send_ref)


def input_kernel(rows, cols, d_ref, rim_ref, w_ref, out_ref, done_ref, plain, shifted, w_t, wide, mixed):
    cells = rows * cols
    cin = out_ref.shape[2]
    depth = d_ref.shape[1]
    pitch = cols + 8
    plain[0:cells, :] = d_ref[...]
    plain[cells:, :] = rim_ref[0:cols, :].astype(BF16)
    for p in range(rows + 1):
        first = p * pitch
        wide[first : first + cols, :] = plain[p * cols : (p + 1) * cols, :].astype(F32)
        next_cell = cols + 8 + p if p < rows else cols
        wide[first + cols : first + cols + 1, :] = rim_ref[next_cell : next_cell + 1, :]
        shifted[p * cols : (p + 1) * cols, :] = wide[first + 1 : first + 1 + cols, :].astype(BF16)
    for place, tap in enumerate((4, 5, 7, 8, 3, 6, 1, 2, 0)):
        w_t[:, place * cin : (place + 1) * cin] = w_ref[tap * cin : (tap + 1) * cin, :].T
    done_ref[...] = jnp.zeros(done_ref.shape, F32)
    step = CHUNK // cols

    def chunk(i, carry):
        row = pl.multiple_of(i * CHUNK, CHUNK)
        under = pl.multiple_of(row + cols, cols)
        own = dot(plain[pl.ds(row, CHUNK), :], w_t[:, 0 : 4 * cin])
        right = dot(shifted[pl.ds(row, CHUNK), :], w_t[:, 4 * cin : 6 * cin])
        below = dot(plain[pl.ds(under, CHUNK), :], w_t[:, 6 * cin : 8 * cin])
        corner = dot(shifted[pl.ds(under, CHUNK), :], w_t[:, 8 * cin :])
        even_even = own[:, 0:cin]
        even_odd = own[:, cin : 2 * cin] + right[:, 0:cin]
        odd_even = own[:, 2 * cin : 3 * cin] + below[:, 0:cin]
        odd_odd = own[:, 3 * cin :] + right[:, cin:] + below[:, cin:] + corner
        for parity, pair in enumerate(((even_even, even_odd), (odd_even, odd_odd))):
            for side in range(2):
                mixed[pl.ds(parity, step, stride=2), pl.ds(side, cols, stride=2), :] = pair[side].reshape(
                    step, cols, cin
                )
        out_ref[pl.ds(pl.multiple_of(i * 2 * step, 2 * step), 2 * step)] = mixed[...].astype(BF16)
        return carry

    lax.fori_loop(0, rows // step, chunk, 0)


def first_split_kernel(place_ref, mine_ref, other_ref, keep_ref, send_ref):
    even = place_ref[4] == 0
    none, along_y, along_x, both = [mine_ref[k] + other_ref[k].astype(F32) for k in range(4)]
    keep_ref[0] = none
    keep_ref[1] = jnp.where(even, along_y, along_x)
    send_ref[0] = jnp.where(even, along_x, along_y).astype(BF16)
    send_ref[1] = both.astype(BF16)


def second_split_kernel(mine_ref, other_ref, keep_ref, send_ref):
    keep_ref[...] = mine_ref[0] + other_ref[0].astype(F32)
    send_ref[...] = (mine_ref[1] + other_ref[1].astype(F32)).astype(BF16)


def half_kernel(slots_ref, other_ref, *refs):
    own_ref, one_ref, two_ref, three_ref = refs[-4:]
    rows = slots_ref.shape[1]
    own_ref[...] = slots_ref[0] + other_ref[0]
    for k, ref in enumerate((one_ref, two_ref, three_ref)):
        ref[0:rows, :] = (slots_ref[k + 1] + other_ref[k + 1]).astype(BF16)
    if len(refs) > 4:
        two_ref[rows:, :] = three_parts(refs[0][...])


def three_parts(pair):
    high = pair.astype(BF16).astype(F32)
    rest = pair - high
    middle = rest.astype(BF16).astype(F32)
    low = rest - middle
    zeros = jnp.zeros((10, pair.shape[1]), F32)
    return jnp.concatenate([high, middle, low, zeros], 0).astype(BF16)


def from_parts(parts):
    parts = parts.astype(F32)
    return parts[0:2, :] + parts[2:4, :] + parts[4:6, :]


def total_kernel(*refs):
    rows = refs[-1].shape[0]
    refs[-1][...] = tree_sum([r[0:rows, :].astype(F32) for r in refs[:-1]]).astype(BF16)


def both_kernel(count, *refs):
    second, first, out_ref = refs[:count], refs[count:-1], refs[-1]
    rows = second[0].shape[0]
    out_ref[0:rows, :] = tree_sum([r[...].astype(F32) for r in second]).astype(BF16)
    out_ref[rows:, :] = tree_sum([r[...].astype(F32) for r in first]).astype(BF16)


def first_total_kernel(own_ref, one_ref, two_ref, three_ref, pair_ref, out_ref, bias_ref, gain_ref):
    total_kernel(own_ref, one_ref, two_ref, three_ref, out_ref)
    rows = out_ref.shape[0]
    both = from_parts(three_parts(pair_ref[...])) + from_parts(two_ref[rows:, :])
    bias_ref[...] = both[0:1, :]
    gain_ref[...] = both[1:2, :]


def gather_kernel(place_ref, *refs):
    me = place_ref[5]
    *own, other_ref, second_ref, first_ref = refs
    rows = second_ref.shape[1]
    for slot in range(4):
        second_ref[me ^ slot] = own[slot][0:rows, :].astype(F32)
        first_ref[me ^ slot] = own[slot][rows:, :].astype(F32)
        second_ref[me ^ slot ^ 4] = other_ref[slot, 0:rows, :].astype(F32)
        first_ref[me ^ slot ^ 4] = other_ref[slot, rows:, :].astype(F32)


def on_device(dp_size, tiles, images, first_weight, norm_gain, norm_bias, second_weight, upstream):
    rows, cols, depth = upstream.shape[2:]
    cin = images.shape[4]
    cells = rows * cols
    group_size = depth // GROUPS
    norm_count = float(cells * tiles * group_size)
    tile_rows = tiles // TCOLS
    axes = ("dp", "space")
    devices = dp_size * tiles

    def flip(value, mask):
        return lax.ppermute(value, axes, [(i, i ^ mask) for i in range(devices)])

    def swapped(value, down, right):
        pairs = []
        for t in range(tiles):
            spot = (t + TCOLS + 2) % tiles
            r, c = spot // TCOLS, spot % TCOLS
            r = r if not down else ((r + down - 1) ^ 1) - down + 1
            c = c if not right else ((c + right - 1) ^ 1) - right + 1
            if 0 <= r < tile_rows and 0 <= c < TCOLS:
                pairs.append((t, (r * TCOLS + c - TCOLS - 2) % tiles))
        return lax.ppermute(value, "space", pairs)

    def added(parts, after=()):
        return call(add_kernel, [shape(parts[0].shape, F32)], parts, after=after)[0]

    def fetched(value, after=()):
        parts = [value] + [flip(value, 2 * k) for k in (1, 2, 3)]
        for k in range(3, tiles.bit_length() - 1):
            total = added(parts, after)
            parts, after = [total, flip(total, 1 << k)], ()
        return parts

    def crossed(value, even, odd):
        return lax.ppermute(value, axes, [(i, i ^ (odd if i % 2 else even)) for i in range(devices)])

    def along(value, size, step):
        return [value] + [flip(value, step * k) for k in range(1, size)]

    def total(parts, after=()):
        if len(parts) == 1:
            return parts[0]
        return call(total_kernel, [shape(parts[0].shape, BF16)], parts, after=after)[0]

    def halved(slots, more=(), after=()):
        part = slots[0].shape[1:]
        longer = (part[0] + 16 * len(more), part[1])
        outs = [shape(part, F32), shape(part, BF16), shape(longer, BF16), shape(part, BF16)]
        return call(half_kernel, outs, [slots[0], flip(slots[1], 1), *more], after=after)

    masks = [0, 2, tiles, tiles + 2]

    def quartered(parts):
        return [parts[0]] + [flip(parts[k], masks[k]) for k in (1, 2, 3)]

    def quarters(shard):
        return [shard] + [flip(shard, masks[k]) for k in (1, 2, 3)]

    def gathered(own, after=()):
        (stacked,) = call(stack_kernel, [shape((4,) + own[0].shape, BF16)], own, after=after)
        return own + [flip(stacked, 1)]

    space = lax.axis_index("space")
    spot = (space + TCOLS + 2) % tiles
    column, row = spot % TCOLS, spot // TCOLS
    me = (space % 2) * 4 + (lax.axis_index("dp") % 2) * 2 + (space // 2) % 2
    place = jnp.stack([column % 2, row % 2, column < TCOLS - 1, row < tile_rows - 1, space % 2, me]).astype(jnp.int32)
    x = images[0, 0]
    g3 = upstream[0, 0]
    w1 = first_weight.reshape(9 * cin, depth)
    w2 = second_weight.reshape(9 * depth, depth)
    gain = norm_gain.reshape(1, depth)
    bias = norm_bias.reshape(1, depth)

    g_block = (rows, 16, depth)
    smem = pl.BlockSpec(memory_space=pltpu.SMEM)
    vmem = pl.BlockSpec(memory_space=pltpu.VMEM)
    ends = shape((4 * 2 * rows, cin), BF16)
    half_ends = shape((2 * 2 * rows, cin), BF16)
    one, two, own_column = call(
        functools.partial(pack_kernel, rows, cols),
        [ends, ends, half_ends],
        [place, x, x, g3, g3],
        [pltpu.VMEM((2 * rows * 16, cin), F32), pltpu.VMEM((rows * 16, 128), F32)],
        specs=[
            smem,
            pl.BlockSpec((2 * rows, 16, cin), lambda i: (0, 0, 0)),
            pl.BlockSpec((2 * rows, 16, cin), lambda i: (0, 2 * cols // 16 - 1, 0)),
            pl.BlockSpec(g_block, lambda i: (0, 0, 0)),
            pl.BlockSpec(g_block, lambda i: (0, cols // 16 - 1, 0)),
        ],
        grid=(1,),
    )
    one = swapped(one, 0, 1)
    two = swapped(two, 0, 2)
    (planes,) = call(
        functools.partial(planes_kernel, rows, cols),
        [shape((cells + cols, 6 * cin), BF16)],
        [x],
        [pltpu.VMEM((2 * CHUNK // cols, 2 * cols + 8, cin), F32)],
        flops=cells * 9 * cin * depth,
    )
    lines = shape((4 * (2 * cols + 32), cin), BF16)
    half_lines = shape((2 * (2 * cols + 32), cin), BF16)
    from_left, from_right, one, two, own_row = call(
        functools.partial(rows_kernel, rows, cols),
        [half_ends, ends, lines, lines, half_lines],
        [place, x, x, g3, g3, one, two],
        [pltpu.VMEM((2 * cols + 32, cin), F32), pltpu.VMEM((cols + 16, 128), F32)],
        specs=[
            smem,
            pl.BlockSpec((1, 2 * cols, cin), lambda i: (2 * rows - 1, 0, 0)),
            pl.BlockSpec((2, 2 * cols, cin), lambda i: (0, 0, 0)),
            pl.BlockSpec((1, cols, depth), lambda i: (rows - 1, 0, 0)),
            pl.BlockSpec((2, cols, depth), lambda i: (0, 0, 0)),
            vmem,
            vmem,
        ],
        grid=(1,),
        after=[planes],
    )
    got_one = swapped(one, 1, 0)
    got_two = swapped(two, 2, 0)
    (z,) = call(
        functools.partial(stride_kernel, rows, cols),
        [shape((cells, depth), F32)],
        [planes, w1],
        flops=2 * cells * 9 * cin * depth,
        after=[one],
    )
    pads = [pltpu.VMEM((2 * rows + 8, cin), F32), pltpu.VMEM((2 * cols + 8, cin), F32)]
    rim = rows + cols + 8
    z, stats, from_above, from_below, z_rim = call(
        functools.partial(edges_kernel, rows, cols),
        [shape((cells, depth), F32), shape((2, depth), F32), half_lines, lines, shape((rim, depth), F32)],
        [place, z, from_left, from_right, own_column, own_row, got_one, got_two, w1],
        pads
        + [
            pltpu.VMEM((rows, depth), F32),
            pltpu.VMEM((3, 2 * cols + 32, cin), F32),
            pltpu.VMEM((3, 2 * rows + 8, cin), F32),
        ],
        smem=1,
        flops=2 * 80 * 3 * cin * depth,
    )
    stats = fetched(added([stats, flip(stats, 1)]))
    taps, act_grad, act_rim = call(
        functools.partial(upstream_kernel, rows, cols),
        [shape((3, cells + 2 * cols, depth), BF16), shape((cells, depth), F32), shape((rim, depth), F32)],
        [g3.reshape(cells, depth), from_left, from_right, own_column, own_row, from_above, from_below, w2],
        [
            pltpu.VMEM(((rows + 2) * (cols + 16), depth), F32),
            pltpu.VMEM((9 * depth, depth), BF16),
            pltpu.VMEM((2, rows, depth), F32),
            pltpu.VMEM((3, cols + 24, depth), F32),
            pltpu.VMEM((3, rows + 16, depth), F32),
        ],
        flops=2 * cells * 9 * depth * depth,
    )
    activated, pre_grad, sums, moments = call(
        functools.partial(activate_kernel, norm_count),
        [shape((cells, depth), BF16), shape((cells, depth), F32), shape((2, depth), F32), shape((2, depth), F32)],
        stats + [z, act_grad, gain, bias],
        flops=cells * depth * 30,
    )
    other = flip(sums, 1)
    second_slots = call(
        functools.partial(second_kernel, rows, cols),
        [shape((4, 9 * depth // 8, depth), F32), shape((4, 9 * depth // 8, depth), BF16)],
        [place, activated, taps],
        [pltpu.VMEM((9 * depth, depth), F32)],
        flops=2 * cells * 9 * depth * depth,
        smem=1,
    )
    near = added([sums, other], second_slots[1:])
    part = second_slots[0].shape[1:]
    kept, sent = call(
        first_split_kernel,
        [shape((2,) + part, F32), shape((2,) + part, BF16)],
        [place, second_slots[0], flip(second_slots[1], 1)],
        smem=1,
        after=[near],
    )
    parts = fetched(near, [kept])
    second_parts = call(
        second_split_kernel,
        [shape(part, F32), shape(part, BF16)],
        [kept, crossed(sent, tiles, 2)],
        after=parts[:1],
    )
    (windows,) = call(
        functools.partial(windows_kernel, rows, cols),
        [shape((9 * cin, cells), BF16)],
        [planes, from_left, from_above],
        pads + [pltpu.VMEM((cells, cin), F32)],
        flops=2 * cells * 9 * cin * depth,
        after=second_parts[:1],
    )
    second_shard = total([second_parts[0], crossed(second_parts[1], 2, tiles)])
    pair = along(total(along(second_shard, dp_size // 2, 2 * tiles)), tiles // 4, 4)
    conv_grad, grad_rim, sum_pair, *first_slots = call(
        functools.partial(conv_grad_kernel, norm_count, rows, cols),
        [
            shape((cells, depth), BF16),
            shape((rim, depth), F32),
            shape((2, depth), F32),
            shape((4, 9 * cin // 8, depth), F32),
            shape((4, 9 * cin // 8, depth), BF16),
        ],
        [place] + parts + [z, pre_grad, moments, gain, bias, z_rim, act_rim, windows],
        [pltpu.VMEM((9 * cin, depth), F32)],
        flops=2 * cells * 9 * cin * depth,
        smem=1,
        after=[second_shard],
    )
    first_parts = quartered(halved(first_slots, [sum_pair]))
    first_shard, bias_grad, gain_grad = call(
        first_total_kernel,
        [shape(first_slots[0].shape[1:], BF16), shape((1, depth), F32), shape((1, depth), F32)],
        first_parts + [sum_pair],
    )
    first_shard = along(total(along(first_shard, dp_size // 2, 2 * tiles)), tiles // 4, 4)
    input_grad, done = call(
        functools.partial(input_kernel, rows, cols),
        [shape((2 * rows, 2 * cols, cin), BF16), shape((8, 128), F32)],
        [conv_grad, grad_rim, w1],
        [
            pltpu.VMEM((cells + cols, depth), BF16),
            pltpu.VMEM((cells + cols, depth), BF16),
            pltpu.VMEM((depth, 9 * cin), BF16),
            pltpu.VMEM(((rows + 1) * (cols + 8), depth), F32),
            pltpu.VMEM((2 * CHUNK // cols, 2 * cols, cin), F32),
        ],
        flops=2 * cells * 9 * cin * depth,
    )
    sizes = second_slots[0].shape[1], first_slots[0].shape[1]
    (shard,) = call(
        functools.partial(both_kernel, len(pair)),
        [shape((sum(sizes), depth), BF16)],
        pair + first_shard,
        after=[done],
    )
    for k in range(1, dp_size.bit_length() - 1):
        bias_grad = bias_grad + flip(bias_grad, tiles << k)
        gain_grad = gain_grad + flip(gain_grad, tiles << k)
    second_grad, first_grad = call(
        gather_kernel,
        [shape((8, sizes[0], depth), F32), shape((8, sizes[1], depth), F32)],
        [place] + gathered(quarters(shard)),
        smem=1,
    )
    return (
        input_grad[None, None],
        first_grad.reshape(first_weight.shape),
        second_grad.reshape(second_weight.shape),
        gain_grad.reshape(depth),
        bias_grad.reshape(depth),
    )


def solution(mesh):
    placed = (
        P("dp", "space", None, None, None),
        P(),
        P(),
        P(),
        P(),
        P("dp", "space", None, None, None),
    )
    return jax.shard_map(
        functools.partial(on_device, mesh.shape["dp"], mesh.shape["space"]),
        mesh=mesh,
        in_specs=placed,
        out_specs=(P("dp", "space", None, None, None), P(), P(), P(), P()),
        check_vma=False,
    )
```

```python
import functools

import jax
import jax.numpy as jnp
from jax import lax
from jax.experimental import pallas as pl
from jax.experimental.pallas import tpu as pltpu
from jax.sharding import PartitionSpec as P

GROUPS = 32
TCOLS = 4
F32 = jnp.float32
BF16 = jnp.bfloat16
MIB = 1024 * 1024
CHUNK = 256
LONG = 512


def call(kernel, outs, args, scratch=(), flops=0, limit=20, smem=0, after=(), specs=None, grid=(), out_specs=None, aliases=None):
    if specs is None:
        specs = [pl.BlockSpec(memory_space=pltpu.SMEM)] * smem
        specs += [pl.BlockSpec(memory_space=pltpu.VMEM)] * (len(args) - smem)
    moved = sum(a.size * a.dtype.itemsize for a in list(args) + list(outs))
    count = len(args)

    def body(*refs):
        kernel(*refs[:count], *refs[count + len(after) :])

    return pl.pallas_call(
        body,
        out_shape=list(outs),
        grid=grid,
        in_specs=list(specs) + [pl.BlockSpec(memory_space=pl.ANY)] * len(after),
        out_specs=out_specs or [pl.BlockSpec(memory_space=pltpu.VMEM)] * len(outs),
        scratch_shapes=list(scratch),
        input_output_aliases=aliases or {},
        compiler_params=pltpu.CompilerParams(vmem_limit_bytes=limit * MIB),
        cost_estimate=pl.CostEstimate(flops=flops, bytes_accessed=moved, transcendentals=0),
    )(*args, *after)


def shape(dims, dtype):
    return jax.ShapeDtypeStruct(tuple(dims), dtype)


def dot(a, b):
    return lax.dot_general(a, b, (((1,), (0,)), ((), ())), preferred_element_type=F32)


def tree_sum(values):
    while len(values) > 1:
        values = [
            values[i] + values[i + 1] if i + 1 < len(values) else values[i]
            for i in range(0, len(values), 2)
        ]
    return values[0]


def pack_kernel(
    rows, cols, place_ref, x_ref, g_ref, one_ref, two_ref, own_ref, x_lines, g_lines, x_first, x_last, g_first, g_last, wide, flat, sems,
):
    cin = x_first.shape[2]
    even = place_ref[0] == 0
    copies = [
        pltpu.make_async_copy(source, target, sems.at[k])
        for k, (source, target) in enumerate(
            (
                (x_ref.at[:, 2 * cols - 16 : 2 * cols, :], x_last),
                (x_ref.at[:, 0:16, :], x_first),
                (g_ref.at[:, cols - 16 : cols, :], g_last),
                (g_ref.at[:, 0:16, :], g_first),
                (x_ref.at[2 * rows - 1], x_lines.at[0]),
                (x_ref.at[0:2], x_lines.at[1:3]),
                (g_ref.at[rows - 1], g_lines.at[0]),
                (g_ref.at[0:2], g_lines.at[1:3]),
            )
        )
    ]
    for copy in copies:
        copy.start()

    def x_column(ref, index):
        wide[...] = ref[...].astype(F32).reshape(2 * rows * 16, cin)
        return wide[pl.ds(index, 2 * rows, stride=16), :]

    def g_column(ref, index):
        halves = []
        for half in range(ref.shape[2] // 128):
            flat[...] = ref[:, :, half * 128 : (half + 1) * 128].astype(F32).reshape(rows * 16, 128)
            halves.append(flat[pl.ds(index, rows, stride=16), :])
        return jnp.concatenate(halves, 0)

    size = 2 * rows
    copies[0].wait()
    last = x_column(x_last, 15)
    copies[1].wait()
    leftwards = (x_column(x_first, 0), x_column(x_first, 1))
    copies[2].wait()
    rightwards = (last, g_column(g_last, 15))
    for copy in copies[3:]:
        copy.wait()
    for k in range(2):
        part = slice(k * size, (k + 1) * size)
        own_ref[part, :] = rightwards[k].astype(BF16)
        one_ref[part, :] = jnp.where(even, rightwards[k], leftwards[k]).astype(BF16)
        two_ref[part, :] = jnp.where(even, leftwards[k], rightwards[k]).astype(BF16)
        both = g_column(g_first, k).astype(BF16)
        one_ref[(k + 2) * size : (k + 3) * size, :] = both
        two_ref[(k + 2) * size : (k + 3) * size, :] = both


def choose(even, one, two):
    return jnp.where(even, one.astype(F32), two.astype(F32)).astype(BF16)


def rows_kernel(
    rows, cols, place_ref, x_lines, g_lines, got_one, got_two,
    left_ref, right_ref, one_ref, two_ref, own_ref, x_wide, g_wide,
):
    cin = x_lines.shape[2]
    depth = g_lines.shape[2]
    even_col = place_ref[0] == 0
    even_row = place_ref[1] == 0
    size = 2 * rows
    left_ref[...] = choose(even_col, got_two[0 : 2 * size, :], got_one[0 : 2 * size, :])
    right_ref[...] = choose(even_col, got_one[...], got_two[...])

    def cell(ref, index):
        first = index // 16 * 16
        return ref[first : first + 16, :].astype(F32)[index - first : index - first + 1, :]

    def x_line(cells, r):
        x_wide[...] = jnp.zeros((2 * cols + 32, cin), F32)
        x_wide[16 : 16 + 2 * cols, :] = cells.astype(F32)
        x_wide[15:16, :] = cell(left_ref, r)
        x_wide[16 + 2 * cols : 17 + 2 * cols, :] = cell(right_ref, r)
        x_wide[17 + 2 * cols : 18 + 2 * cols, :] = cell(right_ref, size + r)
        return x_wide[...]

    def g_line(cells, p):
        halves = []
        for half in range(depth // 128):
            g_wide[...] = jnp.zeros((cols + 16, 128), F32)
            g_wide[8 : 8 + cols, :] = cells[:, half * 128 : (half + 1) * 128].astype(F32)
            g_wide[7:8, :] = cell(left_ref, size + half * rows + p)
            g_wide[8 + cols : 9 + cols, :] = cell(right_ref, 2 * size + half * rows + p)
            g_wide[9 + cols : 10 + cols, :] = cell(right_ref, 3 * size + half * rows + p)
            halves.append(g_wide[...])
        return jnp.concatenate(halves, 0)

    line = 2 * cols + 32
    down = (x_line(x_lines[0], 2 * rows - 1), g_line(g_lines[0], rows - 1))
    up = (x_line(x_lines[1], 0), x_line(x_lines[2], 1))
    for k in range(2):
        part = slice(k * line, (k + 1) * line)
        own_ref[part, :] = down[k].astype(BF16)
        one_ref[part, :] = jnp.where(even_row, down[k], up[k]).astype(BF16)
        two_ref[part, :] = jnp.where(even_row, up[k], down[k]).astype(BF16)
        both = g_line(g_lines[1 + k], k).astype(BF16)
        one_ref[(k + 2) * line : (k + 3) * line, :] = both
        two_ref[(k + 2) * line : (k + 3) * line, :] = both


def planes_kernel(rows, cols, x_ref, planes_ref, wide, held, sems):
    cin = x_ref.shape[2]
    planes_ref[0:cols, :] = jnp.zeros((cols, 6 * cin), BF16)
    step = CHUNK // cols
    copies = [
        pltpu.make_async_copy(x_ref.at[2 * step * i : 2 * step * (i + 1)], held.at[i], sems.at[i])
        for i in range(rows // step)
    ]
    for copy in copies:
        copy.start()
    wide[:, 0:8, :] = jnp.zeros((2 * step, 8, cin), F32)

    def deinterleave(i):
        copies[i].wait()
        wide[:, 8 : 8 + 2 * cols, :] = held[i].astype(F32)
        row = (i * step + 1) * cols
        for parity in range(2):
            for slot, first in enumerate((7, 8, 9)):
                part = wide[pl.ds(parity, step, stride=2), pl.ds(first, cols, stride=2), :]
                lane = (parity * 3 + slot) * cin
                planes_ref[row : row + CHUNK, lane : lane + cin] = part.reshape(CHUNK, cin).astype(BF16)

    for i in range(rows // step):
        deinterleave(i)


def stride_kernel(rows, cols, planes_ref, w_ref, z_ref):
    cin = planes_ref.shape[1] // 6

    def convolve(i, carry):
        row = pl.multiple_of(i * LONG, LONG)
        above = planes_ref[pl.ds(row, LONG), 3 * cin :]
        here = planes_ref[pl.ds(pl.multiple_of(row + cols, cols), LONG), :]
        z_ref[pl.ds(row, LONG), :] = dot(jnp.concatenate([above, here], 1), w_ref[...])
        return carry

    lax.fori_loop(0, rows * cols // LONG, convolve, 0)


def edge_parts(rows, cols, xcol_ref, xrow_ref, col_pad, row_pad):
    col_pad[0:8, :] = xrow_ref[0:16, :].astype(F32)[8:16, :]
    col_pad[8 : 8 + 2 * rows, :] = xcol_ref[0 : 2 * rows, :].astype(F32)
    row_pad[0:8, :] = jnp.zeros((8, xrow_ref.shape[1]), F32)
    row_pad[8 : 8 + 2 * cols, :] = xrow_ref[16 : 16 + 2 * cols, :].astype(F32)
    left = [col_pad[pl.ds(first, rows, stride=2), :] for first in (7, 8, 9)]
    over = [row_pad[pl.ds(first, cols, stride=2), :] for first in (7, 8, 9)]
    return left, over


def edges_kernel(
    rows, cols, place_ref, z_in, xcol_ref, right_ref, own_col_ref, own_row_ref, got_one, got_two, w_ref,
    z_ref, stats_ref, xrow_ref, below_ref, z_rim_ref, col_pad, row_pad, rim, bottom, side,
):
    cin = xcol_ref.shape[1]
    even_row = place_ref[1] == 0
    line = 2 * cols + 32
    xrow_ref[...] = choose(even_row, got_two[0 : 2 * line, :], got_one[0 : 2 * line, :])
    below_ref[...] = choose(even_row, got_one[...], got_two[...])
    left, over = edge_parts(rows, cols, xcol_ref, xrow_ref, col_pad, row_pad)
    z_ref[...] = z_in[...]
    from_above = dot(jnp.concatenate(over, 1).astype(BF16), w_ref[0 : 3 * cin])
    from_left = (
        dot(left[0].astype(BF16), w_ref[0:cin])
        + dot(left[1].astype(BF16), w_ref[3 * cin : 4 * cin])
        + dot(left[2].astype(BF16), w_ref[6 * cin : 7 * cin])
    )
    z_ref[0:cols, :] = z_ref[0:cols, :] + from_above
    rim[...] = from_left
    for p in range(rows):
        z_ref[p * cols : p * cols + 1, :] = z_ref[p * cols : p * cols + 1, :] + rim[p : p + 1, :]
    z = z_ref[...]
    stats_ref[0:1, :] = jnp.sum(z, axis=0, keepdims=True)
    stats_ref[1:2, :] = jnp.sum(z * z, axis=0, keepdims=True)
    bottom[0] = own_row_ref[0:line, :].astype(F32)
    bottom[1] = below_ref[0:line, :].astype(F32)
    bottom[2] = below_ref[line : 2 * line, :].astype(F32)
    over_end = xrow_ref[2 * cols : 2 * cols + 32, :].astype(F32)
    for b, ref in enumerate((own_col_ref, right_ref, right_ref)):
        first = 2 * rows if b == 2 else 0
        side[b, 8:, :] = ref[first : first + 2 * rows, :].astype(F32)
        side[b, 7:8, :] = over_end[15 + b : 16 + b, :]
    parts = []
    for a in range(3):
        for b in range(3):
            low = bottom[a, pl.ds(15 + b, cols + 8, stride=2), :]
            beside = side[b, pl.ds(7 + a, rows, stride=2), :]
            parts.append(jnp.concatenate([low, beside], 0).astype(BF16))
    z_rim_ref[...] = dot(jnp.concatenate(parts, 1), w_ref[...])


def windows_kernel(rows, cols, planes_ref, xcol_ref, xrow_ref, t_ref, col_pad, row_pad, wide):
    cin = xrow_ref.shape[1]
    cells = rows * cols
    left, over = edge_parts(rows, cols, xcol_ref, xrow_ref, col_pad, row_pad)
    for half, parts in ((0, left[1]), (3, left[2])):
        wide[...] = planes_ref[cols:, half * cin : (half + 1) * cin].astype(F32)
        wide[pl.ds(0, rows, stride=cols), :] = parts
        window = wide[...].astype(BF16)
        t_ref[(half + 3) * cin : (half + 4) * cin, :] = window.T
    wide[cols:, :] = planes_ref[cols:cells, 3 * cin : 4 * cin].astype(F32)
    wide[0:cols, :] = over[0]
    wide[pl.ds(0, rows, stride=cols), :] = left[0]
    t_ref[0:cin, :] = wide[...].astype(BF16).T
    for slot in (1, 2):
        lane = (3 + slot) * cin
        below = planes_ref[cols:cells, lane : lane + cin]
        window = jnp.concatenate([over[slot].astype(BF16), below], 0)
        t_ref[slot * cin : (slot + 1) * cin, :] = window.T
    for slot in (1, 2, 4, 5):
        lane = slot * cin
        t_ref[lane + 3 * cin : lane + 4 * cin, :] = planes_ref[cols:, lane : lane + cin].T


def prepare_kernel(rows, cols, g_hbm, left_ref, right_ref, w_ref, body_ref, w_t_ref, done_ref, wide, rims, g_ref, sem):
    pitch = cols + 16
    depth = w_ref.shape[1]
    size = 2 * rows
    copy = pltpu.make_async_copy(g_hbm, g_ref, sem)
    copy.start()
    for tap in range(9):
        w_t_ref[tap * depth : (tap + 1) * depth, :] = w_ref[tap * depth : (tap + 1) * depth, :].T
    done_ref[...] = jnp.zeros(done_ref.shape, F32)
    for half in range(depth // 128):
        lanes = slice(half * 128, (half + 1) * 128)
        rims[0, :, lanes] = left_ref[size + half * rows : size + (half + 1) * rows, :].astype(F32)
        rims[1, :, lanes] = right_ref[2 * size + half * rows : 2 * size + (half + 1) * rows, :].astype(F32)
    copy.wait()
    for p in range(rows):
        first = p * pitch
        wide[first + 8 : first + 8 + cols, :] = g_ref[p].astype(F32)
        wide[first + 7 : first + 8, :] = rims[0, p : p + 1, :]
        wide[first + 8 + cols : first + 9 + cols, :] = rims[1, p : p + 1, :]
        for b in (0, 2):
            body_ref[b, p * cols : (p + 1) * cols, :] = wide[first + 9 - b : first + 9 - b + cols, :].astype(BF16)
    body_ref[1] = g_ref[...].reshape(body_ref.shape[1:])


def window(cols, body_ref, edge_ref, b, first, size):
    cells = body_ref.shape[1]
    parts = []
    if first < cols:
        parts.append(edge_ref[b, first:cols, :])
    start, stop = max(first, cols) - cols, min(first + size, cells + cols) - cols
    parts.append(body_ref[b, start:stop, :])
    if first + size > cells + cols:
        parts.append(edge_ref[b, cols : first + size - cells, :])
    return parts[0] if len(parts) == 1 else jnp.concatenate(parts, 0)


def upstream_kernel(
    rows, cols, body_ref, w_t_ref, right_ref, own_col_ref, own_row_ref, above_ref, below_ref,
    edge_ref, act_grad_ref, rim_ref, wide, bottom, side,
):
    pitch = cols + 16
    depth = act_grad_ref.shape[1]
    size = 2 * rows
    line = 2 * cols + 32
    for half in range(depth // 128):
        lanes = slice(half * 128, (half + 1) * 128)
        side[0, 8 : 8 + rows, lanes] = right_ref[3 * size + half * rows : 3 * size + (half + 1) * rows, :].astype(F32)
        side[1, 8 : 8 + rows, lanes] = right_ref[2 * size + half * rows : 2 * size + (half + 1) * rows, :].astype(F32)
        side[2, 8 : 8 + rows, lanes] = own_col_ref[size + half * rows : size + (half + 1) * rows, :].astype(F32)
        over = above_ref[line + half * pitch : line + (half + 1) * pitch, :].astype(F32)
        under = below_ref[2 * line + half * pitch : 2 * line + (half + 1) * pitch, :].astype(F32)
        wide[0:pitch, lanes] = over
        wide[pitch : 2 * pitch, lanes] = under
        for b in range(3):
            side[b, 7:8, lanes] = over[9 + cols - b : 10 + cols - b, :]
            side[b, 8 + rows : 9 + rows, lanes] = under[9 + cols - b : 10 + cols - b, :]
        bottom[0, 0:pitch, lanes] = below_ref[3 * line + half * pitch : 3 * line + (half + 1) * pitch, :].astype(F32)
        bottom[1, 0:pitch, lanes] = under
        bottom[2, 0:pitch, lanes] = own_row_ref[line + half * pitch : line + (half + 1) * pitch, :].astype(F32)
    bottom[:, pitch:, :] = jnp.zeros((3, 8, depth), F32)
    for b in range(3):
        edge_ref[b, 0:cols, :] = wide[9 - b : 9 - b + cols, :].astype(BF16)
        edge_ref[b, cols:, :] = wide[pitch + 9 - b : pitch + 9 - b + cols, :].astype(BF16)
    for row in range(0, rows * cols, LONG):
        parts = []
        for a in range(3):
            for b in range(3):
                parts.append(window(cols, body_ref, edge_ref, b, row + (2 - a) * cols, LONG))
        act_grad_ref[row : row + LONG, :] = dot(jnp.concatenate(parts, 1), w_t_ref[...])
    parts = []
    for a in range(3):
        for b in range(3):
            low = bottom[a, 9 - b : 17 - b + cols, :]
            beside = side[b, 9 - a : 9 - a + rows, :]
            parts.append(jnp.concatenate([low, beside], 0).astype(BF16))
    rim_ref[...] = dot(jnp.concatenate(parts, 1), w_t_ref[...])


def group_sum(value, depth):
    size = depth // GROUPS
    one = lax.broadcasted_iota(jnp.int32, (depth, depth), 0) // size
    two = lax.broadcasted_iota(jnp.int32, (depth, depth), 1) // size
    same = jnp.where(one == two, 1.0, 0.0).astype(F32)
    return lax.dot_general(
        value, same, (((1,), (0,)), ((), ())), precision=lax.Precision.HIGHEST, preferred_element_type=F32
    )


def add_kernel(*refs):
    refs[-1][...] = tree_sum([r[...] for r in refs[:-1]])


def stack_kernel(*refs):
    for k, ref in enumerate(refs[:-1]):
        refs[-1][k] = ref[...]


def activate_kernel(norm_count, own_ref, pair_ref, z_ref, act_grad_ref, gain_ref, bias_ref, act_ref, pre_ref, sums_ref, moments_ref):
    cells, depth = z_ref.shape
    total = group_sum(own_ref[...] + pair_ref[...], depth) / norm_count
    mean = total[0:1, :]
    inv_std = 1.0 / jnp.sqrt(total[1:2, :] - mean * mean + 1e-05)
    moments_ref[0:1, :] = mean
    moments_ref[1:2, :] = inv_std
    gain = gain_ref[...]
    bias = bias_ref[...]

    def chunk(i, carry):
        row = pl.multiple_of(i * 64, 64)
        normed = (z_ref[pl.ds(row, 64), :] - mean) * inv_std
        shifted = normed * gain + bias
        sig = 1.0 / (1.0 + jnp.exp(-shifted))
        act_ref[pl.ds(row, 64), :] = (shifted * sig).astype(BF16)
        pre = act_grad_ref[pl.ds(row, 64), :] * sig * (1.0 + shifted * (1.0 - sig))
        pre_ref[pl.ds(row, 64), :] = pre
        one = jnp.sum(pre.reshape(8, 8, depth), axis=0)
        two = jnp.sum((pre * normed).reshape(8, 8, depth), axis=0)
        return carry[0] + one, carry[1] + two

    zero = jnp.zeros((8, depth), F32)
    one, two = lax.fori_loop(0, cells // 64, chunk, (zero, zero))
    sums_ref[0:1, :] = jnp.sum(one, axis=0, keepdims=True)
    sums_ref[1:2, :] = jnp.sum(two, axis=0, keepdims=True)


def second_kernel(rows, cols, place_ref, act_ref, body_ref, edge_ref, keep_ref, send_ref):
    cells = rows * cols
    depth = act_ref.shape[1]
    act_t = act_ref[...].T
    half, size = depth // 2, depth // 8
    even = place_ref[4] == 0
    spot = place_ref[5] & 3
    for a in range(3):
        for b in range(3):
            first = (2 - a) * cols
            tap = a * 3 + b
            both = dot(act_t, window(cols, body_ref, edge_ref, b, first, cells))
            mine = jnp.where(even, both[0:half, :], both[half:, :])
            theirs = jnp.where(even, both[half:, :], both[0:half, :]).astype(BF16)
            for j in range(4):
                keep_ref[j ^ spot, tap * size : (tap + 1) * size, :] = mine[j * size : (j + 1) * size, :]
                send_ref[j ^ spot, tap * size : (tap + 1) * size, :] = theirs[j * size : (j + 1) * size, :]


def conv_grad_kernel(norm_count, rows, cols, place_ref, own_ref, pair_ref, *refs):
    z_ref, pre_ref, moments_ref, gain_ref, bias_ref, z_rim_ref, act_rim_ref, t_ref = refs[:8]
    grad_ref, rim_ref, total_ref, keep_ref, send_ref = refs[8:]
    cells, depth = z_ref.shape
    total = own_ref[...] + pair_ref[...]
    total_ref[...] = total
    gain = gain_ref[...]
    means = group_sum(total * gain, depth) / norm_count
    mean = moments_ref[0:1, :]
    inv_std = moments_ref[1:2, :]
    shift = means[0:1, :]
    scale = means[1:2, :]

    def value(z, pre):
        return ((gain * pre - shift - (z - mean) * inv_std * scale) * inv_std).astype(BF16)

    def chunk(i, carry):
        row = pl.multiple_of(i * 64, 64)
        grad_ref[pl.ds(row, 64), :] = value(z_ref[pl.ds(row, 64), :], pre_ref[pl.ds(row, 64), :])
        return carry

    lax.fori_loop(0, cells // 64, chunk, 0)
    z = z_rim_ref[...]
    shifted = (z - mean) * inv_std * gain + bias_ref[...]
    sig = 1.0 / (1.0 + jnp.exp(-shifted))
    pre = act_rim_ref[...] * sig * (1.0 + shifted * (1.0 - sig))
    cell = lax.broadcasted_iota(jnp.int32, z.shape, 0)
    to_right = jnp.where(cell >= cols, place_ref[2], 1)
    to_below = jnp.where(cell < cols + 8, place_ref[3], 1)
    rim_ref[...] = jnp.where(to_right * to_below == 1, value(z, pre).astype(F32), 0.0)

    half = t_ref.shape[0] // 2
    size = half // 4
    core = place_ref[4]
    spot = place_ref[5] & 3
    theirs = dot(t_ref[pl.ds(pl.multiple_of((1 - core) * half, 16), half), :], grad_ref[...]).astype(BF16)
    mine = dot(t_ref[pl.ds(pl.multiple_of(core * half, 16), half), :], grad_ref[...])
    for j in range(4):
        send_ref[j ^ spot] = theirs[j * size : (j + 1) * size, :]
        keep_ref[j ^ spot] = mine[j * size : (j + 1) * size, :]


def input_kernel(rows, cols, d_ref, rim_ref, w_ref, out_ref, done_ref, plain, shifted, w_t, wide, mixed):
    cells = rows * cols
    cin = out_ref.shape[2]
    depth = d_ref.shape[1]
    pitch = cols + 8
    plain[0:cells, :] = d_ref[...]
    plain[cells:, :] = rim_ref[0:cols, :].astype(BF16)
    for p in range(rows + 1):
        first = p * pitch
        wide[first : first + cols, :] = plain[p * cols : (p + 1) * cols, :].astype(F32)
        next_cell = cols + 8 + p if p < rows else cols
        wide[first + cols : first + cols + 1, :] = rim_ref[next_cell : next_cell + 1, :]
        shifted[p * cols : (p + 1) * cols, :] = wide[first + 1 : first + 1 + cols, :].astype(BF16)
    for place, tap in enumerate((4, 5, 7, 8, 3, 6, 1, 2, 0)):
        w_t[:, place * cin : (place + 1) * cin] = w_ref[tap * cin : (tap + 1) * cin, :].T
    done_ref[...] = jnp.zeros(done_ref.shape, F32)
    step = CHUNK // cols

    def chunk(i, carry):
        row = pl.multiple_of(i * CHUNK, CHUNK)
        under = pl.multiple_of(row + cols, cols)
        own = dot(plain[pl.ds(row, CHUNK), :], w_t[:, 0 : 4 * cin])
        right = dot(shifted[pl.ds(row, CHUNK), :], w_t[:, 4 * cin : 6 * cin])
        below = dot(plain[pl.ds(under, CHUNK), :], w_t[:, 6 * cin : 8 * cin])
        corner = dot(shifted[pl.ds(under, CHUNK), :], w_t[:, 8 * cin :])
        even_even = own[:, 0:cin]
        even_odd = own[:, cin : 2 * cin] + right[:, 0:cin]
        odd_even = own[:, 2 * cin : 3 * cin] + below[:, 0:cin]
        odd_odd = own[:, 3 * cin :] + right[:, cin:] + below[:, cin:] + corner
        for parity, pair in enumerate(((even_even, even_odd), (odd_even, odd_odd))):
            for side in range(2):
                mixed[pl.ds(parity, step, stride=2), pl.ds(side, cols, stride=2), :] = pair[side].reshape(
                    step, cols, cin
                )
        out_ref[pl.ds(pl.multiple_of(i * 2 * step, 2 * step), 2 * step)] = mixed[...].astype(BF16)
        return carry

    lax.fori_loop(0, rows // step, chunk, 0)


def first_split_kernel(place_ref, mine_ref, other_ref, keep_ref, send_ref):
    even = place_ref[4] == 0
    none, along_y, along_x, both = [mine_ref[k] + other_ref[k].astype(F32) for k in range(4)]
    keep_ref[0] = none
    keep_ref[1] = jnp.where(even, along_y, along_x)
    send_ref[0] = jnp.where(even, along_x, along_y).astype(BF16)
    send_ref[1] = both.astype(BF16)


def second_split_kernel(mine_ref, other_ref, keep_ref, send_ref):
    keep_ref[...] = mine_ref[0] + other_ref[0].astype(F32)
    send_ref[...] = (mine_ref[1] + other_ref[1].astype(F32)).astype(BF16)


def half_kernel(slots_ref, other_ref, *refs):
    own_ref, one_ref, two_ref, three_ref = refs[-4:]
    rows = slots_ref.shape[1]
    own_ref[...] = slots_ref[0] + other_ref[0]
    for k, ref in enumerate((one_ref, two_ref, three_ref)):
        ref[0:rows, :] = (slots_ref[k + 1] + other_ref[k + 1]).astype(BF16)
    if len(refs) > 4:
        two_ref[rows:, :] = three_parts(refs[0][...])


def three_parts(pair):
    high = pair.astype(BF16).astype(F32)
    rest = pair - high
    middle = rest.astype(BF16).astype(F32)
    low = rest - middle
    zeros = jnp.zeros((10, pair.shape[1]), F32)
    return jnp.concatenate([high, middle, low, zeros], 0).astype(BF16)


def from_parts(parts):
    parts = parts.astype(F32)
    return parts[0:2, :] + parts[2:4, :] + parts[4:6, :]


def total_kernel(*refs):
    rows = refs[-1].shape[0]
    refs[-1][...] = tree_sum([r[0:rows, :].astype(F32) for r in refs[:-1]]).astype(BF16)


def both_kernel(count, *refs):
    second, first, out_ref = refs[:count], refs[count:-1], refs[-1]
    rows = second[0].shape[0]
    out_ref[0:rows, :] = tree_sum([r[...].astype(F32) for r in second]).astype(BF16)
    out_ref[rows:, :] = tree_sum([r[...].astype(F32) for r in first]).astype(BF16)


def first_total_kernel(own_ref, one_ref, two_ref, three_ref, pair_ref, out_ref, bias_ref, gain_ref):
    total_kernel(own_ref, one_ref, two_ref, three_ref, out_ref)
    rows = out_ref.shape[0]
    both = from_parts(three_parts(pair_ref[...])) + from_parts(two_ref[rows:, :])
    bias_ref[...] = both[0:1, :]
    gain_ref[...] = both[1:2, :]


def gather_kernel(slots, rows, place_ref, *refs):
    me = place_ref[5]
    count = len(slots)
    shards = refs[: 2 * count]
    second_ref, first_ref, second_stage, first_stage, sems = refs[-5:]
    copies = []
    for i, slot in enumerate(slots):
        for k, where in ((i, me ^ slot), (i + count, me ^ slot ^ 4)):
            second_stage[k] = shards[k][0:rows, :].astype(F32).reshape(second_stage.shape[1:])
            first_stage[k] = shards[k][rows:, :].astype(F32)
            copies.append(pltpu.make_async_copy(second_stage.at[k], second_ref.at[:, where], sems.at[2 * k]))
            copies.append(pltpu.make_async_copy(first_stage.at[k], first_ref.at[where], sems.at[2 * k + 1]))
            copies[-2].start()
            copies[-1].start()
    for copy in copies:
        copy.wait()


def on_device(dp_size, tiles, images, first_weight, norm_gain, norm_bias, second_weight, upstream):
    rows, cols, depth = upstream.shape[2:]
    cin = images.shape[4]
    cells = rows * cols
    group_size = depth // GROUPS
    norm_count = float(cells * tiles * group_size)
    tile_rows = tiles // TCOLS
    axes = ("dp", "space")
    devices = dp_size * tiles

    def flip(value, mask):
        return lax.ppermute(value, axes, [(i, i ^ mask) for i in range(devices)])

    def swapped(value, down, right):
        pairs = []
        for t in range(tiles):
            spot = (t + TCOLS + 2) % tiles
            r, c = spot // TCOLS, spot % TCOLS
            r = r if not down else ((r + down - 1) ^ 1) - down + 1
            c = c if not right else ((c + right - 1) ^ 1) - right + 1
            if 0 <= r < tile_rows and 0 <= c < TCOLS:
                pairs.append((t, (r * TCOLS + c - TCOLS - 2) % tiles))
        return lax.ppermute(value, "space", pairs)

    def added(parts, after=()):
        return call(add_kernel, [shape(parts[0].shape, F32)], parts, after=after)[0]

    def fetched(value, after=()):
        parts = [value] + [flip(value, 2 * k) for k in (1, 2, 3)]
        for k in range(3, tiles.bit_length() - 1):
            total = added(parts, after)
            parts, after = [total, flip(total, 1 << k)], ()
        return parts

    def crossed(value, even, odd):
        return lax.ppermute(value, axes, [(i, i ^ (odd if i % 2 else even)) for i in range(devices)])

    def along(value, size, step):
        return [value] + [flip(value, step * k) for k in range(1, size)]

    def total(parts, after=()):
        if len(parts) == 1:
            return parts[0]
        return call(total_kernel, [shape(parts[0].shape, BF16)], parts, after=after)[0]

    def halved(slots, more=(), after=()):
        part = slots[0].shape[1:]
        longer = (part[0] + 16 * len(more), part[1])
        outs = [shape(part, F32), shape(part, BF16), shape(longer, BF16), shape(part, BF16)]
        return call(half_kernel, outs, [slots[0], flip(slots[1], 1), *more], after=after)

    masks = [0, 2, tiles, tiles + 2]

    def quartered(parts):
        return [parts[0]] + [flip(parts[k], masks[k]) for k in (1, 2, 3)]

    def quarters(shard):
        return [shard] + [flip(shard, masks[k]) for k in (1, 2, 3)]

    space = lax.axis_index("space")
    spot = (space + TCOLS + 2) % tiles
    column, row = spot % TCOLS, spot // TCOLS
    me = (space % 2) * 4 + (lax.axis_index("dp") % 2) * 2 + (space // 2) % 2
    place = jnp.stack([column % 2, row % 2, column < TCOLS - 1, row < tile_rows - 1, space % 2, me]).astype(jnp.int32)
    x = pltpu.with_memory_space_constraint(images[0, 0], pltpu.HBM)
    g3 = pltpu.with_memory_space_constraint(upstream[0, 0], pltpu.HBM)
    w1 = first_weight.reshape(9 * cin, depth)
    w2 = second_weight.reshape(9 * depth, depth)
    gain = norm_gain.reshape(1, depth)
    bias = norm_bias.reshape(1, depth)

    hbm = pl.BlockSpec(memory_space=pltpu.HBM)
    smem = pl.BlockSpec(memory_space=pltpu.SMEM)
    vmem = pl.BlockSpec(memory_space=pltpu.VMEM)
    ends = shape((4 * 2 * rows, cin), BF16)
    half_ends = shape((2 * 2 * rows, cin), BF16)
    one, two, own_column, x_lines, g_lines = call(
        functools.partial(pack_kernel, rows, cols),
        [ends, ends, half_ends, shape((3, 2 * cols, cin), BF16), shape((3, cols, depth), BF16)],
        [place, x, g3],
        [pltpu.VMEM((2 * rows, 16, cin), BF16)] * 2
        + [pltpu.VMEM((rows, 16, depth), BF16)] * 2
        + [pltpu.VMEM((2 * rows * 16, cin), F32), pltpu.VMEM((rows * 16, 128), F32), pltpu.SemaphoreType.DMA((8,))],
        specs=[smem, hbm, hbm],
    )
    one = swapped(one, 0, 1)
    two = swapped(two, 0, 2)
    (planes,) = call(
        functools.partial(planes_kernel, rows, cols),
        [shape((cells + cols, 6 * cin), BF16)],
        [x],
        [
            pltpu.VMEM((2 * CHUNK // cols, 2 * cols + 8, cin), F32),
            pltpu.VMEM((cells // CHUNK, 2 * CHUNK // cols, 2 * cols, cin), BF16),
            pltpu.SemaphoreType.DMA((cells // CHUNK,)),
        ],
        specs=[hbm],
        flops=cells * 9 * cin * depth,
    )
    lines = shape((4 * (2 * cols + 32), cin), BF16)
    half_lines = shape((2 * (2 * cols + 32), cin), BF16)
    from_left, from_right, one, two, own_row = call(
        functools.partial(rows_kernel, rows, cols),
        [half_ends, ends, lines, lines, half_lines],
        [place, x_lines, g_lines, one, two],
        [pltpu.VMEM((2 * cols + 32, cin), F32), pltpu.VMEM((cols + 16, 128), F32)],
        smem=1,
        after=[planes],
    )
    got_one = swapped(one, 1, 0)
    got_two = swapped(two, 2, 0)
    (z,) = call(
        functools.partial(stride_kernel, rows, cols),
        [shape((cells, depth), F32)],
        [planes, w1],
        flops=2 * cells * 9 * cin * depth,
        after=[one],
    )
    pads = [pltpu.VMEM((2 * rows + 8, cin), F32), pltpu.VMEM((2 * cols + 8, cin), F32)]
    body, w_t, prepared = call(
        functools.partial(prepare_kernel, rows, cols),
        [shape((3, cells, depth), BF16), shape((9 * depth, depth), BF16), shape((8, 128), F32)],
        [g3, from_left, from_right, w2],
        [
            pltpu.VMEM((rows * (cols + 16), depth), F32),
            pltpu.VMEM((2, rows, depth), F32),
            pltpu.VMEM((rows, cols, depth), BF16),
            pltpu.SemaphoreType.DMA,
        ],
        specs=[hbm, vmem, vmem, vmem],
        after=[one],
    )
    rim = rows + cols + 8
    z, stats, from_above, from_below, z_rim = call(
        functools.partial(edges_kernel, rows, cols),
        [shape((cells, depth), F32), shape((2, depth), F32), half_lines, lines, shape((rim, depth), F32)],
        [place, z, from_left, from_right, own_column, own_row, got_one, got_two, w1],
        pads
        + [
            pltpu.VMEM((rows, depth), F32),
            pltpu.VMEM((3, 2 * cols + 32, cin), F32),
            pltpu.VMEM((3, 2 * rows + 8, cin), F32),
        ],
        smem=1,
        after=[prepared],
        flops=2 * 80 * 3 * cin * depth,
    )
    stats = fetched(added([stats, flip(stats, 1)]))
    edge, act_grad, act_rim = call(
        functools.partial(upstream_kernel, rows, cols),
        [shape((3, 2 * cols, depth), BF16), shape((cells, depth), F32), shape((rim, depth), F32)],
        [body, w_t, from_right, own_column, own_row, from_above, from_below],
        [
            pltpu.VMEM((2 * (cols + 16), depth), F32),
            pltpu.VMEM((3, cols + 24, depth), F32),
            pltpu.VMEM((3, rows + 16, depth), F32),
        ],
        flops=2 * cells * 9 * depth * depth,
    )
    activated, pre_grad, sums, moments = call(
        functools.partial(activate_kernel, norm_count),
        [shape((cells, depth), BF16), shape((cells, depth), F32), shape((2, depth), F32), shape((2, depth), F32)],
        stats + [z, act_grad, gain, bias],
        flops=cells * depth * 30,
    )
    other = flip(sums, 1)
    second_slots = call(
        functools.partial(second_kernel, rows, cols),
        [shape((4, 9 * depth // 8, depth), F32), shape((4, 9 * depth // 8, depth), BF16)],
        [place, activated, body, edge],
        flops=2 * cells * 9 * depth * depth,
        smem=1,
    )
    near = added([sums, other], second_slots[1:])
    part = second_slots[0].shape[1:]
    kept, sent = call(
        first_split_kernel,
        [shape((2,) + part, F32), shape((2,) + part, BF16)],
        [place, second_slots[0], flip(second_slots[1], 1)],
        smem=1,
        after=[near],
    )
    parts = fetched(near, [kept])
    second_parts = call(
        second_split_kernel,
        [shape(part, F32), shape(part, BF16)],
        [kept, crossed(sent, tiles, 2)],
        after=parts[:1],
    )
    (windows,) = call(
        functools.partial(windows_kernel, rows, cols),
        [shape((9 * cin, cells), BF16)],
        [planes, from_left, from_above],
        pads + [pltpu.VMEM((cells, cin), F32)],
        flops=2 * cells * 9 * cin * depth,
        after=second_parts[:1],
    )
    second_shard = total([second_parts[0], crossed(second_parts[1], 2, tiles)])
    pair = along(total(along(second_shard, dp_size // 2, 2 * tiles)), tiles // 4, 4)
    conv_grad, grad_rim, sum_pair, *first_slots = call(
        functools.partial(conv_grad_kernel, norm_count, rows, cols),
        [
            shape((cells, depth), BF16),
            shape((rim, depth), F32),
            shape((2, depth), F32),
            shape((4, 9 * cin // 8, depth), F32),
            shape((4, 9 * cin // 8, depth), BF16),
        ],
        [place] + parts + [z, pre_grad, moments, gain, bias, z_rim, act_rim, windows],
        flops=2 * cells * 9 * cin * depth,
        smem=1,
        after=[second_shard],
    )
    first_parts = quartered(halved(first_slots, [sum_pair]))
    first_shard, bias_grad, gain_grad = call(
        first_total_kernel,
        [shape(first_slots[0].shape[1:], BF16), shape((1, depth), F32), shape((1, depth), F32)],
        first_parts + [sum_pair],
    )
    first_shard = along(total(along(first_shard, dp_size // 2, 2 * tiles)), tiles // 4, 4)
    input_grad, done = call(
        functools.partial(input_kernel, rows, cols),
        [shape((2 * rows, 2 * cols, cin), BF16), shape((8, 128), F32)],
        [conv_grad, grad_rim, w1],
        [
            pltpu.VMEM((cells + cols, depth), BF16),
            pltpu.VMEM((cells + cols, depth), BF16),
            pltpu.VMEM((depth, 9 * cin), BF16),
            pltpu.VMEM(((rows + 1) * (cols + 8), depth), F32),
            pltpu.VMEM((2 * CHUNK // cols, 2 * cols, cin), F32),
        ],
        flops=2 * cells * 9 * cin * depth,
    )
    sizes = second_slots[0].shape[1], first_slots[0].shape[1]
    (shard,) = call(
        functools.partial(both_kernel, len(pair)),
        [shape((sum(sizes), depth), BF16)],
        pair + first_shard,
        after=[done],
    )
    for k in range(1, dp_size.bit_length() - 1):
        bias_grad = bias_grad + flip(bias_grad, tiles << k)
        gain_grad = gain_grad + flip(gain_grad, tiles << k)
    own = quarters(shard)
    grads = [shape((9, 8, depth // 8, depth), F32), shape((8, sizes[1], depth), F32)]
    for slots in ((0,), (1, 2, 3)):
        here = [own[slot] for slot in slots]
        shards = here + [flip(value, 1) for value in here]
        left = list(grads) if len(slots) > 1 else []
        grads = call(
            functools.partial(gather_kernel, slots, sizes[0]),
            [shape(g.shape, F32) for g in grads],
            [place] + shards + left,
            [
                pltpu.VMEM((len(shards), 9, depth // 8, depth), F32),
                pltpu.VMEM((len(shards), sizes[1], depth), F32),
                pltpu.SemaphoreType.DMA((2 * len(shards),)),
            ],
            specs=[smem] + [vmem] * len(shards) + [hbm] * len(left),
            out_specs=[hbm] * 2,
            aliases={1 + len(shards) + k: k for k in range(len(left))},
        )
    second_grad, first_grad = grads
    return (
        input_grad[None, None],
        first_grad.reshape(first_weight.shape),
        second_grad.reshape(second_weight.shape),
        gain_grad.reshape(depth),
        bias_grad.reshape(depth),
    )


def solution(mesh):
    placed = (
        P("dp", "space", None, None, None),
        P(),
        P(),
        P(),
        P(),
        P("dp", "space", None, None, None),
    )
    return jax.shard_map(
        functools.partial(on_device, mesh.shape["dp"], mesh.shape["space"]),
        mesh=mesh,
        in_specs=placed,
        out_specs=(P("dp", "space", None, None, None), P(), P(), P(), P()),
        check_vma=False,
    )
```

```python
import functools

import jax
import jax.numpy as jnp
from jax import lax
from jax.experimental import pallas as pl
from jax.experimental.pallas import tpu as pltpu
from jax.sharding import PartitionSpec as P

GROUPS = 32
TCOLS = 4
F32 = jnp.float32
BF16 = jnp.bfloat16
MIB = 1024 * 1024
CHUNK = 256
LONG = 512


def call(kernel, outs, args, scratch=(), flops=0, limit=20, smem=0, after=(), specs=None, grid=(), out_specs=None, aliases=None):
    if specs is None:
        specs = [pl.BlockSpec(memory_space=pltpu.SMEM)] * smem
        specs += [pl.BlockSpec(memory_space=pltpu.VMEM)] * (len(args) - smem)
    moved = sum(a.size * a.dtype.itemsize for a in list(args) + list(outs))
    count = len(args)

    def body(*refs):
        kernel(*refs[:count], *refs[count + len(after) :])

    return pl.pallas_call(
        body,
        out_shape=list(outs),
        grid=grid,
        in_specs=list(specs) + [pl.BlockSpec(memory_space=pl.ANY)] * len(after),
        out_specs=out_specs or [pl.BlockSpec(memory_space=pltpu.VMEM)] * len(outs),
        scratch_shapes=list(scratch),
        input_output_aliases=aliases or {},
        compiler_params=pltpu.CompilerParams(vmem_limit_bytes=limit * MIB),
        cost_estimate=pl.CostEstimate(flops=flops, bytes_accessed=moved, transcendentals=0),
    )(*args, *after)


def shape(dims, dtype):
    return jax.ShapeDtypeStruct(tuple(dims), dtype)


def dot(a, b):
    return lax.dot_general(a, b, (((1,), (0,)), ((), ())), preferred_element_type=F32)


def tree_sum(values):
    while len(values) > 1:
        values = [
            values[i] + values[i + 1] if i + 1 < len(values) else values[i]
            for i in range(0, len(values), 2)
        ]
    return values[0]


def pack_kernel(
    rows, cols, place_ref, x_ref, g_ref, one_ref, two_ref, own_ref, x_lines, g_lines, x_first, x_last, g_first, g_last, wide, flat, sems,
):
    cin = x_first.shape[2]
    even = place_ref[0] == 0
    copies = [
        pltpu.make_async_copy(source, target, sems.at[k])
        for k, (source, target) in enumerate(
            (
                (x_ref.at[:, 2 * cols - 16 : 2 * cols, :], x_last),
                (x_ref.at[:, 0:16, :], x_first),
                (g_ref.at[:, cols - 16 : cols, :], g_last),
                (g_ref.at[:, 0:16, :], g_first),
                (x_ref.at[2 * rows - 1], x_lines.at[0]),
                (x_ref.at[0:2], x_lines.at[1:3]),
                (g_ref.at[rows - 1], g_lines.at[0]),
                (g_ref.at[0:2], g_lines.at[1:3]),
            )
        )
    ]
    for copy in copies:
        copy.start()

    def x_column(ref, index):
        wide[...] = ref[...].astype(F32).reshape(2 * rows * 16, cin)
        return wide[pl.ds(index, 2 * rows, stride=16), :]

    def g_column(ref, index):
        halves = []
        for half in range(ref.shape[2] // 128):
            flat[...] = ref[:, :, half * 128 : (half + 1) * 128].astype(F32).reshape(rows * 16, 128)
            halves.append(flat[pl.ds(index, rows, stride=16), :])
        return jnp.concatenate(halves, 0)

    size = 2 * rows
    copies[0].wait()
    last = x_column(x_last, 15)
    copies[1].wait()
    leftwards = (x_column(x_first, 0), x_column(x_first, 1))
    copies[2].wait()
    rightwards = (last, g_column(g_last, 15))
    for copy in copies[3:]:
        copy.wait()
    for k in range(2):
        part = slice(k * size, (k + 1) * size)
        own_ref[part, :] = rightwards[k].astype(BF16)
        one_ref[part, :] = jnp.where(even, rightwards[k], leftwards[k]).astype(BF16)
        two_ref[part, :] = jnp.where(even, leftwards[k], rightwards[k]).astype(BF16)
        both = g_column(g_first, k).astype(BF16)
        one_ref[(k + 2) * size : (k + 3) * size, :] = both
        two_ref[(k + 2) * size : (k + 3) * size, :] = both


def choose(even, one, two):
    return jnp.where(even, one.astype(F32), two.astype(F32)).astype(BF16)


def rows_kernel(
    rows, cols, place_ref, x_lines, g_lines, got_one, got_two,
    left_ref, right_ref, one_ref, two_ref, own_ref, x_wide, g_wide,
):
    cin = x_lines.shape[2]
    depth = g_lines.shape[2]
    even_col = place_ref[0] == 0
    even_row = place_ref[1] == 0
    size = 2 * rows
    left_ref[...] = choose(even_col, got_two[0 : 2 * size, :], got_one[0 : 2 * size, :])
    right_ref[...] = choose(even_col, got_one[...], got_two[...])

    def cell(ref, index):
        first = index // 16 * 16
        return ref[first : first + 16, :].astype(F32)[index - first : index - first + 1, :]

    def x_line(cells, r):
        x_wide[...] = jnp.zeros((2 * cols + 32, cin), F32)
        x_wide[16 : 16 + 2 * cols, :] = cells.astype(F32)
        x_wide[15:16, :] = cell(left_ref, r)
        x_wide[16 + 2 * cols : 17 + 2 * cols, :] = cell(right_ref, r)
        x_wide[17 + 2 * cols : 18 + 2 * cols, :] = cell(right_ref, size + r)
        return x_wide[...]

    def g_line(cells, p):
        halves = []
        for half in range(depth // 128):
            g_wide[...] = jnp.zeros((cols + 16, 128), F32)
            g_wide[8 : 8 + cols, :] = cells[:, half * 128 : (half + 1) * 128].astype(F32)
            g_wide[7:8, :] = cell(left_ref, size + half * rows + p)
            g_wide[8 + cols : 9 + cols, :] = cell(right_ref, 2 * size + half * rows + p)
            g_wide[9 + cols : 10 + cols, :] = cell(right_ref, 3 * size + half * rows + p)
            halves.append(g_wide[...])
        return jnp.concatenate(halves, 0)

    line = 2 * cols + 32
    down = (x_line(x_lines[0], 2 * rows - 1), g_line(g_lines[0], rows - 1))
    up = (x_line(x_lines[1], 0), x_line(x_lines[2], 1))
    for k in range(2):
        part = slice(k * line, (k + 1) * line)
        own_ref[part, :] = down[k].astype(BF16)
        one_ref[part, :] = jnp.where(even_row, down[k], up[k]).astype(BF16)
        two_ref[part, :] = jnp.where(even_row, up[k], down[k]).astype(BF16)
        both = g_line(g_lines[1 + k], k).astype(BF16)
        one_ref[(k + 2) * line : (k + 3) * line, :] = both
        two_ref[(k + 2) * line : (k + 3) * line, :] = both


def planes_kernel(rows, cols, x_ref, planes_ref, wide, held, sems):
    cin = x_ref.shape[2]
    planes_ref[0:cols, :] = jnp.zeros((cols, 6 * cin), BF16)
    step = CHUNK // cols
    copies = [
        pltpu.make_async_copy(x_ref.at[2 * step * i : 2 * step * (i + 1)], held.at[i], sems.at[i])
        for i in range(rows // step)
    ]
    for copy in copies:
        copy.start()
    wide[:, 0:8, :] = jnp.zeros((2 * step, 8, cin), F32)

    def deinterleave(i):
        copies[i].wait()
        wide[:, 8 : 8 + 2 * cols, :] = held[i].astype(F32)
        row = (i * step + 1) * cols
        for parity in range(2):
            for slot, first in enumerate((7, 8, 9)):
                part = wide[pl.ds(parity, step, stride=2), pl.ds(first, cols, stride=2), :]
                lane = (parity * 3 + slot) * cin
                planes_ref[row : row + CHUNK, lane : lane + cin] = part.reshape(CHUNK, cin).astype(BF16)

    for i in range(rows // step):
        deinterleave(i)


def stride_kernel(rows, cols, planes_ref, w_ref, z_ref):
    cin = planes_ref.shape[1] // 6

    def convolve(i, carry):
        row = pl.multiple_of(i * LONG, LONG)
        above = planes_ref[pl.ds(row, LONG), 3 * cin :]
        here = planes_ref[pl.ds(pl.multiple_of(row + cols, cols), LONG), :]
        z_ref[pl.ds(row, LONG), :] = dot(jnp.concatenate([above, here], 1), w_ref[...])
        return carry

    lax.fori_loop(0, rows * cols // LONG, convolve, 0)


def edge_parts(rows, cols, xcol_ref, xrow_ref, col_pad, row_pad):
    col_pad[0:8, :] = xrow_ref[0:16, :].astype(F32)[8:16, :]
    col_pad[8 : 8 + 2 * rows, :] = xcol_ref[0 : 2 * rows, :].astype(F32)
    row_pad[0:8, :] = jnp.zeros((8, xrow_ref.shape[1]), F32)
    row_pad[8 : 8 + 2 * cols, :] = xrow_ref[16 : 16 + 2 * cols, :].astype(F32)
    left = [col_pad[pl.ds(first, rows, stride=2), :] for first in (7, 8, 9)]
    over = [row_pad[pl.ds(first, cols, stride=2), :] for first in (7, 8, 9)]
    return left, over


def edges_kernel(
    rows, cols, place_ref, z_in, xcol_ref, right_ref, own_col_ref, own_row_ref, got_one, got_two, w_ref,
    z_ref, stats_ref, xrow_ref, below_ref, z_rim_ref, col_pad, row_pad, rim, bottom, side,
):
    cin = xcol_ref.shape[1]
    even_row = place_ref[1] == 0
    line = 2 * cols + 32
    xrow_ref[...] = choose(even_row, got_two[0 : 2 * line, :], got_one[0 : 2 * line, :])
    below_ref[...] = choose(even_row, got_one[...], got_two[...])
    left, over = edge_parts(rows, cols, xcol_ref, xrow_ref, col_pad, row_pad)
    z_ref[...] = z_in[...]
    from_above = dot(jnp.concatenate(over, 1).astype(BF16), w_ref[0 : 3 * cin])
    from_left = (
        dot(left[0].astype(BF16), w_ref[0:cin])
        + dot(left[1].astype(BF16), w_ref[3 * cin : 4 * cin])
        + dot(left[2].astype(BF16), w_ref[6 * cin : 7 * cin])
    )
    z_ref[0:cols, :] = z_ref[0:cols, :] + from_above
    rim[...] = from_left
    for p in range(rows):
        z_ref[p * cols : p * cols + 1, :] = z_ref[p * cols : p * cols + 1, :] + rim[p : p + 1, :]
    z = z_ref[...]
    stats_ref[0:1, :] = jnp.sum(z, axis=0, keepdims=True)
    stats_ref[1:2, :] = jnp.sum(z * z, axis=0, keepdims=True)
    bottom[0] = own_row_ref[0:line, :].astype(F32)
    bottom[1] = below_ref[0:line, :].astype(F32)
    bottom[2] = below_ref[line : 2 * line, :].astype(F32)
    over_end = xrow_ref[2 * cols : 2 * cols + 32, :].astype(F32)
    for b, ref in enumerate((own_col_ref, right_ref, right_ref)):
        first = 2 * rows if b == 2 else 0
        side[b, 8:, :] = ref[first : first + 2 * rows, :].astype(F32)
        side[b, 7:8, :] = over_end[15 + b : 16 + b, :]
    parts = []
    for a in range(3):
        for b in range(3):
            low = bottom[a, pl.ds(15 + b, cols + 8, stride=2), :]
            beside = side[b, pl.ds(7 + a, rows, stride=2), :]
            parts.append(jnp.concatenate([low, beside], 0).astype(BF16))
    z_rim_ref[...] = dot(jnp.concatenate(parts, 1), w_ref[...])


def windows_kernel(rows, cols, planes_ref, xcol_ref, xrow_ref, t_ref, col_pad, row_pad, wide):
    cin = xrow_ref.shape[1]
    cells = rows * cols
    left, over = edge_parts(rows, cols, xcol_ref, xrow_ref, col_pad, row_pad)
    for half, parts in ((0, left[1]), (3, left[2])):
        wide[...] = planes_ref[cols:, half * cin : (half + 1) * cin].astype(F32)
        wide[pl.ds(0, rows, stride=cols), :] = parts
        window = wide[...].astype(BF16)
        t_ref[(half + 3) * cin : (half + 4) * cin, :] = window.T
    wide[cols:, :] = planes_ref[cols:cells, 3 * cin : 4 * cin].astype(F32)
    wide[0:cols, :] = over[0]
    wide[pl.ds(0, rows, stride=cols), :] = left[0]
    t_ref[0:cin, :] = wide[...].astype(BF16).T
    for slot in (1, 2):
        lane = (3 + slot) * cin
        below = planes_ref[cols:cells, lane : lane + cin]
        window = jnp.concatenate([over[slot].astype(BF16), below], 0)
        t_ref[slot * cin : (slot + 1) * cin, :] = window.T
    for slot in (1, 2, 4, 5):
        lane = slot * cin
        t_ref[lane + 3 * cin : lane + 4 * cin, :] = planes_ref[cols:, lane : lane + cin].T


def prepare_kernel(rows, cols, g_hbm, left_ref, right_ref, w_ref, body_ref, w_t_ref, done_ref, wide, rims, g_ref, sem):
    pitch = cols + 16
    depth = w_ref.shape[1]
    size = 2 * rows
    copy = pltpu.make_async_copy(g_hbm, g_ref, sem)
    copy.start()
    for tap in range(9):
        w_t_ref[tap * depth : (tap + 1) * depth, :] = w_ref[tap * depth : (tap + 1) * depth, :].T
    done_ref[...] = jnp.zeros(done_ref.shape, F32)
    for half in range(depth // 128):
        lanes = slice(half * 128, (half + 1) * 128)
        rims[0, :, lanes] = left_ref[size + half * rows : size + (half + 1) * rows, :].astype(F32)
        rims[1, :, lanes] = right_ref[2 * size + half * rows : 2 * size + (half + 1) * rows, :].astype(F32)
    copy.wait()
    for p in range(rows):
        first = p * pitch
        wide[first + 8 : first + 8 + cols, :] = g_ref[p].astype(F32)
        wide[first + 7 : first + 8, :] = rims[0, p : p + 1, :]
        wide[first + 8 + cols : first + 9 + cols, :] = rims[1, p : p + 1, :]
        for b in (0, 2):
            body_ref[b, p * cols : (p + 1) * cols, :] = wide[first + 9 - b : first + 9 - b + cols, :].astype(BF16)
    body_ref[1] = g_ref[...].reshape(body_ref.shape[1:])


def window(cols, body_ref, edge_ref, b, first, size):
    cells = body_ref.shape[1]
    parts = []
    if first < cols:
        parts.append(edge_ref[b, first:cols, :])
    start, stop = max(first, cols) - cols, min(first + size, cells + cols) - cols
    parts.append(body_ref[b, start:stop, :])
    if first + size > cells + cols:
        parts.append(edge_ref[b, cols : first + size - cells, :])
    return parts[0] if len(parts) == 1 else jnp.concatenate(parts, 0)


def upstream_kernel(
    rows, cols, body_ref, w_t_ref, right_ref, own_col_ref, own_row_ref, above_ref, below_ref,
    edge_ref, act_grad_ref, rim_ref, wide, bottom, side,
):
    pitch = cols + 16
    depth = act_grad_ref.shape[1]
    size = 2 * rows
    line = 2 * cols + 32
    for half in range(depth // 128):
        lanes = slice(half * 128, (half + 1) * 128)
        side[0, 8 : 8 + rows, lanes] = right_ref[3 * size + half * rows : 3 * size + (half + 1) * rows, :].astype(F32)
        side[1, 8 : 8 + rows, lanes] = right_ref[2 * size + half * rows : 2 * size + (half + 1) * rows, :].astype(F32)
        side[2, 8 : 8 + rows, lanes] = own_col_ref[size + half * rows : size + (half + 1) * rows, :].astype(F32)
        over = above_ref[line + half * pitch : line + (half + 1) * pitch, :].astype(F32)
        under = below_ref[2 * line + half * pitch : 2 * line + (half + 1) * pitch, :].astype(F32)
        wide[0:pitch, lanes] = over
        wide[pitch : 2 * pitch, lanes] = under
        for b in range(3):
            side[b, 7:8, lanes] = over[9 + cols - b : 10 + cols - b, :]
            side[b, 8 + rows : 9 + rows, lanes] = under[9 + cols - b : 10 + cols - b, :]
        bottom[0, 0:pitch, lanes] = below_ref[3 * line + half * pitch : 3 * line + (half + 1) * pitch, :].astype(F32)
        bottom[1, 0:pitch, lanes] = under
        bottom[2, 0:pitch, lanes] = own_row_ref[line + half * pitch : line + (half + 1) * pitch, :].astype(F32)
    bottom[:, pitch:, :] = jnp.zeros((3, 8, depth), F32)
    for b in range(3):
        edge_ref[b, 0:cols, :] = wide[9 - b : 9 - b + cols, :].astype(BF16)
        edge_ref[b, cols:, :] = wide[pitch + 9 - b : pitch + 9 - b + cols, :].astype(BF16)
    for row in range(0, rows * cols, LONG):
        parts = []
        for a in range(3):
            for b in range(3):
                parts.append(window(cols, body_ref, edge_ref, b, row + (2 - a) * cols, LONG))
        act_grad_ref[row : row + LONG, :] = dot(jnp.concatenate(parts, 1), w_t_ref[...])
    parts = []
    for a in range(3):
        for b in range(3):
            low = bottom[a, 9 - b : 17 - b + cols, :]
            beside = side[b, 9 - a : 9 - a + rows, :]
            parts.append(jnp.concatenate([low, beside], 0).astype(BF16))
    rim_ref[...] = dot(jnp.concatenate(parts, 1), w_t_ref[...])


def group_sum(value, depth):
    size = depth // GROUPS
    one = lax.broadcasted_iota(jnp.int32, (depth, depth), 0) // size
    two = lax.broadcasted_iota(jnp.int32, (depth, depth), 1) // size
    same = jnp.where(one == two, 1.0, 0.0).astype(F32)
    return lax.dot_general(
        value, same, (((1,), (0,)), ((), ())), precision=lax.Precision.HIGHEST, preferred_element_type=F32
    )


def add_kernel(*refs):
    refs[-1][...] = tree_sum([r[...] for r in refs[:-1]])


def stack_kernel(*refs):
    for k, ref in enumerate(refs[:-1]):
        refs[-1][k] = ref[...]


def activate_kernel(norm_count, own_ref, pair_ref, z_ref, act_grad_ref, gain_ref, bias_ref, act_ref, pre_ref, sums_ref, moments_ref):
    cells, depth = z_ref.shape
    total = group_sum(own_ref[...] + pair_ref[...], depth) / norm_count
    mean = total[0:1, :]
    inv_std = 1.0 / jnp.sqrt(total[1:2, :] - mean * mean + 1e-05)
    moments_ref[0:1, :] = mean
    moments_ref[1:2, :] = inv_std
    gain = gain_ref[...]
    bias = bias_ref[...]

    def chunk(i, carry):
        row = pl.multiple_of(i * 64, 64)
        normed = (z_ref[pl.ds(row, 64), :] - mean) * inv_std
        shifted = normed * gain + bias
        sig = 1.0 / (1.0 + jnp.exp(-shifted))
        act_ref[pl.ds(row, 64), :] = (shifted * sig).astype(BF16)
        pre = act_grad_ref[pl.ds(row, 64), :] * sig * (1.0 + shifted * (1.0 - sig))
        pre_ref[pl.ds(row, 64), :] = pre
        one = jnp.sum(pre.reshape(8, 8, depth), axis=0)
        two = jnp.sum((pre * normed).reshape(8, 8, depth), axis=0)
        return carry[0] + one, carry[1] + two

    zero = jnp.zeros((8, depth), F32)
    one, two = lax.fori_loop(0, cells // 64, chunk, (zero, zero))
    sums_ref[0:1, :] = jnp.sum(one, axis=0, keepdims=True)
    sums_ref[1:2, :] = jnp.sum(two, axis=0, keepdims=True)


def second_kernel(rows, cols, place_ref, act_ref, body_ref, edge_ref, keep_ref, send_ref):
    cells = rows * cols
    depth = act_ref.shape[1]
    act_t = act_ref[...].T
    half, size = depth // 2, depth // 8
    even = place_ref[4] == 0
    spot = place_ref[5] & 3
    for a in range(3):
        for b in range(3):
            first = (2 - a) * cols
            tap = a * 3 + b
            both = dot(act_t, window(cols, body_ref, edge_ref, b, first, cells))
            mine = jnp.where(even, both[0:half, :], both[half:, :])
            theirs = jnp.where(even, both[half:, :], both[0:half, :]).astype(BF16)
            for j in range(4):
                keep_ref[j ^ spot, tap * size : (tap + 1) * size, :] = mine[j * size : (j + 1) * size, :]
                send_ref[j ^ spot, tap * size : (tap + 1) * size, :] = theirs[j * size : (j + 1) * size, :]


def conv_grad_kernel(norm_count, rows, cols, place_ref, own_ref, pair_ref, *refs):
    z_ref, pre_ref, moments_ref, gain_ref, bias_ref, z_rim_ref, act_rim_ref, t_ref = refs[:8]
    grad_ref, rim_ref, total_ref, keep_ref, send_ref = refs[8:]
    cells, depth = z_ref.shape
    total = own_ref[...] + pair_ref[...]
    total_ref[...] = total
    gain = gain_ref[...]
    means = group_sum(total * gain, depth) / norm_count
    mean = moments_ref[0:1, :]
    inv_std = moments_ref[1:2, :]
    shift = means[0:1, :]
    scale = means[1:2, :]

    def value(z, pre):
        return ((gain * pre - shift - (z - mean) * inv_std * scale) * inv_std).astype(BF16)

    def chunk(i, carry):
        row = pl.multiple_of(i * 64, 64)
        grad_ref[pl.ds(row, 64), :] = value(z_ref[pl.ds(row, 64), :], pre_ref[pl.ds(row, 64), :])
        return carry

    lax.fori_loop(0, cells // 64, chunk, 0)
    z = z_rim_ref[...]
    shifted = (z - mean) * inv_std * gain + bias_ref[...]
    sig = 1.0 / (1.0 + jnp.exp(-shifted))
    pre = act_rim_ref[...] * sig * (1.0 + shifted * (1.0 - sig))
    cell = lax.broadcasted_iota(jnp.int32, z.shape, 0)
    to_right = jnp.where(cell >= cols, place_ref[2], 1)
    to_below = jnp.where(cell < cols + 8, place_ref[3], 1)
    rim_ref[...] = jnp.where(to_right * to_below == 1, value(z, pre).astype(F32), 0.0)

    half = t_ref.shape[0] // 2
    size = half // 4
    core = place_ref[4]
    spot = place_ref[5] & 3
    theirs = dot(t_ref[pl.ds(pl.multiple_of((1 - core) * half, 16), half), :], grad_ref[...]).astype(BF16)
    mine = dot(t_ref[pl.ds(pl.multiple_of(core * half, 16), half), :], grad_ref[...])
    for j in range(4):
        send_ref[j ^ spot] = theirs[j * size : (j + 1) * size, :]
        keep_ref[j ^ spot] = mine[j * size : (j + 1) * size, :]


def input_kernel(rows, cols, d_ref, rim_ref, w_ref, out_ref, done_ref, plain, shifted, w_t, wide, mixed):
    cells = rows * cols
    cin = out_ref.shape[2]
    depth = d_ref.shape[1]
    pitch = cols + 8
    plain[0:cells, :] = d_ref[...]
    plain[cells:, :] = rim_ref[0:cols, :].astype(BF16)
    for p in range(rows + 1):
        first = p * pitch
        wide[first : first + cols, :] = plain[p * cols : (p + 1) * cols, :].astype(F32)
        next_cell = cols + 8 + p if p < rows else cols
        wide[first + cols : first + cols + 1, :] = rim_ref[next_cell : next_cell + 1, :]
        shifted[p * cols : (p + 1) * cols, :] = wide[first + 1 : first + 1 + cols, :].astype(BF16)
    for place, tap in enumerate((4, 5, 7, 8, 3, 6, 1, 2, 0)):
        w_t[:, place * cin : (place + 1) * cin] = w_ref[tap * cin : (tap + 1) * cin, :].T
    done_ref[...] = jnp.zeros(done_ref.shape, F32)
    step = CHUNK // cols

    def chunk(i, carry):
        row = pl.multiple_of(i * CHUNK, CHUNK)
        under = pl.multiple_of(row + cols, cols)
        own = dot(plain[pl.ds(row, CHUNK), :], w_t[:, 0 : 4 * cin])
        right = dot(shifted[pl.ds(row, CHUNK), :], w_t[:, 4 * cin : 6 * cin])
        below = dot(plain[pl.ds(under, CHUNK), :], w_t[:, 6 * cin : 8 * cin])
        corner = dot(shifted[pl.ds(under, CHUNK), :], w_t[:, 8 * cin :])
        even_even = own[:, 0:cin]
        even_odd = own[:, cin : 2 * cin] + right[:, 0:cin]
        odd_even = own[:, 2 * cin : 3 * cin] + below[:, 0:cin]
        odd_odd = own[:, 3 * cin :] + right[:, cin:] + below[:, cin:] + corner
        for parity, pair in enumerate(((even_even, even_odd), (odd_even, odd_odd))):
            for side in range(2):
                mixed[pl.ds(parity, step, stride=2), pl.ds(side, cols, stride=2), :] = pair[side].reshape(
                    step, cols, cin
                )
        out_ref[pl.ds(pl.multiple_of(i * 2 * step, 2 * step), 2 * step)] = mixed[...].astype(BF16)
        return carry

    lax.fori_loop(0, rows // step, chunk, 0)


def first_split_kernel(place_ref, mine_ref, other_ref, keep_ref, send_ref):
    even = place_ref[4] == 0
    none, along_y, along_x, both = [mine_ref[k] + other_ref[k].astype(F32) for k in range(4)]
    keep_ref[0] = none
    keep_ref[1] = jnp.where(even, along_y, along_x)
    send_ref[0] = jnp.where(even, along_x, along_y).astype(BF16)
    send_ref[1] = both.astype(BF16)


def second_split_kernel(mine_ref, other_ref, keep_ref, send_ref):
    keep_ref[...] = mine_ref[0] + other_ref[0].astype(F32)
    send_ref[...] = (mine_ref[1] + other_ref[1].astype(F32)).astype(BF16)


def half_kernel(slots_ref, other_ref, *refs):
    own_ref, one_ref, two_ref, three_ref = refs[-4:]
    rows = slots_ref.shape[1]
    own_ref[...] = slots_ref[0] + other_ref[0]
    for k, ref in enumerate((one_ref, two_ref, three_ref)):
        ref[0:rows, :] = (slots_ref[k + 1] + other_ref[k + 1]).astype(BF16)
    if len(refs) > 4:
        two_ref[rows:, :] = three_parts(refs[0][...])


def three_parts(pair):
    high = pair.astype(BF16).astype(F32)
    rest = pair - high
    middle = rest.astype(BF16).astype(F32)
    low = rest - middle
    zeros = jnp.zeros((10, pair.shape[1]), F32)
    return jnp.concatenate([high, middle, low, zeros], 0).astype(BF16)


def from_parts(parts):
    parts = parts.astype(F32)
    return parts[0:2, :] + parts[2:4, :] + parts[4:6, :]


def total_kernel(*refs):
    rows = refs[-1].shape[0]
    refs[-1][...] = tree_sum([r[0:rows, :].astype(F32) for r in refs[:-1]]).astype(BF16)


def both_kernel(count, *refs):
    second, first, out_ref = refs[:count], refs[count:-1], refs[-1]
    rows = second[0].shape[0]
    out_ref[0:rows, :] = tree_sum([r[...].astype(F32) for r in second]).astype(BF16)
    out_ref[rows:, :] = tree_sum([r[...].astype(F32) for r in first]).astype(BF16)


def first_total_kernel(own_ref, one_ref, two_ref, three_ref, pair_ref, out_ref, bias_ref, gain_ref):
    total_kernel(own_ref, one_ref, two_ref, three_ref, out_ref)
    rows = out_ref.shape[0]
    both = from_parts(three_parts(pair_ref[...])) + from_parts(two_ref[rows:, :])
    bias_ref[...] = both[0:1, :]
    gain_ref[...] = both[1:2, :]


def gather_kernel(slots, rows, place_ref, *refs):
    me = place_ref[5]
    count = len(slots)
    shards = refs[: 2 * count]
    second_ref, first_ref, second_stage, first_stage, sems = refs[-5:]
    copies = []
    for i, slot in enumerate(slots):
        for k, where in ((i, me ^ slot), (i + count, me ^ slot ^ 4)):
            second_stage[k] = shards[k][0:rows, :].astype(F32).reshape(second_stage.shape[1:])
            first_stage[k] = shards[k][rows:, :].astype(F32)
            copies.append(pltpu.make_async_copy(second_stage.at[k], second_ref.at[:, where], sems.at[2 * k]))
            copies.append(pltpu.make_async_copy(first_stage.at[k], first_ref.at[where], sems.at[2 * k + 1]))
            copies[-2].start()
            copies[-1].start()
    for copy in copies:
        copy.wait()


def on_device(dp_size, tiles, images, first_weight, norm_gain, norm_bias, second_weight, upstream):
    rows, cols, depth = upstream.shape[2:]
    cin = images.shape[4]
    cells = rows * cols
    group_size = depth // GROUPS
    norm_count = float(cells * tiles * group_size)
    tile_rows = tiles // TCOLS
    axes = ("dp", "space")
    devices = dp_size * tiles

    def flip(value, mask):
        return lax.ppermute(value, axes, [(i, i ^ mask) for i in range(devices)])

    def swapped(value, down, right):
        pairs = []
        for t in range(tiles):
            spot = (t + TCOLS + 2) % tiles
            r, c = spot // TCOLS, spot % TCOLS
            r = r if not down else ((r + down - 1) ^ 1) - down + 1
            c = c if not right else ((c + right - 1) ^ 1) - right + 1
            if 0 <= r < tile_rows and 0 <= c < TCOLS:
                pairs.append((t, (r * TCOLS + c - TCOLS - 2) % tiles))
        return lax.ppermute(value, "space", pairs)

    def added(parts, after=()):
        return call(add_kernel, [shape(parts[0].shape, F32)], parts, after=after)[0]

    def fetched(value, after=()):
        parts = [value] + [flip(value, 2 * k) for k in (1, 2, 3)]
        for k in range(3, tiles.bit_length() - 1):
            total = added(parts, after)
            parts, after = [total, flip(total, 1 << k)], ()
        return parts

    def crossed(value, even, odd):
        return lax.ppermute(value, axes, [(i, i ^ (odd if i % 2 else even)) for i in range(devices)])

    def along(value, size, step):
        return [value] + [flip(value, step * k) for k in range(1, size)]

    def total(parts, after=()):
        if len(parts) == 1:
            return parts[0]
        return call(total_kernel, [shape(parts[0].shape, BF16)], parts, after=after)[0]

    def halved(slots, more=(), after=()):
        part = slots[0].shape[1:]
        longer = (part[0] + 16 * len(more), part[1])
        outs = [shape(part, F32), shape(part, BF16), shape(longer, BF16), shape(part, BF16)]
        return call(half_kernel, outs, [slots[0], flip(slots[1], 1), *more], after=after)

    def halves(value):
        pair = [value]
        for k in range(2, tiles.bit_length() - 1):
            pair = [total(pair)]
            pair.append(flip(pair[0], 1 << k))
        return pair

    masks = [0, 2, tiles, tiles + 2]

    def quartered(parts):
        return [parts[0]] + [flip(parts[k], masks[k]) for k in (1, 2, 3)]

    def quarters(shard):
        return [shard] + [flip(shard, masks[k]) for k in (1, 2, 3)]

    space = lax.axis_index("space")
    spot = (space + TCOLS + 2) % tiles
    column, row = spot % TCOLS, spot // TCOLS
    me = (space % 2) * 4 + (lax.axis_index("dp") % 2) * 2 + (space // 2) % 2
    place = jnp.stack([column % 2, row % 2, column < TCOLS - 1, row < tile_rows - 1, space % 2, me]).astype(jnp.int32)
    x = pltpu.with_memory_space_constraint(images[0, 0], pltpu.HBM)
    g3 = pltpu.with_memory_space_constraint(upstream[0, 0], pltpu.HBM)
    w1 = first_weight.reshape(9 * cin, depth)
    w2 = second_weight.reshape(9 * depth, depth)
    gain = norm_gain.reshape(1, depth)
    bias = norm_bias.reshape(1, depth)

    hbm = pl.BlockSpec(memory_space=pltpu.HBM)
    smem = pl.BlockSpec(memory_space=pltpu.SMEM)
    vmem = pl.BlockSpec(memory_space=pltpu.VMEM)
    ends = shape((4 * 2 * rows, cin), BF16)
    half_ends = shape((2 * 2 * rows, cin), BF16)
    one, two, own_column, x_lines, g_lines = call(
        functools.partial(pack_kernel, rows, cols),
        [ends, ends, half_ends, shape((3, 2 * cols, cin), BF16), shape((3, cols, depth), BF16)],
        [place, x, g3],
        [pltpu.VMEM((2 * rows, 16, cin), BF16)] * 2
        + [pltpu.VMEM((rows, 16, depth), BF16)] * 2
        + [pltpu.VMEM((2 * rows * 16, cin), F32), pltpu.VMEM((rows * 16, 128), F32), pltpu.SemaphoreType.DMA((8,))],
        specs=[smem, hbm, hbm],
    )
    one = swapped(one, 0, 1)
    two = swapped(two, 0, 2)
    (planes,) = call(
        functools.partial(planes_kernel, rows, cols),
        [shape((cells + cols, 6 * cin), BF16)],
        [x],
        [
            pltpu.VMEM((2 * CHUNK // cols, 2 * cols + 8, cin), F32),
            pltpu.VMEM((cells // CHUNK, 2 * CHUNK // cols, 2 * cols, cin), BF16),
            pltpu.SemaphoreType.DMA((cells // CHUNK,)),
        ],
        specs=[hbm],
        flops=cells * 9 * cin * depth,
    )
    lines = shape((4 * (2 * cols + 32), cin), BF16)
    half_lines = shape((2 * (2 * cols + 32), cin), BF16)
    from_left, from_right, one, two, own_row = call(
        functools.partial(rows_kernel, rows, cols),
        [half_ends, ends, lines, lines, half_lines],
        [place, x_lines, g_lines, one, two],
        [pltpu.VMEM((2 * cols + 32, cin), F32), pltpu.VMEM((cols + 16, 128), F32)],
        smem=1,
        after=[planes],
    )
    got_one = swapped(one, 1, 0)
    got_two = swapped(two, 2, 0)
    (z,) = call(
        functools.partial(stride_kernel, rows, cols),
        [shape((cells, depth), F32)],
        [planes, w1],
        flops=2 * cells * 9 * cin * depth,
        after=[one],
    )
    pads = [pltpu.VMEM((2 * rows + 8, cin), F32), pltpu.VMEM((2 * cols + 8, cin), F32)]
    body, w_t, prepared = call(
        functools.partial(prepare_kernel, rows, cols),
        [shape((3, cells, depth), BF16), shape((9 * depth, depth), BF16), shape((8, 128), F32)],
        [g3, from_left, from_right, w2],
        [
            pltpu.VMEM((rows * (cols + 16), depth), F32),
            pltpu.VMEM((2, rows, depth), F32),
            pltpu.VMEM((rows, cols, depth), BF16),
            pltpu.SemaphoreType.DMA,
        ],
        specs=[hbm, vmem, vmem, vmem],
        after=[one],
    )
    rim = rows + cols + 8
    z, stats, from_above, from_below, z_rim = call(
        functools.partial(edges_kernel, rows, cols),
        [shape((cells, depth), F32), shape((2, depth), F32), half_lines, lines, shape((rim, depth), F32)],
        [place, z, from_left, from_right, own_column, own_row, got_one, got_two, w1],
        pads
        + [
            pltpu.VMEM((rows, depth), F32),
            pltpu.VMEM((3, 2 * cols + 32, cin), F32),
            pltpu.VMEM((3, 2 * rows + 8, cin), F32),
        ],
        smem=1,
        after=[prepared],
        flops=2 * 80 * 3 * cin * depth,
    )
    stats = fetched(added([stats, flip(stats, 1)]))
    edge, act_grad, act_rim = call(
        functools.partial(upstream_kernel, rows, cols),
        [shape((3, 2 * cols, depth), BF16), shape((cells, depth), F32), shape((rim, depth), F32)],
        [body, w_t, from_right, own_column, own_row, from_above, from_below],
        [
            pltpu.VMEM((2 * (cols + 16), depth), F32),
            pltpu.VMEM((3, cols + 24, depth), F32),
            pltpu.VMEM((3, rows + 16, depth), F32),
        ],
        flops=2 * cells * 9 * depth * depth,
    )
    activated, pre_grad, sums, moments = call(
        functools.partial(activate_kernel, norm_count),
        [shape((cells, depth), BF16), shape((cells, depth), F32), shape((2, depth), F32), shape((2, depth), F32)],
        stats + [z, act_grad, gain, bias],
        flops=cells * depth * 30,
    )
    other = flip(sums, 1)
    second_slots = call(
        functools.partial(second_kernel, rows, cols),
        [shape((4, 9 * depth // 8, depth), F32), shape((4, 9 * depth // 8, depth), BF16)],
        [place, activated, body, edge],
        flops=2 * cells * 9 * depth * depth,
        smem=1,
    )
    near = added([sums, other], second_slots[1:])
    part = second_slots[0].shape[1:]
    kept, sent = call(
        first_split_kernel,
        [shape((2,) + part, F32), shape((2,) + part, BF16)],
        [place, second_slots[0], flip(second_slots[1], 1)],
        smem=1,
        after=[near],
    )
    parts = fetched(near, [kept])
    second_parts = call(
        second_split_kernel,
        [shape(part, F32), shape(part, BF16)],
        [kept, crossed(sent, tiles, 2)],
        after=parts[:1],
    )
    (windows,) = call(
        functools.partial(windows_kernel, rows, cols),
        [shape((9 * cin, cells), BF16)],
        [planes, from_left, from_above],
        pads + [pltpu.VMEM((cells, cin), F32)],
        flops=2 * cells * 9 * cin * depth,
        after=second_parts[:1],
    )
    second_shard = total([second_parts[0], crossed(second_parts[1], 2, tiles)])
    pair = halves(total(along(second_shard, dp_size // 2, 2 * tiles)))
    conv_grad, grad_rim, sum_pair, *first_slots = call(
        functools.partial(conv_grad_kernel, norm_count, rows, cols),
        [
            shape((cells, depth), BF16),
            shape((rim, depth), F32),
            shape((2, depth), F32),
            shape((4, 9 * cin // 8, depth), F32),
            shape((4, 9 * cin // 8, depth), BF16),
        ],
        [place] + parts + [z, pre_grad, moments, gain, bias, z_rim, act_rim, windows],
        flops=2 * cells * 9 * cin * depth,
        smem=1,
        after=[second_shard],
    )
    first_parts = quartered(halved(first_slots, [sum_pair]))
    first_shard, bias_grad, gain_grad = call(
        first_total_kernel,
        [shape(first_slots[0].shape[1:], BF16), shape((1, depth), F32), shape((1, depth), F32)],
        first_parts + [sum_pair],
    )
    first_shard = along(total(along(first_shard, dp_size // 2, 2 * tiles)), tiles // 4, 4)
    input_grad, done = call(
        functools.partial(input_kernel, rows, cols),
        [shape((2 * rows, 2 * cols, cin), BF16), shape((8, 128), F32)],
        [conv_grad, grad_rim, w1],
        [
            pltpu.VMEM((cells + cols, depth), BF16),
            pltpu.VMEM((cells + cols, depth), BF16),
            pltpu.VMEM((depth, 9 * cin), BF16),
            pltpu.VMEM(((rows + 1) * (cols + 8), depth), F32),
            pltpu.VMEM((2 * CHUNK // cols, 2 * cols, cin), F32),
        ],
        flops=2 * cells * 9 * cin * depth,
    )
    sizes = second_slots[0].shape[1], first_slots[0].shape[1]
    (shard,) = call(
        functools.partial(both_kernel, len(pair)),
        [shape((sum(sizes), depth), BF16)],
        pair + first_shard,
        after=[done],
    )
    for k in range(1, dp_size.bit_length() - 1):
        bias_grad = bias_grad + flip(bias_grad, tiles << k)
        gain_grad = gain_grad + flip(gain_grad, tiles << k)
    own = quarters(shard)
    grads = [shape((9, 8, depth // 8, depth), F32), shape((8, sizes[1], depth), F32)]
    for slots in ((0,), (1, 2, 3)):
        here = [own[slot] for slot in slots]
        shards = here + [flip(value, 1) for value in here]
        left = list(grads) if len(slots) > 1 else []
        grads = call(
            functools.partial(gather_kernel, slots, sizes[0]),
            [shape(g.shape, F32) for g in grads],
            [place] + shards + left,
            [
                pltpu.VMEM((len(shards), 9, depth // 8, depth), F32),
                pltpu.VMEM((len(shards), sizes[1], depth), F32),
                pltpu.SemaphoreType.DMA((2 * len(shards),)),
            ],
            specs=[smem] + [vmem] * len(shards) + [hbm] * len(left),
            out_specs=[hbm] * 2,
            aliases={1 + len(shards) + k: k for k in range(len(left))},
        )
    second_grad, first_grad = grads
    return (
        input_grad[None, None],
        first_grad.reshape(first_weight.shape),
        second_grad.reshape(second_weight.shape),
        gain_grad.reshape(depth),
        bias_grad.reshape(depth),
    )


def solution(mesh):
    placed = (
        P("dp", "space", None, None, None),
        P(),
        P(),
        P(),
        P(),
        P("dp", "space", None, None, None),
    )
    return jax.shard_map(
        functools.partial(on_device, mesh.shape["dp"], mesh.shape["space"]),
        mesh=mesh,
        in_specs=placed,
        out_specs=(P("dp", "space", None, None, None), P(), P(), P(), P()),
        check_vma=False,
    )
```

```python
import functools

import jax
import jax.numpy as jnp
from jax import lax
from jax.experimental import pallas as pl
from jax.experimental.pallas import tpu as pltpu
from jax.sharding import PartitionSpec as P

GROUPS = 32
TCOLS = 4
F32 = jnp.float32
BF16 = jnp.bfloat16
MIB = 1024 * 1024
CHUNK = 256
LONG = 512


def call(kernel, outs, args, scratch=(), flops=0, limit=20, smem=0, after=(), specs=None, grid=(), out_specs=None, aliases=None):
    if specs is None:
        specs = [pl.BlockSpec(memory_space=pltpu.SMEM)] * smem
        specs += [pl.BlockSpec(memory_space=pltpu.VMEM)] * (len(args) - smem)
    moved = sum(a.size * a.dtype.itemsize for a in list(args) + list(outs))
    count = len(args)

    def body(*refs):
        kernel(*refs[:count], *refs[count + len(after) :])

    return pl.pallas_call(
        body,
        out_shape=list(outs),
        grid=grid,
        in_specs=list(specs) + [pl.BlockSpec(memory_space=pl.ANY)] * len(after),
        out_specs=out_specs or [pl.BlockSpec(memory_space=pltpu.VMEM)] * len(outs),
        scratch_shapes=list(scratch),
        input_output_aliases=aliases or {},
        compiler_params=pltpu.CompilerParams(vmem_limit_bytes=limit * MIB),
        cost_estimate=pl.CostEstimate(flops=flops, bytes_accessed=moved, transcendentals=0),
    )(*args, *after)


def shape(dims, dtype):
    return jax.ShapeDtypeStruct(tuple(dims), dtype)


def dot(a, b):
    return lax.dot_general(a, b, (((1,), (0,)), ((), ())), preferred_element_type=F32)


def tree_sum(values):
    while len(values) > 1:
        values = [
            values[i] + values[i + 1] if i + 1 < len(values) else values[i]
            for i in range(0, len(values), 2)
        ]
    return values[0]


def pack_kernel(
    rows, cols, place_ref, x_ref, g_ref, one_ref, two_ref, own_ref, x_lines, g_lines, x_first, x_last, g_first, g_last, wide, flat, sems,
):
    cin = x_first.shape[2]
    even = place_ref[0] == 0
    copies = [
        pltpu.make_async_copy(source, target, sems.at[k])
        for k, (source, target) in enumerate(
            (
                (x_ref.at[:, 2 * cols - 16 : 2 * cols, :], x_last),
                (x_ref.at[:, 0:16, :], x_first),
                (g_ref.at[:, cols - 16 : cols, :], g_last),
                (g_ref.at[:, 0:16, :], g_first),
                (x_ref.at[2 * rows - 1], x_lines.at[0]),
                (x_ref.at[0:2], x_lines.at[1:3]),
                (g_ref.at[rows - 1], g_lines.at[0]),
                (g_ref.at[0:2], g_lines.at[1:3]),
            )
        )
    ]
    for copy in copies:
        copy.start()

    def x_column(ref, index):
        wide[0 : 2 * rows * 16, :] = ref[...].astype(F32).reshape(2 * rows * 16, cin)
        return wide[pl.ds(index, 2 * rows, stride=16), :]

    def g_column(ref, index):
        halves = []
        for half in range(ref.shape[2] // 128):
            flat[0 : rows * 16, :] = ref[:, :, half * 128 : (half + 1) * 128].astype(F32).reshape(rows * 16, 128)
            halves.append(flat[pl.ds(index, rows, stride=16), :])
        return jnp.concatenate(halves, 0)

    size = 2 * rows
    copies[0].wait()
    last = x_column(x_last, 15)
    copies[1].wait()
    leftwards = (x_column(x_first, 0), x_column(x_first, 1))
    copies[2].wait()
    rightwards = (last, g_column(g_last, 15))
    for copy in copies[3:]:
        copy.wait()
    for k in range(2):
        part = slice(k * size, (k + 1) * size)
        own_ref[part, :] = rightwards[k].astype(BF16)
        one_ref[part, :] = jnp.where(even, rightwards[k], leftwards[k]).astype(BF16)
        two_ref[part, :] = jnp.where(even, leftwards[k], rightwards[k]).astype(BF16)
        both = g_column(g_first, k).astype(BF16)
        one_ref[(k + 2) * size : (k + 3) * size, :] = both
        two_ref[(k + 2) * size : (k + 3) * size, :] = both


def choose(even, one, two):
    return jnp.where(even, one.astype(F32), two.astype(F32)).astype(BF16)


def rows_kernel(
    rows, cols, place_ref, x_lines, g_lines, got_one, got_two,
    left_ref, right_ref, one_ref, two_ref, own_ref, x_wide, g_wide,
):
    cin = x_lines.shape[2]
    depth = g_lines.shape[2]
    even_col = place_ref[0] == 0
    even_row = place_ref[1] == 0
    size = 2 * rows
    left_ref[...] = choose(even_col, got_two[0 : 2 * size, :], got_one[0 : 2 * size, :])
    right_ref[...] = choose(even_col, got_one[...], got_two[...])

    def cell(ref, index):
        first = index // 16 * 16
        return ref[first : first + 16, :].astype(F32)[index - first : index - first + 1, :]

    def x_line(cells, r):
        x_wide[...] = jnp.zeros((2 * cols + 32, cin), F32)
        x_wide[16 : 16 + 2 * cols, :] = cells.astype(F32)
        x_wide[15:16, :] = cell(left_ref, r)
        x_wide[16 + 2 * cols : 17 + 2 * cols, :] = cell(right_ref, r)
        x_wide[17 + 2 * cols : 18 + 2 * cols, :] = cell(right_ref, size + r)
        return x_wide[...]

    def g_line(cells, p):
        halves = []
        for half in range(depth // 128):
            g_wide[...] = jnp.zeros((cols + 16, 128), F32)
            g_wide[8 : 8 + cols, :] = cells[:, half * 128 : (half + 1) * 128].astype(F32)
            g_wide[7:8, :] = cell(left_ref, size + half * rows + p)
            g_wide[8 + cols : 9 + cols, :] = cell(right_ref, 2 * size + half * rows + p)
            g_wide[9 + cols : 10 + cols, :] = cell(right_ref, 3 * size + half * rows + p)
            halves.append(g_wide[...])
        return jnp.concatenate(halves, 0)

    line = 2 * cols + 32
    down = (x_line(x_lines[0], 2 * rows - 1), g_line(g_lines[0], rows - 1))
    up = (x_line(x_lines[1], 0), x_line(x_lines[2], 1))
    for k in range(2):
        part = slice(k * line, (k + 1) * line)
        own_ref[part, :] = down[k].astype(BF16)
        one_ref[part, :] = jnp.where(even_row, down[k], up[k]).astype(BF16)
        two_ref[part, :] = jnp.where(even_row, up[k], down[k]).astype(BF16)
        both = g_line(g_lines[1 + k], k).astype(BF16)
        one_ref[(k + 2) * line : (k + 3) * line, :] = both
        two_ref[(k + 2) * line : (k + 3) * line, :] = both


def planes_kernel(rows, cols, x_ref, planes_ref, wide, held, sems):
    cin = x_ref.shape[2]
    planes_ref[0:cols, :] = jnp.zeros((cols, 6 * cin), BF16)
    step = CHUNK // cols
    copies = [
        pltpu.make_async_copy(x_ref.at[2 * step * i : 2 * step * (i + 1)], held.at[i], sems.at[i])
        for i in range(rows // step)
    ]
    for copy in copies:
        copy.start()
    wide[0 : 2 * step, 0:8, :] = jnp.zeros((2 * step, 8, cin), F32)

    def deinterleave(i):
        copies[i].wait()
        wide[0 : 2 * step, 8 : 8 + 2 * cols, :] = held[i].astype(F32)
        row = (i * step + 1) * cols
        for parity in range(2):
            for slot, first in enumerate((7, 8, 9)):
                part = wide[pl.ds(parity, step, stride=2), pl.ds(first, cols, stride=2), :]
                lane = (parity * 3 + slot) * cin
                planes_ref[row : row + CHUNK, lane : lane + cin] = part.reshape(CHUNK, cin).astype(BF16)

    for i in range(rows // step):
        deinterleave(i)


def stride_kernel(rows, cols, planes_ref, w_ref, z_ref):
    cin = planes_ref.shape[1] // 6

    def convolve(i, carry):
        row = pl.multiple_of(i * LONG, LONG)
        above = planes_ref[pl.ds(row, LONG), 3 * cin :]
        here = planes_ref[pl.ds(pl.multiple_of(row + cols, cols), LONG), :]
        z_ref[pl.ds(row, LONG), :] = dot(jnp.concatenate([above, here], 1), w_ref[...])
        return carry

    lax.fori_loop(0, rows * cols // LONG, convolve, 0)


def edge_parts(rows, cols, xcol_ref, xrow_ref, col_pad, row_pad):
    col_pad[0:8, :] = xrow_ref[0:16, :].astype(F32)[8:16, :]
    col_pad[8 : 8 + 2 * rows, :] = xcol_ref[0 : 2 * rows, :].astype(F32)
    row_pad[0:8, :] = jnp.zeros((8, xrow_ref.shape[1]), F32)
    row_pad[8 : 8 + 2 * cols, :] = xrow_ref[16 : 16 + 2 * cols, :].astype(F32)
    left = [col_pad[pl.ds(first, rows, stride=2), :] for first in (7, 8, 9)]
    over = [row_pad[pl.ds(first, cols, stride=2), :] for first in (7, 8, 9)]
    return left, over


def edges_kernel(
    rows, cols, place_ref, z_in, xcol_ref, right_ref, own_col_ref, own_row_ref, got_one, got_two, w_ref,
    z_ref, stats_ref, xrow_ref, below_ref, z_rim_ref, col_pad, row_pad, rim, bottom, side,
):
    cin = xcol_ref.shape[1]
    even_row = place_ref[1] == 0
    line = 2 * cols + 32
    xrow_ref[...] = choose(even_row, got_two[0 : 2 * line, :], got_one[0 : 2 * line, :])
    below_ref[...] = choose(even_row, got_one[...], got_two[...])
    left, over = edge_parts(rows, cols, xcol_ref, xrow_ref, col_pad, row_pad)
    z_ref[...] = z_in[...]
    from_above = dot(jnp.concatenate(over, 1).astype(BF16), w_ref[0 : 3 * cin])
    from_left = (
        dot(left[0].astype(BF16), w_ref[0:cin])
        + dot(left[1].astype(BF16), w_ref[3 * cin : 4 * cin])
        + dot(left[2].astype(BF16), w_ref[6 * cin : 7 * cin])
    )
    z_ref[0:cols, :] = z_ref[0:cols, :] + from_above
    rim[...] = from_left
    for p in range(rows):
        z_ref[p * cols : p * cols + 1, :] = z_ref[p * cols : p * cols + 1, :] + rim[p : p + 1, :]
    z = z_ref[...]
    stats_ref[0:1, :] = jnp.sum(z, axis=0, keepdims=True)
    stats_ref[1:2, :] = jnp.sum(z * z, axis=0, keepdims=True)
    bottom[0, 0:line, :] = own_row_ref[0:line, :].astype(F32)
    bottom[1, 0:line, :] = below_ref[0:line, :].astype(F32)
    bottom[2, 0:line, :] = below_ref[line : 2 * line, :].astype(F32)
    over_end = xrow_ref[2 * cols : 2 * cols + 32, :].astype(F32)
    for b, ref in enumerate((own_col_ref, right_ref, right_ref)):
        first = 2 * rows if b == 2 else 0
        side[b, 8 : 8 + 2 * rows, :] = ref[first : first + 2 * rows, :].astype(F32)
        side[b, 7:8, :] = over_end[15 + b : 16 + b, :]
    parts = []
    for a in range(3):
        for b in range(3):
            low = bottom[a, pl.ds(15 + b, cols + 8, stride=2), :]
            beside = side[b, pl.ds(7 + a, rows, stride=2), :]
            parts.append(jnp.concatenate([low, beside], 0).astype(BF16))
    z_rim_ref[...] = dot(jnp.concatenate(parts, 1), w_ref[...])


def windows_kernel(rows, cols, planes_ref, xcol_ref, xrow_ref, t_ref, col_pad, row_pad, wide):
    cin = xrow_ref.shape[1]
    cells = rows * cols
    left, over = edge_parts(rows, cols, xcol_ref, xrow_ref, col_pad, row_pad)
    for half, parts in ((0, left[1]), (3, left[2])):
        wide[...] = planes_ref[cols:, half * cin : (half + 1) * cin].astype(F32)
        wide[pl.ds(0, rows, stride=cols), :] = parts
        window = wide[...].astype(BF16)
        t_ref[(half + 3) * cin : (half + 4) * cin, :] = window.T
    wide[cols:, :] = planes_ref[cols:cells, 3 * cin : 4 * cin].astype(F32)
    wide[0:cols, :] = over[0]
    wide[pl.ds(0, rows, stride=cols), :] = left[0]
    t_ref[0:cin, :] = wide[...].astype(BF16).T
    for slot in (1, 2):
        lane = (3 + slot) * cin
        below = planes_ref[cols:cells, lane : lane + cin]
        window = jnp.concatenate([over[slot].astype(BF16), below], 0)
        t_ref[slot * cin : (slot + 1) * cin, :] = window.T
    for slot in (1, 2, 4, 5):
        lane = slot * cin
        t_ref[lane + 3 * cin : lane + 4 * cin, :] = planes_ref[cols:, lane : lane + cin].T


def prepare_kernel(rows, cols, g_hbm, left_ref, right_ref, w_ref, body_ref, w_t_ref, done_ref, wide, rims, g_ref, sem):
    pitch = cols + 16
    depth = w_ref.shape[1]
    size = 2 * rows
    copy = pltpu.make_async_copy(g_hbm, g_ref, sem)
    copy.start()
    for tap in range(9):
        w_t_ref[tap * depth : (tap + 1) * depth, :] = w_ref[tap * depth : (tap + 1) * depth, :].T
    done_ref[...] = jnp.zeros(done_ref.shape, F32)
    for half in range(depth // 128):
        lanes = slice(half * 128, (half + 1) * 128)
        rims[0, :, lanes] = left_ref[size + half * rows : size + (half + 1) * rows, :].astype(F32)
        rims[1, :, lanes] = right_ref[2 * size + half * rows : 2 * size + (half + 1) * rows, :].astype(F32)
    copy.wait()
    for p in range(rows):
        first = p * pitch
        wide[first + 8 : first + 8 + cols, :] = g_ref[p].astype(F32)
        wide[first + 7 : first + 8, :] = rims[0, p : p + 1, :]
        wide[first + 8 + cols : first + 9 + cols, :] = rims[1, p : p + 1, :]
        for b in (0, 2):
            body_ref[b, p * cols : (p + 1) * cols, :] = wide[first + 9 - b : first + 9 - b + cols, :].astype(BF16)
    body_ref[1] = g_ref[...].reshape(body_ref.shape[1:])


def window(cols, body_ref, edge_ref, b, first, size):
    cells = body_ref.shape[1]
    parts = []
    if first < cols:
        parts.append(edge_ref[b, first:cols, :])
    start, stop = max(first, cols) - cols, min(first + size, cells + cols) - cols
    parts.append(body_ref[b, start:stop, :])
    if first + size > cells + cols:
        parts.append(edge_ref[b, cols : first + size - cells, :])
    return parts[0] if len(parts) == 1 else jnp.concatenate(parts, 0)


def upstream_kernel(
    rows, cols, body_ref, w_t_ref, right_ref, own_col_ref, own_row_ref, above_ref, below_ref,
    edge_ref, act_grad_ref, rim_ref, wide, bottom, side,
):
    pitch = cols + 16
    depth = act_grad_ref.shape[1]
    size = 2 * rows
    line = 2 * cols + 32
    for half in range(depth // 128):
        lanes = slice(half * 128, (half + 1) * 128)
        side[0, 8 : 8 + rows, lanes] = right_ref[3 * size + half * rows : 3 * size + (half + 1) * rows, :].astype(F32)
        side[1, 8 : 8 + rows, lanes] = right_ref[2 * size + half * rows : 2 * size + (half + 1) * rows, :].astype(F32)
        side[2, 8 : 8 + rows, lanes] = own_col_ref[size + half * rows : size + (half + 1) * rows, :].astype(F32)
        over = above_ref[line + half * pitch : line + (half + 1) * pitch, :].astype(F32)
        under = below_ref[2 * line + half * pitch : 2 * line + (half + 1) * pitch, :].astype(F32)
        wide[0:pitch, lanes] = over
        wide[pitch : 2 * pitch, lanes] = under
        for b in range(3):
            side[b, 7:8, lanes] = over[9 + cols - b : 10 + cols - b, :]
            side[b, 8 + rows : 9 + rows, lanes] = under[9 + cols - b : 10 + cols - b, :]
        bottom[0, 0:pitch, lanes] = below_ref[3 * line + half * pitch : 3 * line + (half + 1) * pitch, :].astype(F32)
        bottom[1, 0:pitch, lanes] = under
        bottom[2, 0:pitch, lanes] = own_row_ref[line + half * pitch : line + (half + 1) * pitch, :].astype(F32)
    bottom[:, pitch:, :] = jnp.zeros((3, 8, depth), F32)
    for b in range(3):
        edge_ref[b, 0:cols, :] = wide[9 - b : 9 - b + cols, :].astype(BF16)
        edge_ref[b, cols:, :] = wide[pitch + 9 - b : pitch + 9 - b + cols, :].astype(BF16)
    for row in range(0, rows * cols, LONG):
        parts = []
        for a in range(3):
            for b in range(3):
                parts.append(window(cols, body_ref, edge_ref, b, row + (2 - a) * cols, LONG))
        act_grad_ref[row : row + LONG, :] = dot(jnp.concatenate(parts, 1), w_t_ref[...])
    parts = []
    for a in range(3):
        for b in range(3):
            low = bottom[a, 9 - b : 17 - b + cols, :]
            beside = side[b, 9 - a : 9 - a + rows, :]
            parts.append(jnp.concatenate([low, beside], 0).astype(BF16))
    rim_ref[...] = dot(jnp.concatenate(parts, 1), w_t_ref[...])


def group_sum(value, depth):
    size = depth // GROUPS
    one = lax.broadcasted_iota(jnp.int32, (depth, depth), 0) // size
    two = lax.broadcasted_iota(jnp.int32, (depth, depth), 1) // size
    same = jnp.where(one == two, 1.0, 0.0).astype(F32)
    return lax.dot_general(
        value, same, (((1,), (0,)), ((), ())), precision=lax.Precision.HIGHEST, preferred_element_type=F32
    )


def add_kernel(*refs):
    refs[-1][...] = tree_sum([r[...] for r in refs[:-1]])


def stack_kernel(*refs):
    for k, ref in enumerate(refs[:-1]):
        refs[-1][k] = ref[...]


def activate_kernel(norm_count, own_ref, pair_ref, z_ref, act_grad_ref, gain_ref, bias_ref, act_ref, pre_ref, sums_ref, moments_ref):
    cells, depth = z_ref.shape
    total = group_sum(own_ref[...] + pair_ref[...], depth) / norm_count
    mean = total[0:1, :]
    inv_std = 1.0 / jnp.sqrt(total[1:2, :] - mean * mean + 1e-05)
    moments_ref[0:1, :] = mean
    moments_ref[1:2, :] = inv_std
    gain = gain_ref[...]
    bias = bias_ref[...]

    def chunk(i, carry):
        row = pl.multiple_of(i * 64, 64)
        normed = (z_ref[pl.ds(row, 64), :] - mean) * inv_std
        shifted = normed * gain + bias
        sig = 1.0 / (1.0 + jnp.exp(-shifted))
        act_ref[pl.ds(row, 64), :] = (shifted * sig).astype(BF16)
        pre = act_grad_ref[pl.ds(row, 64), :] * sig * (1.0 + shifted * (1.0 - sig))
        pre_ref[pl.ds(row, 64), :] = pre
        one = jnp.sum(pre.reshape(8, 8, depth), axis=0)
        two = jnp.sum((pre * normed).reshape(8, 8, depth), axis=0)
        return carry[0] + one, carry[1] + two

    zero = jnp.zeros((8, depth), F32)
    one, two = lax.fori_loop(0, cells // 64, chunk, (zero, zero))
    sums_ref[0:1, :] = jnp.sum(one, axis=0, keepdims=True)
    sums_ref[1:2, :] = jnp.sum(two, axis=0, keepdims=True)


def second_kernel(rows, cols, place_ref, act_ref, body_ref, edge_ref, keep_ref, send_ref):
    cells = rows * cols
    depth = act_ref.shape[1]
    act_t = act_ref[...].T
    half, size = depth // 2, depth // 8
    even = place_ref[4] == 0
    spot = place_ref[5] & 3
    for a in range(3):
        for b in range(3):
            first = (2 - a) * cols
            tap = a * 3 + b
            both = dot(act_t, window(cols, body_ref, edge_ref, b, first, cells))
            mine = jnp.where(even, both[0:half, :], both[half:, :])
            theirs = jnp.where(even, both[half:, :], both[0:half, :]).astype(BF16)
            for j in range(4):
                keep_ref[j ^ spot, tap * size : (tap + 1) * size, :] = mine[j * size : (j + 1) * size, :]
                send_ref[j ^ spot, tap * size : (tap + 1) * size, :] = theirs[j * size : (j + 1) * size, :]


def conv_grad_kernel(norm_count, rows, cols, place_ref, own_ref, pair_ref, *refs):
    z_ref, pre_ref, moments_ref, gain_ref, bias_ref, z_rim_ref, act_rim_ref, t_ref = refs[:8]
    grad_ref, rim_ref, total_ref, keep_ref, send_ref = refs[8:]
    cells, depth = z_ref.shape
    total = own_ref[...] + pair_ref[...]
    total_ref[...] = total
    gain = gain_ref[...]
    means = group_sum(total * gain, depth) / norm_count
    mean = moments_ref[0:1, :]
    inv_std = moments_ref[1:2, :]
    shift = means[0:1, :]
    scale = means[1:2, :]

    def value(z, pre):
        return ((gain * pre - shift - (z - mean) * inv_std * scale) * inv_std).astype(BF16)

    def chunk(i, carry):
        row = pl.multiple_of(i * 64, 64)
        grad_ref[pl.ds(row, 64), :] = value(z_ref[pl.ds(row, 64), :], pre_ref[pl.ds(row, 64), :])
        return carry

    lax.fori_loop(0, cells // 64, chunk, 0)
    z = z_rim_ref[...]
    shifted = (z - mean) * inv_std * gain + bias_ref[...]
    sig = 1.0 / (1.0 + jnp.exp(-shifted))
    pre = act_rim_ref[...] * sig * (1.0 + shifted * (1.0 - sig))
    cell = lax.broadcasted_iota(jnp.int32, z.shape, 0)
    to_right = jnp.where(cell >= cols, place_ref[2], 1)
    to_below = jnp.where(cell < cols + 8, place_ref[3], 1)
    rim_ref[...] = jnp.where(to_right * to_below == 1, value(z, pre).astype(F32), 0.0)

    half = t_ref.shape[0] // 2
    size = half // 4
    core = place_ref[4]
    spot = place_ref[5] & 3
    theirs = dot(t_ref[pl.ds(pl.multiple_of((1 - core) * half, 16), half), :], grad_ref[...]).astype(BF16)
    mine = dot(t_ref[pl.ds(pl.multiple_of(core * half, 16), half), :], grad_ref[...])
    for j in range(4):
        send_ref[j ^ spot] = theirs[j * size : (j + 1) * size, :]
        keep_ref[j ^ spot] = mine[j * size : (j + 1) * size, :]


def input_kernel(rows, cols, d_ref, rim_ref, w_ref, out_ref, done_ref, plain, shifted, w_t, wide, mixed):
    cells = rows * cols
    cin = out_ref.shape[2]
    depth = d_ref.shape[1]
    pitch = cols + 8
    plain[0:cells, :] = d_ref[...]
    plain[cells:, :] = rim_ref[0:cols, :].astype(BF16)
    for p in range(rows + 1):
        first = p * pitch
        wide[first : first + cols, :] = plain[p * cols : (p + 1) * cols, :].astype(F32)
        next_cell = cols + 8 + p if p < rows else cols
        wide[first + cols : first + cols + 1, :] = rim_ref[next_cell : next_cell + 1, :]
        shifted[p * cols : (p + 1) * cols, :] = wide[first + 1 : first + 1 + cols, :].astype(BF16)
    for place, tap in enumerate((4, 5, 7, 8, 3, 6, 1, 2, 0)):
        w_t[:, place * cin : (place + 1) * cin] = w_ref[tap * cin : (tap + 1) * cin, :].T
    done_ref[...] = jnp.zeros(done_ref.shape, F32)
    step = CHUNK // cols

    def chunk(i, carry):
        row = pl.multiple_of(i * CHUNK, CHUNK)
        under = pl.multiple_of(row + cols, cols)
        own = dot(plain[pl.ds(row, CHUNK), :], w_t[:, 0 : 4 * cin])
        right = dot(shifted[pl.ds(row, CHUNK), :], w_t[:, 4 * cin : 6 * cin])
        below = dot(plain[pl.ds(under, CHUNK), :], w_t[:, 6 * cin : 8 * cin])
        corner = dot(shifted[pl.ds(under, CHUNK), :], w_t[:, 8 * cin :])
        even_even = own[:, 0:cin]
        even_odd = own[:, cin : 2 * cin] + right[:, 0:cin]
        odd_even = own[:, 2 * cin : 3 * cin] + below[:, 0:cin]
        odd_odd = own[:, 3 * cin :] + right[:, cin:] + below[:, cin:] + corner
        for parity, pair in enumerate(((even_even, even_odd), (odd_even, odd_odd))):
            for side in range(2):
                mixed[pl.ds(parity, step, stride=2), pl.ds(side, cols, stride=2), :] = pair[side].reshape(
                    step, cols, cin
                )
        out_ref[pl.ds(pl.multiple_of(i * 2 * step, 2 * step), 2 * step)] = mixed[
            0 : 2 * step, 0 : 2 * cols, :
        ].astype(BF16)
        return carry

    lax.fori_loop(0, rows // step, chunk, 0)


def first_split_kernel(place_ref, mine_ref, other_ref, keep_ref, send_ref):
    even = place_ref[4] == 0
    none, along_y, along_x, both = [mine_ref[k] + other_ref[k].astype(F32) for k in range(4)]
    keep_ref[0] = none
    keep_ref[1] = jnp.where(even, along_y, along_x)
    send_ref[0] = jnp.where(even, along_x, along_y).astype(BF16)
    send_ref[1] = both.astype(BF16)


def second_split_kernel(mine_ref, other_ref, keep_ref, send_ref):
    keep_ref[...] = mine_ref[0] + other_ref[0].astype(F32)
    send_ref[...] = (mine_ref[1] + other_ref[1].astype(F32)).astype(BF16)


def half_kernel(slots_ref, other_ref, *refs):
    own_ref, one_ref, two_ref, three_ref = refs[-4:]
    rows = slots_ref.shape[1]
    own_ref[...] = slots_ref[0] + other_ref[0]
    for k, ref in enumerate((one_ref, two_ref, three_ref)):
        ref[0:rows, :] = (slots_ref[k + 1] + other_ref[k + 1]).astype(BF16)
    if len(refs) > 4:
        two_ref[rows:, :] = three_parts(refs[0][...])


def three_parts(pair):
    high = pair.astype(BF16).astype(F32)
    rest = pair - high
    middle = rest.astype(BF16).astype(F32)
    low = rest - middle
    zeros = jnp.zeros((10, pair.shape[1]), F32)
    return jnp.concatenate([high, middle, low, zeros], 0).astype(BF16)


def from_parts(parts):
    parts = parts.astype(F32)
    return parts[0:2, :] + parts[2:4, :] + parts[4:6, :]


def total_kernel(*refs):
    rows = refs[-1].shape[0]
    refs[-1][...] = tree_sum([r[0:rows, :].astype(F32) for r in refs[:-1]]).astype(BF16)


def both_kernel(count, *refs):
    second, first, out_ref = refs[:count], refs[count:-1], refs[-1]
    rows = second[0].shape[0]
    out_ref[0:rows, :] = tree_sum([r[...].astype(F32) for r in second]).astype(BF16)
    out_ref[rows:, :] = tree_sum([r[...].astype(F32) for r in first]).astype(BF16)


def first_total_kernel(own_ref, one_ref, two_ref, three_ref, pair_ref, out_ref, bias_ref, gain_ref):
    total_kernel(own_ref, one_ref, two_ref, three_ref, out_ref)
    rows = out_ref.shape[0]
    both = from_parts(three_parts(pair_ref[...])) + from_parts(two_ref[rows:, :])
    bias_ref[...] = both[0:1, :]
    gain_ref[...] = both[1:2, :]


def gather_kernel(slots, rows, place_ref, *refs):
    me = place_ref[5]
    count = len(slots)
    shards = refs[: 2 * count]
    second_ref, first_ref, second_stage, first_stage, sems = refs[-5:]
    copies = []
    for i, slot in enumerate(slots):
        for k, where in ((i, me ^ slot), (i + count, me ^ slot ^ 4)):
            second_stage[k] = shards[k][0:rows, :].astype(F32).reshape(second_stage.shape[1:])
            first_stage[k] = shards[k][rows:, :].astype(F32)
            copies.append(pltpu.make_async_copy(second_stage.at[k], second_ref.at[:, where], sems.at[2 * k]))
            copies.append(pltpu.make_async_copy(first_stage.at[k], first_ref.at[where], sems.at[2 * k + 1]))
            copies[-2].start()
            copies[-1].start()
    for copy in copies:
        copy.wait()


def on_device(dp_size, tiles, images, first_weight, norm_gain, norm_bias, second_weight, upstream):
    rows, cols, depth = upstream.shape[2:]
    cin = images.shape[4]
    cells = rows * cols
    group_size = depth // GROUPS
    norm_count = float(cells * tiles * group_size)
    tile_rows = tiles // TCOLS
    axes = ("dp", "space")
    devices = dp_size * tiles

    def flip(value, mask):
        return lax.ppermute(value, axes, [(i, i ^ mask) for i in range(devices)])

    def swapped(value, down, right):
        pairs = []
        for t in range(tiles):
            spot = (t + TCOLS + 2) % tiles
            r, c = spot // TCOLS, spot % TCOLS
            r = r if not down else ((r + down - 1) ^ 1) - down + 1
            c = c if not right else ((c + right - 1) ^ 1) - right + 1
            if 0 <= r < tile_rows and 0 <= c < TCOLS:
                pairs.append((t, (r * TCOLS + c - TCOLS - 2) % tiles))
        return lax.ppermute(value, "space", pairs)

    def added(parts, after=()):
        return call(add_kernel, [shape(parts[0].shape, F32)], parts, after=after)[0]

    def fetched(value, after=()):
        parts = [value] + [flip(value, 2 * k) for k in (1, 2, 3)]
        for k in range(3, tiles.bit_length() - 1):
            total = added(parts, after)
            parts, after = [total, flip(total, 1 << k)], ()
        return parts

    def crossed(value, even, odd):
        return lax.ppermute(value, axes, [(i, i ^ (odd if i % 2 else even)) for i in range(devices)])

    def along(value, size, step):
        return [value] + [flip(value, step * k) for k in range(1, size)]

    def total(parts, after=()):
        if len(parts) == 1:
            return parts[0]
        return call(total_kernel, [shape(parts[0].shape, BF16)], parts, after=after)[0]

    def halved(slots, more=(), after=()):
        part = slots[0].shape[1:]
        longer = (part[0] + 16 * len(more), part[1])
        outs = [shape(part, F32), shape(part, BF16), shape(longer, BF16), shape(part, BF16)]
        return call(half_kernel, outs, [slots[0], flip(slots[1], 1), *more], after=after)

    def halves(value):
        pair = [value]
        for k in range(2, tiles.bit_length() - 1):
            pair = [total(pair)]
            pair.append(flip(pair[0], 1 << k))
        return pair

    masks = [0, 2, tiles, tiles + 2]

    def quartered(parts):
        return [parts[0]] + [flip(parts[k], masks[k]) for k in (1, 2, 3)]

    def quarters(shard):
        return [shard] + [flip(shard, masks[k]) for k in (1, 2, 3)]

    space = lax.axis_index("space")
    spot = (space + TCOLS + 2) % tiles
    column, row = spot % TCOLS, spot // TCOLS
    me = (space % 2) * 4 + (lax.axis_index("dp") % 2) * 2 + (space // 2) % 2
    place = jnp.stack([column % 2, row % 2, column < TCOLS - 1, row < tile_rows - 1, space % 2, me]).astype(jnp.int32)
    x = pltpu.with_memory_space_constraint(images[0, 0], pltpu.HBM)
    g3 = pltpu.with_memory_space_constraint(upstream[0, 0], pltpu.HBM)
    w1 = first_weight.reshape(9 * cin, depth)
    w2 = second_weight.reshape(9 * depth, depth)
    gain = norm_gain.reshape(1, depth)
    bias = norm_bias.reshape(1, depth)

    hbm = pl.BlockSpec(memory_space=pltpu.HBM)
    smem = pl.BlockSpec(memory_space=pltpu.SMEM)
    vmem = pl.BlockSpec(memory_space=pltpu.VMEM)
    ends = shape((4 * 2 * rows, cin), BF16)
    half_ends = shape((2 * 2 * rows, cin), BF16)
    one, two, own_column, x_lines, g_lines = call(
        functools.partial(pack_kernel, rows, cols),
        [ends, ends, half_ends, shape((3, 2 * cols, cin), BF16), shape((3, cols, depth), BF16)],
        [place, x, g3],
        [pltpu.VMEM((2 * rows, 16, cin), BF16)] * 2
        + [pltpu.VMEM((rows, 16, depth), BF16)] * 2
        + [
            pltpu.VMEM((2 * rows * 16 + 16, cin), F32),
            pltpu.VMEM((rows * 16 + 16, 128), F32),
            pltpu.SemaphoreType.DMA((8,)),
        ],
        specs=[smem, hbm, hbm],
    )
    one = swapped(one, 0, 1)
    two = swapped(two, 0, 2)
    (planes,) = call(
        functools.partial(planes_kernel, rows, cols),
        [shape((cells + cols, 6 * cin), BF16)],
        [x],
        [
            pltpu.VMEM((2 * CHUNK // cols + 2, 2 * cols + 16, cin), F32),
            pltpu.VMEM((cells // CHUNK, 2 * CHUNK // cols, 2 * cols, cin), BF16),
            pltpu.SemaphoreType.DMA((cells // CHUNK,)),
        ],
        specs=[hbm],
        flops=cells * 9 * cin * depth,
    )
    lines = shape((4 * (2 * cols + 32), cin), BF16)
    half_lines = shape((2 * (2 * cols + 32), cin), BF16)
    from_left, from_right, one, two, own_row = call(
        functools.partial(rows_kernel, rows, cols),
        [half_ends, ends, lines, lines, half_lines],
        [place, x_lines, g_lines, one, two],
        [pltpu.VMEM((2 * cols + 32, cin), F32), pltpu.VMEM((cols + 16, 128), F32)],
        smem=1,
        after=[planes],
    )
    got_one = swapped(one, 1, 0)
    got_two = swapped(two, 2, 0)
    (z,) = call(
        functools.partial(stride_kernel, rows, cols),
        [shape((cells, depth), F32)],
        [planes, w1],
        flops=2 * cells * 9 * cin * depth,
        after=[one],
    )
    pads = [pltpu.VMEM((2 * rows + 16, cin), F32), pltpu.VMEM((2 * cols + 16, cin), F32)]
    body, w_t, prepared = call(
        functools.partial(prepare_kernel, rows, cols),
        [shape((3, cells, depth), BF16), shape((9 * depth, depth), BF16), shape((8, 128), F32)],
        [g3, from_left, from_right, w2],
        [
            pltpu.VMEM((rows * (cols + 16), depth), F32),
            pltpu.VMEM((2, rows, depth), F32),
            pltpu.VMEM((rows, cols, depth), BF16),
            pltpu.SemaphoreType.DMA,
        ],
        specs=[hbm, vmem, vmem, vmem],
        after=[one],
    )
    rim = rows + cols + 8
    z, stats, from_above, from_below, z_rim = call(
        functools.partial(edges_kernel, rows, cols),
        [shape((cells, depth), F32), shape((2, depth), F32), half_lines, lines, shape((rim, depth), F32)],
        [place, z, from_left, from_right, own_column, own_row, got_one, got_two, w1],
        pads
        + [
            pltpu.VMEM((rows, depth), F32),
            pltpu.VMEM((3, 2 * cols + 40, cin), F32),
            pltpu.VMEM((3, 2 * rows + 16, cin), F32),
        ],
        smem=1,
        after=[prepared],
        flops=2 * 80 * 3 * cin * depth,
    )
    stats = fetched(added([stats, flip(stats, 1)]))
    edge, act_grad, act_rim = call(
        functools.partial(upstream_kernel, rows, cols),
        [shape((3, 2 * cols, depth), BF16), shape((cells, depth), F32), shape((rim, depth), F32)],
        [body, w_t, from_right, own_column, own_row, from_above, from_below],
        [
            pltpu.VMEM((2 * (cols + 16), depth), F32),
            pltpu.VMEM((3, cols + 24, depth), F32),
            pltpu.VMEM((3, rows + 16, depth), F32),
        ],
        flops=2 * cells * 9 * depth * depth,
    )
    activated, pre_grad, sums, moments = call(
        functools.partial(activate_kernel, norm_count),
        [shape((cells, depth), BF16), shape((cells, depth), F32), shape((2, depth), F32), shape((2, depth), F32)],
        stats + [z, act_grad, gain, bias],
        flops=cells * depth * 30,
    )
    other = flip(sums, 1)
    second_slots = call(
        functools.partial(second_kernel, rows, cols),
        [shape((4, 9 * depth // 8, depth), F32), shape((4, 9 * depth // 8, depth), BF16)],
        [place, activated, body, edge],
        flops=2 * cells * 9 * depth * depth,
        smem=1,
    )
    near = added([sums, other], second_slots[1:])
    part = second_slots[0].shape[1:]
    kept, sent = call(
        first_split_kernel,
        [shape((2,) + part, F32), shape((2,) + part, BF16)],
        [place, second_slots[0], flip(second_slots[1], 1)],
        smem=1,
        after=[near],
    )
    parts = fetched(near, [kept])
    second_parts = call(
        second_split_kernel,
        [shape(part, F32), shape(part, BF16)],
        [kept, crossed(sent, tiles, 2)],
        after=parts[:1],
    )
    (windows,) = call(
        functools.partial(windows_kernel, rows, cols),
        [shape((9 * cin, cells), BF16)],
        [planes, from_left, from_above],
        pads + [pltpu.VMEM((cells, cin), F32)],
        flops=2 * cells * 9 * cin * depth,
        after=second_parts[:1],
    )
    second_shard = total([second_parts[0], crossed(second_parts[1], 2, tiles)])
    pair = halves(total(along(second_shard, dp_size // 2, 2 * tiles)))
    conv_grad, grad_rim, sum_pair, *first_slots = call(
        functools.partial(conv_grad_kernel, norm_count, rows, cols),
        [
            shape((cells, depth), BF16),
            shape((rim, depth), F32),
            shape((2, depth), F32),
            shape((4, 9 * cin // 8, depth), F32),
            shape((4, 9 * cin // 8, depth), BF16),
        ],
        [place] + parts + [z, pre_grad, moments, gain, bias, z_rim, act_rim, windows],
        flops=2 * cells * 9 * cin * depth,
        smem=1,
        after=[second_shard],
    )
    first_parts = quartered(halved(first_slots, [sum_pair]))
    first_shard, bias_grad, gain_grad = call(
        first_total_kernel,
        [shape(first_slots[0].shape[1:], BF16), shape((1, depth), F32), shape((1, depth), F32)],
        first_parts + [sum_pair],
    )
    first_shard = along(total(along(first_shard, dp_size // 2, 2 * tiles)), tiles // 4, 4)
    input_grad, done = call(
        functools.partial(input_kernel, rows, cols),
        [shape((2 * rows, 2 * cols, cin), BF16), shape((8, 128), F32)],
        [conv_grad, grad_rim, w1],
        [
            pltpu.VMEM((cells + cols, depth), BF16),
            pltpu.VMEM((cells + cols, depth), BF16),
            pltpu.VMEM((depth, 9 * cin), BF16),
            pltpu.VMEM(((rows + 1) * (cols + 8), depth), F32),
            pltpu.VMEM((2 * CHUNK // cols + 2, 2 * cols + 8, cin), F32),
        ],
        flops=2 * cells * 9 * cin * depth,
    )
    sizes = second_slots[0].shape[1], first_slots[0].shape[1]
    (shard,) = call(
        functools.partial(both_kernel, len(pair)),
        [shape((sum(sizes), depth), BF16)],
        pair + first_shard,
        after=[done],
    )
    for k in range(1, dp_size.bit_length() - 1):
        bias_grad = bias_grad + flip(bias_grad, tiles << k)
        gain_grad = gain_grad + flip(gain_grad, tiles << k)
    own = quarters(shard)
    grads = [shape((9, 8, depth // 8, depth), F32), shape((8, sizes[1], depth), F32)]
    for slots in ((0,), (1, 2, 3)):
        here = [own[slot] for slot in slots]
        shards = here + [flip(value, 1) for value in here]
        left = list(grads) if len(slots) > 1 else []
        grads = call(
            functools.partial(gather_kernel, slots, sizes[0]),
            [shape(g.shape, F32) for g in grads],
            [place] + shards + left,
            [
                pltpu.VMEM((len(shards), 9, depth // 8, depth), F32),
                pltpu.VMEM((len(shards), sizes[1], depth), F32),
                pltpu.SemaphoreType.DMA((2 * len(shards),)),
            ],
            specs=[smem] + [vmem] * len(shards) + [hbm] * len(left),
            out_specs=[hbm] * 2,
            aliases={1 + len(shards) + k: k for k in range(len(left))},
        )
    second_grad, first_grad = grads
    return (
        input_grad[None, None],
        first_grad.reshape(first_weight.shape),
        second_grad.reshape(second_weight.shape),
        gain_grad.reshape(depth),
        bias_grad.reshape(depth),
    )


def solution(mesh):
    placed = (
        P("dp", "space", None, None, None),
        P(),
        P(),
        P(),
        P(),
        P("dp", "space", None, None, None),
    )
    return jax.shard_map(
        functools.partial(on_device, mesh.shape["dp"], mesh.shape["space"]),
        mesh=mesh,
        in_specs=placed,
        out_specs=(P("dp", "space", None, None, None), P(), P(), P(), P()),
        check_vma=False,
    )
```
